256 devices in a mesh: subj: 64 (over y, z, core), strip: 4 (over x).
Axes of the slice: x: 4, y: 4, z: 8, core: 2. Of those that a mesh axis runs over, the one named last changes fastest.
Arguments:
- displacement: bfloat16 [128, 3, 4, 512, 512], P('subj', None, None, None, 'strip'), may hold values from -0.14941406 to 0.14941406
- age: float32 [128], replicated, may hold values from -4 to 4
- group_codes: int32 [128], replicated, may hold values from 0 to 2, as said below
- perms: int32 [256, 128], replicated, may hold values from 0 to 127, each once within a row
Outputs:
- t_map: float32 [2, 512, 512], P(None, 'subj', 'strip')
- peaks: float32 [256], replicated
The draws below stay inside these ranges and needn't reach their ends.
Inputs may be any that keep to these rules, and one draw needn't show every extreme that they name: `group_codes`: each of the three groups holds 42 or more subjects.
All inputs are finite; a program needn't handle non-finite values.
Results may differ from the reference program's by a relative error of at most 0.0014.
Values may be sent and summed in bfloat16 or wider, within the bound.
No kernel may reach another device: no remote copies, remote signals or barrier semaphores. Data moves between devices by JAX's collectives and lax.ppermute only.
A program may use at most 128 MiB of HBM per device.

```python
import jax
import jax.numpy as jnp
from jax import lax

NX = 512
PLANES = 2
NPERM = 256
SUBJECTS = 128
NY = 512


def draw_group_codes(key, part):
    key = jax.random.fold_in(key, 11)
    base = jnp.arange(SUBJECTS, dtype=jnp.int32) % 3
    return jax.random.permutation(key, base).astype(jnp.int32)


def block_levels(own_key, shape, split, least, high):
    level, own = 1.0, jax.random.fold_in(own_key, 6)
    for dim, blocks in split:
        draws = jnp.exp(jax.random.uniform(jax.random.fold_in(own, dim), (blocks,), jnp.float32, least / len(split), high / len(split)))
        level = level * jnp.repeat(draws, shape[dim] // blocks).reshape([-1 if axis == dim else 1 for axis in range(len(shape))])
    return level


def normal_values(own_key, shape, width, reach, kind=jnp.bfloat16):
    values = width * jax.random.normal(own_key, shape, jnp.float32)
    return jnp.clip(values, min=-reach, max=reach).astype(kind)


def setup_inputs(seed: int = 0) -> dict:
    keys = jax.random.split(jax.random.key(seed), 5)
    displacement = jnp.clip(jax.random.uniform(keys[0], (SUBJECTS, 3, PLANES + 2, NX, NY), jnp.float32, -0.14941406, 0.14941406) * block_levels(keys[0], (SUBJECTS, 3, PLANES + 2, NX, NY), ((0, 64), (4, 4)), -0.4, 0.0), -0.14941406, 0.14941406).astype(jnp.bfloat16)
    age = normal_values(keys[1], (SUBJECTS,), 1.0, 4.0, jnp.float32)
    group_codes = draw_group_codes(jax.random.fold_in(keys[4], 71), 0)
    perms = jax.vmap(lambda own: jax.random.permutation(own, SUBJECTS))(jax.random.split(keys[3], NPERM)).reshape((NPERM, SUBJECTS)).astype(jnp.int32)
    return {"displacement": displacement, "age": age, "group_codes": group_codes, "perms": perms}


def invert_small(matrix):
    size = matrix.shape[0]
    work = jnp.concatenate([matrix, jnp.eye(size, dtype=matrix.dtype)], axis=1)
    for column in range(size):
        pivot_row = work[column] / work[column, column]
        work = work - work[:, column:column + 1] * pivot_row[None, :]
        work = work.at[column].set(pivot_row)
    return work[:, size:]

def build_design(age, group_codes):
    ones = jnp.ones_like(age)
    first = (group_codes == 1).astype(age.dtype)
    second = (group_codes == 2).astype(age.dtype)
    return jnp.stack([ones, first, second, age], axis=1)

def log_volume(dz, dx, dy):
    j00 = 1.0 + dz[:, 0]
    j01 = dx[:, 0]
    j02 = dy[:, 0]
    j10 = dz[:, 1]
    j11 = 1.0 + dx[:, 1]
    j12 = dy[:, 1]
    j20 = dz[:, 2]
    j21 = dx[:, 2]
    j22 = 1.0 + dy[:, 2]
    det = j00 * (j11 * j22 - j12 * j21) - j01 * (j10 * j22 - j12 * j20) + j02 * (j10 * j21 - j11 * j20)
    return jnp.log(det)

def one_subject(field):
    wide = field[None].astype(jnp.float32)
    dz = (wide[:, :, 2:] - wide[:, :, :-2]) * 0.5
    center = wide[:, :, 1:-1]
    padx = jnp.pad(center, ((0, 0), (0, 0), (0, 0), (1, 1), (0, 0)))
    dx = (padx[:, :, :, 2:] - padx[:, :, :, :-2]) * 0.5
    pady = jnp.pad(center, ((0, 0), (0, 0), (0, 0), (0, 0), (1, 1)))
    dy = (pady[..., 2:] - pady[..., :-2]) * 0.5
    return log_volume(dz, dx, dy)[0]

def residual_terms(proj, yty, ginv):
    rss = yty[None]
    effect = None
    for row in range(4):
        coef = ginv[row, 0] * proj[:, 0] + ginv[row, 1] * proj[:, 1] + ginv[row, 2] * proj[:, 2] + ginv[row, 3] * proj[:, 3]
        rss = rss - proj[:, row] * coef
        if row == 2:
            effect = coef
    return (effect, rss)

def t_stat(proj, yty, ginv, subjects):
    effect, rss = residual_terms(proj, yty, ginv)
    padded = jnp.pad(rss, ((0, 0), (0, 0), (1, 1), (1, 1)))
    beside_all = padded[:, :, :-2, 1:-1] + padded[:, :, 2:, 1:-1] + padded[:, :, 1:-1, :-2] + padded[:, :, 1:-1, 2:]
    smooth = 0.4 * rss + 0.15 * beside_all
    variance = ginv[2, 2] * (smooth / (subjects - 4) + 1e-06)
    return effect / jnp.sqrt(variance)

def reference(displacement, age, group_codes, perms):
    subjects = displacement.shape[0]
    log_jac = lax.map(one_subject, displacement)
    ymat = log_jac.reshape(subjects, -1)
    yty = lax.optimization_barrier(jnp.sum(ymat * ymat, axis=0)).reshape(log_jac.shape[1:])
    design = build_design(age, group_codes)
    gram = jnp.dot(design.T, design, precision=lax.Precision.HIGHEST)
    ginv = invert_small(gram)

    def stats(zrows):
        proj = jnp.dot(zrows, ymat, precision=lax.Precision.HIGHEST)
        proj = proj.reshape((-1, 4) + log_jac.shape[1:])
        return t_stat(proj, yty, ginv, subjects)
    t_map = stats(design.T)[0]
    permuted = jnp.transpose(design[perms], (0, 2, 1)).reshape(NPERM // 8, 8 * 4, subjects)

    def block_peaks(zrows):
        return lax.optimization_barrier(jnp.max(jnp.abs(stats(zrows)), axis=(1, 2, 3)))
    peaks = lax.map(block_peaks, permuted).reshape(NPERM)
    return (t_map, peaks)
```

```python
import functools

import jax
import jax.numpy as jnp
from jax import lax
from jax.experimental import pallas as pl
from jax.experimental.pallas import tpu as pltpu
from jax.sharding import PartitionSpec as P

F32, BF16 = jnp.float32, jnp.bfloat16
LANES = 128
ROWS = 512
BLOCK = 16
CHUNK = 40
PER = 2
COMPS, PLANES = 3, 4
PERMS, GROUP = 256, 272
REACH = 0.6
LEVELS = 32767.0


def slot(subject, comp, plane):
    return 4 * ((subject * COMPS + comp) * PLANES + plane)


def encode(y):
    level = jnp.sqrt(jnp.sqrt(jnp.abs(y) * (1.0 / REACH))) * LEVELS + 0.5
    return jnp.where(y < 0, -level, level)


def decode(code):
    part = code * (REACH**0.25 / LEVELS)
    return (part * jnp.abs(part)) * (part * part)


def log_det(dz, dx, dy):
    j00, j01, j02 = 2.0 + dz[0], dx[0], dy[0]
    j10, j11, j12 = dz[1], 2.0 + dx[1], dy[1]
    j20, j21, j22 = dz[2], dx[2], 2.0 + dy[2]
    det = (
        j00 * (j11 * j22 - j12 * j21)
        - j01 * (j10 * j22 - j12 * j20)
        + j02 * (j10 * j21 - j11 * j20)
    )
    return jnp.log(det * 0.125)


def edges_kernel(disp_ref, out_ref):
    rows = out_ref.shape[0]
    step = 16
    group = lax.broadcasted_iota(jnp.int32, (step, LANES), 1) // 4

    def body(i, carry):
        at = pl.ds(pl.multiple_of(i * step, step), step)
        acc = jnp.zeros((step, LANES), F32)
        for s in range(PER):
            for c in range(COMPS):
                for q in range(PLANES):
                    k = slot(s, c, q)
                    rolled = pltpu.roll(disp_ref[s, c, q, at, :].astype(F32), (k + 2) % LANES, 1)
                    acc = jnp.where(group == k // 4, rolled, acc)
        out_ref[at, :] = acc.astype(BF16)
        return carry

    lax.fori_loop(0, rows // step, body, 0)


def strip_edges(disp):
    rows = 128
    return pl.pallas_call(
        edges_kernel,
        grid=(ROWS // rows,),
        in_specs=[pl.BlockSpec((PER, COMPS, PLANES, rows, LANES), lambda i: (0, 0, 0, i, 0))],
        out_specs=pl.BlockSpec((rows, LANES), lambda i: (i, 0)),
        out_shape=jax.ShapeDtypeStruct((ROWS, LANES), BF16),
        cost_estimate=pl.CostEstimate(flops=10**6, bytes_accessed=3_200_000, transcendentals=0),
        name="strip_edges",
    )(disp)


def inner_kernel(disp_ref, out_ref, pad_ref):
    pad = 8
    for k in range(COMPS * 2):
        pad_ref[k, 0:pad, :] = jnp.zeros((pad, LANES), F32)
        pad_ref[k, pad + ROWS : 2 * pad + ROWS, :] = jnp.zeros((pad, LANES), F32)
        pad_ref[k, pad : pad + ROWS, :] = disp_ref[0, k // 2, 1 + k % 2].astype(F32)
    step = 32

    def body(i, carry):
        base = pl.multiple_of(i * step, step)
        for p in range(2):
            dz, dx, dy = [], [], []
            for c in range(COMPS):
                up = disp_ref[0, c, p + 2, pl.ds(base, step), :].astype(F32)
                down = disp_ref[0, c, p, pl.ds(base, step), :].astype(F32)
                dz.append(up - down)
                center = pad_ref[c * 2 + p, pl.ds(base + pad, step), :]
                dx.append(
                    pad_ref[c * 2 + p, pl.ds(base + pad + 1, step), :]
                    - pad_ref[c * 2 + p, pl.ds(base + pad - 1, step), :]
                )
                dy.append(pltpu.roll(center, LANES - 1, 1) - pltpu.roll(center, 1, 1))
            out_ref[p, pl.ds(base, step), :] = log_det(dz, dx, dy)
        return carry

    lax.fori_loop(0, ROWS // step, body, 0)


def inner_log(disp):
    return pl.pallas_call(
        inner_kernel,
        grid=(PER,),
        in_specs=[pl.BlockSpec((1, COMPS, PLANES, ROWS, LANES), lambda s: (s, 0, 0, 0, 0))],
        out_specs=pl.BlockSpec((2, ROWS, LANES), lambda s: (s, 0, 0)),
        out_shape=jax.ShapeDtypeStruct((PER * 2, ROWS, LANES), F32),
        scratch_shapes=[pltpu.VMEM((COMPS * 2, ROWS + 16, LANES), F32)],
        cost_estimate=pl.CostEstimate(flops=2 * 10**7, bytes_accessed=4_200_000, transcendentals=262144),
        name="inner_log",
    )(disp)


def chunk_kernel(chunks, log_ref, own_ref, left_ref, right_ref, out_ref, side_ref, fix_ref, far_ref, send_ref):
    pad = 8
    strips = lax.axis_size("strip")
    me = lax.axis_index("strip")
    keep_left = (me > 0).astype(F32)
    keep_right = (me < strips - 1).astype(F32)
    for k in range(2):
        side_ref[k, 0:pad, :] = jnp.zeros((pad, LANES), F32)
        side_ref[k, pad + ROWS : 2 * pad + ROWS, :] = jnp.zeros((pad, LANES), F32)
    lane = lax.broadcasted_iota(jnp.int32, (ROWS, LANES), 1)
    low = (lane & 3) < 2
    own = own_ref[...].astype(F32)
    side_ref[0, pad : pad + ROWS, :] = jnp.where(low, left_ref[...].astype(F32), own)
    side_ref[1, pad : pad + ROWS, :] = jnp.where(low, own, right_ref[...].astype(F32))
    for k in range(PER * 2):
        fix_ref[k, 0:pad, :] = jnp.zeros((pad, LANES), F32)
        fix_ref[k, pad + ROWS : 2 * pad + ROWS, :] = jnp.zeros((pad, LANES), F32)
    step = 16
    here = lax.broadcasted_iota(jnp.int32, (step, LANES), 1)

    def body(i, carry):
        base = pl.multiple_of(i * step, step)
        sides = []
        for k in range(2):
            center = side_ref[k, pl.ds(base + pad, step), :]
            dx = (
                side_ref[k, pl.ds(base + pad + 1, step), :]
                - side_ref[k, pl.ds(base + pad - 1, step), :]
            )
            dy = pltpu.roll(center, LANES - 1, 1) - pltpu.roll(center, 1, 1)
            dz = pltpu.roll(center, LANES - 4, 1) - pltpu.roll(center, 4, 1)

            def comps(field):
                return [field] + [pltpu.roll(field, LANES - slot(0, c, 0), 1) for c in (1, 2)]

            sides.append(log_det(comps(dz), comps(dx), comps(dy)))
        left, right = sides
        inner = jnp.where((here & 3) == 2, left, right)
        outer = jnp.where((here & 3) == 1, left * keep_left, right * keep_right)
        far_ref[pl.ds(base, step), :] = encode(outer)
        for s in range(PER):
            for p in range(2):
                at = slot(s, 0, p + 1) + 2
                moved = pltpu.roll(inner, LANES - at, 1)
                whole = jnp.where(
                    (here == 0) | (here == LANES - 1), moved, log_ref[s * 2 + p, pl.ds(base, step), :]
                )
                code = encode(whole)
                fix_ref[s * 2 + p, pl.ds(base + pad, step), :] = code
                target = pl.multiple_of((2 * i + p) * CHUNK, 8) + s * BLOCK
                send_ref[pl.ds(pl.multiple_of(target, 8), step), :] = code
        return carry

    lax.fori_loop(0, ROWS // step, body, 0)
    blocks = ROWS // BLOCK
    far = far_ref[...].T
    for s in range(PER):
        for p in range(2):
            row = p * CHUNK + PER * BLOCK + s * 4
            send_ref[pl.ds(row, blocks, stride=2 * CHUNK), :] = fix_ref[
                s * 2 + p, pl.ds(pad - 1, blocks, stride=BLOCK), :
            ]
            send_ref[pl.ds(row + 1, blocks, stride=2 * CHUNK), :] = fix_ref[
                s * 2 + p, pl.ds(pad + BLOCK, blocks, stride=BLOCK), :
            ]
            for side in range(2):
                line = slot(s, 0, p + 1) + 1 + side
                many = LANES // BLOCK
                for b in range(ROWS // LANES):
                    piece = far[line : line + 1, b * LANES : (b + 1) * LANES]
                    send_ref[
                        pl.ds(row + 2 + side + b * many * 2 * CHUNK, many, stride=2 * CHUNK), :
                    ] = jnp.broadcast_to(piece, (many, LANES))
    per = 4 * CHUNK

    def pack(i, carry):
        at = pl.ds(pl.multiple_of(i * per, 32), per)
        out_ref[at, :] = send_ref[at, :].astype(jnp.int32).astype(jnp.int16)
        return carry

    lax.fori_loop(0, chunks * CHUNK // per, pack, 0)


def chunked(log, own, left, right, chunks):
    return pl.pallas_call(
        functools.partial(chunk_kernel, chunks),
        out_shape=jax.ShapeDtypeStruct((chunks * CHUNK, LANES), jnp.int16),
        scratch_shapes=[
            pltpu.VMEM((2, ROWS + 16, LANES), F32),
            pltpu.VMEM((PER * 2, ROWS + 16, LANES), F32),
            pltpu.VMEM((ROWS, LANES), F32),
            pltpu.VMEM((chunks * CHUNK, LANES), F32),
        ],
        cost_estimate=pl.CostEstimate(flops=10**7, bytes_accessed=2 * 10**6, transcendentals=10**6),
        name="chunked",
    )(log, own, left, right)


def designs_kernel(age_ref, code_ref, perms_ref, out_ref):
    subjects = age_ref.shape[1]
    half = subjects // PER

    def total(v):
        return jnp.sum(v, axis=1, keepdims=True)

    def centred(v):
        return v - total(v) * (1.0 / subjects)

    basis = []
    for raw in (
        (code_ref[...] == 1).astype(F32),
        age_ref[...],
        (code_ref[...] == 2).astype(F32),
    ):
        v = centred(raw)
        for _ in range(2):
            for q in basis:
                v = v - q * total(q * v)
            v = centred(v)
        basis.append(v / jnp.sqrt(total(v * v)))
    lane = lax.broadcasted_iota(jnp.int32, (8, subjects), 1)
    order = PER * (lane % half) + lane // half
    for k, q in enumerate(basis):
        table = jnp.broadcast_to(q, (8, subjects))

        def put(row, values):
            high = values.astype(BF16)
            rest = (values - high.astype(F32)).astype(BF16)
            at = pl.ds(k * GROUP + row, 16)
            out_ref[at, 0:subjects] = high
            out_ref[at, subjects : 2 * subjects] = high
            out_ref[at, 2 * subjects : 3 * subjects] = rest

        for g in range(PERMS // 16):
            two = []
            for h in range(2):
                who = jnp.take_along_axis(perms_ref[g * 16 + h * 8 : g * 16 + h * 8 + 8, :], order, axis=1)
                two.append(jnp.take_along_axis(table, who, axis=1))
            put(g * 16, jnp.concatenate(two, axis=0))
        plain = jnp.take_along_axis(table, order, axis=1)
        put(PERMS, jnp.concatenate([plain, plain], axis=0))


def design_rows(age, codes, perms):
    subjects = age.shape[0]
    return pl.pallas_call(
        designs_kernel,
        out_shape=jax.ShapeDtypeStruct((3 * GROUP, 3 * subjects), BF16),
        cost_estimate=pl.CostEstimate(flops=4 * 10**6, bytes_accessed=800_000, transcendentals=0),
        name="design_rows",
    )(age.reshape(1, subjects), codes.reshape(1, subjects), perms)


def stats_kernel(senders, code_ref, rows_ref, tmap_ref, peaks_ref, value_ref, y_ref, sum_ref, rss_ref, top_ref, best_ref):
    subjects = PER * senders
    lane = lax.broadcasted_iota(jnp.int32, (subjects, LANES), 1)
    shift = (lax.axis_index("subj") // 2 % (LANES // BLOCK)) * BLOCK
    per = 4 * CHUNK

    def unpack(i, carry):
        at = pl.ds(pl.multiple_of(i * per, 32), per)
        value_ref[at, :] = decode(code_ref[at, :].astype(F32))
        return carry

    lax.fori_loop(0, senders * CHUNK // per, unpack, 0)

    def gathered(offsets):
        return jnp.concatenate(
            [value_ref[pl.ds(offset, senders, stride=CHUNK), :] for offset in offsets], axis=0
        )

    def place(block, y):
        y = y - jnp.sum(y, axis=0, keepdims=True) * (1.0 / subjects)
        at = slice(block * LANES, (block + 1) * LANES)
        sum_ref[0:1, at] = jnp.sum(y * y, axis=0, keepdims=True)
        high = y.astype(BF16)
        y_ref[0:subjects, at] = high
        y_ref[subjects : 2 * subjects, at] = (y - high.astype(F32)).astype(BF16)
        y_ref[2 * subjects : 3 * subjects, at] = high

    extra = PER * BLOCK
    for r in range(BLOCK):
        place(r, gathered([r, BLOCK + r]))
    for h in range(2):
        place(BLOCK + h, gathered([extra + h, extra + 4 + h]))
    first = pltpu.roll(gathered([extra + 2, extra + 6]), LANES - shift, 1)
    second = pltpu.roll(gathered([extra + 3, extra + 7]), LANES + BLOCK - shift, 1)
    place(BLOCK + 2, jnp.where(lane < BLOCK, first, jnp.where(lane < 2 * BLOCK, second, 0.0)))

    blocks = BLOCK + 3
    for start in range(0, blocks, 2):
        at = slice(start * LANES, min(start + 2, blocks) * LANES)
        proj = jnp.dot(rows_ref[...], y_ref[:, at], preferred_element_type=F32)
        q1, q2, q3 = (proj[k * GROUP : (k + 1) * GROUP] for k in range(3))
        rss_ref[:, at] = sum_ref[0:1, at] - q1 * q1 - q2 * q2 - q3 * q3
        top_ref[:, at] = q3

    here = lax.broadcasted_iota(jnp.int32, (8, LANES), 1)
    scale = 1.0 / (subjects - 4)

    def pseudo_t(g, r):
        at = pl.ds(pl.multiple_of(g * 8, 8), 8)

        def block(b):
            return rss_ref[at, b * LANES : (b + 1) * LANES]

        mine = block(r)
        above = block(r - 1 if r > 0 else BLOCK)
        below = block(r + 1 if r < BLOCK - 1 else BLOCK + 1)
        ends = jnp.take_along_axis(
            block(BLOCK + 2), jnp.where(here == 0, r, jnp.where(here == LANES - 1, BLOCK + r, 0)), axis=1
        )
        before = jnp.where(here == 0, ends, pltpu.roll(mine, 1, 1))
        after = jnp.where(here == LANES - 1, ends, pltpu.roll(mine, LANES - 1, 1))
        beside = (above + below) + (before + after)
        variance = (0.4 * scale) * mine + (0.15 * scale) * beside + 1e-06
        return top_ref[at, r * LANES : (r + 1) * LANES] * lax.rsqrt(variance)

    def body(g, carry):
        best = jnp.zeros((8, LANES), F32)
        for r in range(BLOCK):
            best = jnp.maximum(best, jnp.abs(pseudo_t(g, r)))
        best_ref[pl.ds(pl.multiple_of(g * 8, 8), 8), :] = best
        return carry

    lax.fori_loop(0, PERMS // 8, body, 0)
    for r in range(BLOCK):
        tmap_ref[r : r + 1, :] = pseudo_t(PERMS // 8, r)[0:1, :]
    peaks_ref[...] = jnp.max(best_ref[...].T, axis=0, keepdims=True)


def block_stats(codes, rows, senders):
    subjects = PER * senders
    columns = (BLOCK + 3) * LANES
    return pl.pallas_call(
        functools.partial(stats_kernel, senders),
        out_shape=(
            jax.ShapeDtypeStruct((BLOCK, LANES), F32),
            jax.ShapeDtypeStruct((1, PERMS), F32),
        ),
        scratch_shapes=[
            pltpu.VMEM((senders * CHUNK, LANES), F32),
            pltpu.VMEM((3 * subjects, columns), BF16),
            pltpu.VMEM((8, columns), F32),
            pltpu.VMEM((GROUP, columns), F32),
            pltpu.VMEM((GROUP, columns), F32),
            pltpu.VMEM((PERMS, LANES), F32),
        ],
        compiler_params=pltpu.CompilerParams(vmem_limit_bytes=32 * 2**20),
        cost_estimate=pl.CostEstimate(flops=2 * 10**9, bytes_accessed=10**6, transcendentals=10**6),
        name="block_stats",
    )(codes, rows)


def on_device(displacement, age, group_codes, perms):
    senders = lax.axis_size("subj")
    strips = lax.axis_size("strip")
    own = strip_edges(displacement)
    left = lax.ppermute(own, "strip", [(i, i + 1) for i in range(strips - 1)])
    right = lax.ppermute(own, "strip", [(i + 1, i) for i in range(strips - 1)])
    log = inner_log(displacement)
    rows = design_rows(age, group_codes, perms)
    sent = chunked(log, own, left, right, senders)
    codes = lax.all_to_all(
        sent.reshape(senders, CHUNK, LANES), "subj", split_axis=0, concat_axis=0, tiled=True
    )
    tested, peaks = block_stats(codes.reshape(senders * CHUNK, LANES), rows, senders)

    odd = lax.axis_index("subj") % 2 == 1
    low, high = tested[: BLOCK // 2], tested[BLOCK // 2 :]
    kept = jnp.where(odd, high, low)
    swapped = lax.ppermute(
        jnp.where(odd, low, high), "subj", [(i, i ^ 1) for i in range(senders)]
    )
    t_map = jnp.stack([jnp.where(odd, swapped, kept), jnp.where(odd, kept, swapped)])

    everyone = senders * strips
    mine = jnp.broadcast_to(peaks.astype(jnp.float16).reshape(1, 2, LANES), (everyone, 2, LANES))
    theirs = lax.all_to_all(mine, ("subj", "strip"), split_axis=0, concat_axis=0, tiled=True)
    return t_map, jnp.max(theirs, axis=0).astype(F32).reshape(PERMS)


def solution(mesh):
    placed = (P("subj", None, None, None, "strip"), P(), P(), P())
    return jax.shard_map(
        on_device,
        mesh=mesh,
        in_specs=placed,
        out_specs=(P(None, "subj", "strip"), P()),
        check_vma=False,
    )
```

```python
import functools

import jax
import jax.numpy as jnp
from jax import lax
from jax.experimental import pallas as pl
from jax.experimental.pallas import tpu as pltpu
from jax.sharding import PartitionSpec as P

F32, BF16, I16 = jnp.float32, jnp.bfloat16, jnp.int16
LANES = 128
ROWS = 512
BLOCK = 16
MAIN, TAIL = 32, 8
CHUNK = MAIN + TAIL
PAIR = 2 * CHUNK
PER = 2
COMPS, PLANES = 3, 4
PERMS, GROUP = 256, 272
REACH = 0.6
LEVELS = 32767.0
CENTRE = 0.4 / 0.15
FLOOR = 1e-06 / (CENTRE + 4.0)


def encode(y):
    half = y * lax.rsqrt(jnp.maximum(jnp.abs(y), 1e-30))
    fourth = half * lax.rsqrt(jnp.maximum(jnp.abs(half), 1e-15))
    shift = 1.5 * 2.0**23
    return (fourth * (LEVELS / REACH**0.25) + shift) - shift


def decode(code):
    part = code * (REACH**0.25 / LEVELS)
    return (part * jnp.abs(part)) * (part * part)


def packed(code):
    return code.astype(jnp.int32).astype(I16)


def log_det(dz, dx, dy):
    j00, j01, j02 = 2.0 + dz[0], dx[0], dy[0]
    j10, j11, j12 = dz[1], 2.0 + dx[1], dy[1]
    j20, j21, j22 = dz[2], dx[2], 2.0 + dy[2]
    det = (
        j00 * (j11 * j22 - j12 * j21)
        - j01 * (j10 * j22 - j12 * j20)
        + j02 * (j10 * j21 - j11 * j20)
    )
    return jnp.log(det * 0.125)


def edges_kernel(disp_ref, low_ref, high_ref):
    row = lax.broadcasted_iota(jnp.int32, (32, 2 * LANES), 0)
    lane = lax.broadcasted_iota(jnp.int32, (32, 2 * LANES), 1)
    column = jnp.where(row < 16, row // 8, row // 8 - 2 + LANES - 2)
    for c in range(COMPS):
        acc = jnp.zeros((32, low_ref.shape[1]), F32)
        for q in range(PLANES):
            pick = ((row % 8 == 2 * q + lane // LANES) & (lane % LANES == column)).astype(F32)
            both = jnp.concatenate([disp_ref[0, c, q], disp_ref[1, c, q]], axis=1)
            acc = acc + lax.dot_general(
                pick.astype(BF16), both, (((1,), (1,)), ((), ())), preferred_element_type=F32
            )
        low_ref[c * 16 : c * 16 + 16, :] = acc[0:16].astype(BF16)
        high_ref[c * 16 : c * 16 + 16, :] = acc[16:32].astype(BF16)


def strip_edges(disp):
    rows = 256
    out = jax.ShapeDtypeStruct((COMPS * 16, ROWS), BF16)
    return pl.pallas_call(
        edges_kernel,
        grid=(ROWS // rows,),
        in_specs=[pl.BlockSpec((PER, COMPS, PLANES, rows, LANES), lambda i: (0, 0, 0, i, 0))],
        out_specs=[pl.BlockSpec((COMPS * 16, rows), lambda i: (0, i))] * 2,
        out_shape=(out, out),
        compiler_params=pltpu.CompilerParams(vmem_limit_bytes=8 * 2**20),
        cost_estimate=pl.CostEstimate(flops=10**8, bytes_accessed=3_200_000, transcendentals=0),
        name="strip_edges",
    )(disp)


def inner_kernel(disp_ref, out_ref, beside_ref, field_ref, pad_ref, code_ref, in_sem):
    pad, step, parts = 8, 16, 4
    rows = ROWS // parts
    zeros = jnp.zeros((pad, LANES), F32)
    copies = [
        [
            pltpu.make_async_copy(
                disp_ref.at[s, :, :, h * rows : (h + 1) * rows, :],
                field_ref.at[s, :, :, h * rows : (h + 1) * rows, :],
                in_sem.at[s, h],
            )
            for h in range(parts)
        ]
        for s in range(PER)
    ]
    for s in range(PER):
        for h in range(parts):
            copies[s][h].start()
    for k in range(2):
        code_ref[k, 0:pad, :] = zeros
        code_ref[k, pad + ROWS : 2 * pad + ROWS, :] = zeros
        for c in range(COMPS):
            pad_ref[k, c, 0:pad, :] = zeros
            pad_ref[k, c, pad + ROWS : 2 * pad + ROWS, :] = zeros

    for s in range(PER):
        for h in range(parts + 1):
            if h < parts:
                copies[s][h].wait()
                for p in range(2):
                    for c in range(COMPS):
                        pad_ref[p, c, pad + h * rows : pad + (h + 1) * rows, :] = field_ref[
                            s, c, 1 + p, h * rows : (h + 1) * rows, :
                        ].astype(F32)
            if h > 0:

                def body(i, carry):
                    base = pl.multiple_of(i * step, step)
                    for p in range(2):
                        dz, dx, dy = [], [], []
                        for c in range(COMPS):
                            up = field_ref[s, c, p + 2, pl.ds(base, step), :].astype(F32)
                            down = field_ref[s, c, p, pl.ds(base, step), :].astype(F32)
                            dz.append(up - down)
                            center = pad_ref[p, c, pl.ds(base + pad, step), :]
                            dx.append(
                                pad_ref[p, c, pl.ds(base + pad + 1, step), :]
                                - pad_ref[p, c, pl.ds(base + pad - 1, step), :]
                            )
                            dy.append(pltpu.roll(center, LANES - 1, 1) - pltpu.roll(center, 1, 1))
                        code = encode(log_det(dz, dx, dy))
                        code_ref[p, pl.ds(base + pad, step), :] = code
                        out_ref[i, 48 * p + 16 * s : 48 * p + 16 * s + 16, :] = packed(code)
                    return carry

                many = rows // step
                lax.fori_loop((h - 1) * many, h * many, body, 0, unroll=many)
        blocks = ROWS // BLOCK
        for p in range(2):
            beside_ref[2 * p + s, 0] = code_ref[p, pl.ds(pad - 1, blocks, stride=BLOCK), :]
            beside_ref[2 * p + s, 1] = code_ref[p, pl.ds(pad + BLOCK, blocks, stride=BLOCK), :]


def inner_codes(disp):
    blocks = ROWS // BLOCK
    return pl.pallas_call(
        inner_kernel,
        in_specs=[pl.BlockSpec(memory_space=pl.ANY)],
        out_shape=(
            jax.ShapeDtypeStruct((blocks, PAIR, LANES), I16),
            jax.ShapeDtypeStruct((2 * PER, 2, blocks, LANES), F32),
        ),
        scratch_shapes=[
            pltpu.VMEM((PER, COMPS, PLANES, ROWS, LANES), BF16),
            pltpu.VMEM((2, COMPS, ROWS + 16, LANES), F32),
            pltpu.VMEM((2, ROWS + 32, LANES), F32),
            pltpu.SemaphoreType.DMA((PER, 4)),
        ],
        compiler_params=pltpu.CompilerParams(vmem_limit_bytes=16 * 2**20),
        cost_estimate=pl.CostEstimate(flops=2 * 10**7, bytes_accessed=4_200_000, transcendentals=262144),
        name="inner_codes",
    )(disp)


def tail_kernel(low_ref, high_ref, left_ref, right_ref, beside_ref, chunk_ref, out_ref, pad_ref, side_ref, tail_ref, send_ref, sem):
    del chunk_ref
    strips = lax.axis_size("strip")
    me = lax.axis_index("strip")
    keep_left = (me > 0).astype(F32)
    keep_right = (me < strips - 1).astype(F32)
    lane = lax.broadcasted_iota(jnp.int32, (8, ROWS), 1)

    def columns(ref):
        return [[ref[16 * c + 8 * e : 16 * c + 8 * e + 8, :] for e in range(2)] for c in range(COMPS)]

    def codes(around):
        dz, dx, dy = [], [], []
        for before, center, after in around:
            dz.append(pltpu.roll(center, 6, 0) - pltpu.roll(center, 2, 0))
            dx.append(
                jnp.where(lane == ROWS - 1, 0.0, pltpu.roll(center, ROWS - 1, 1))
                - jnp.where(lane == 0, 0.0, pltpu.roll(center, 1, 1))
            )
            dy.append(after - before)
        return encode(log_det(dz, dx, dy))

    low, high, left, right = (
        columns(ref[...].astype(F32)) for ref in (low_ref, high_ref, left_ref, right_ref)
    )
    wide_left = [left[c] + low[c] for c in range(COMPS)]
    wide_right = [high[c] + right[c] for c in range(COMPS)]
    four = [
        codes([w[0:3] for w in wide_left]) * keep_left,
        codes([w[1:4] for w in wide_left]),
        codes([w[0:3] for w in wide_right]),
        codes([w[1:4] for w in wide_right]) * keep_right,
    ]
    zeros = jnp.zeros((8, LANES), F32)
    for k in range(4):
        pad_ref[k, :, 0:LANES] = zeros
        pad_ref[k, :, LANES : LANES + ROWS] = four[k]
        pad_ref[k, :, LANES + ROWS : 2 * LANES + ROWS] = zeros
    here = lax.broadcasted_iota(jnp.int32, (8, LANES), 1)
    blocks = ROWS // BLOCK
    for j in range(blocks):
        start = LANES + j * BLOCK - 1
        line = zeros
        for k in range(4):
            window, offset = start // LANES, start % LANES
            first = pltpu.roll(
                pad_ref[k, :, window * LANES : (window + 1) * LANES], (32 * k - offset) % LANES, 1
            )
            if offset + 18 > LANES:
                second = pltpu.roll(
                    pad_ref[k, :, (window + 1) * LANES : (window + 2) * LANES], (32 * k - offset) % LANES, 1
                )
                first = jnp.where(here - 32 * k < LANES - offset, first, second)
            line = first if k == 0 else jnp.where(here < 32 * k, line, first)
        side_ref[j * 8 : j * 8 + 8, :] = line
    for p in range(2):
        for s in range(PER):
            row = TAIL * p + 4 * s
            for h in range(2):
                tail_ref[pl.ds(row + h, blocks, stride=2 * TAIL), :] = beside_ref[2 * p + s, h]
            tail_ref[pl.ds(row + 2, blocks, stride=2 * TAIL), :] = side_ref[
                pl.ds(2 + 2 * p + s, blocks, stride=8), :
            ]
            tail_ref[pl.ds(row + 3, blocks, stride=2 * TAIL), :] = jnp.zeros((blocks, LANES), F32)
    send_ref[...] = packed(tail_ref[0 : blocks * 2 * TAIL, :]).reshape(blocks, 2 * TAIL, LANES)
    copy = pltpu.make_async_copy(send_ref, out_ref.at[:, MAIN : MAIN + 2 * TAIL, :], sem)
    copy.start()
    copy.wait()


def with_tails(low, high, left, right, beside, chunks):
    blocks = ROWS // BLOCK
    vmem = pl.BlockSpec(memory_space=pltpu.VMEM)
    anywhere = pl.BlockSpec(memory_space=pl.ANY)
    return pl.pallas_call(
        tail_kernel,
        in_specs=[vmem] * 5 + [anywhere],
        out_specs=anywhere,
        out_shape=jax.ShapeDtypeStruct(chunks.shape, chunks.dtype),
        input_output_aliases={5: 0},
        scratch_shapes=[
            pltpu.VMEM((4, 8, ROWS + 2 * LANES), F32),
            pltpu.VMEM((blocks * 8 + 8, LANES), F32),
            pltpu.VMEM((blocks * 2 * TAIL + 16, LANES), F32),
            pltpu.VMEM((blocks, 2 * TAIL, LANES), I16),
            pltpu.SemaphoreType.DMA,
        ],
        compiler_params=pltpu.CompilerParams(vmem_limit_bytes=8 * 2**20),
        cost_estimate=pl.CostEstimate(flops=10**6, bytes_accessed=5 * 10**5, transcendentals=5 * 10**4),
        name="with_tails",
    )(low, high, left, right, beside, chunks)


def designs_kernel(age_ref, code_ref, perms_ref, out_ref):
    subjects = age_ref.shape[1]
    half = subjects // PER

    def total(v):
        return jnp.sum(v, axis=1, keepdims=True)

    def centred(v):
        return v - total(v) * (1.0 / subjects)

    basis = []
    for raw in (
        (code_ref[...] == 1).astype(F32),
        age_ref[...],
        (code_ref[...] == 2).astype(F32),
    ):
        v = centred(raw)
        for _ in range(2):
            for q in basis:
                v = v - q * total(q * v)
            v = centred(v)
        basis.append(v / jnp.sqrt(total(v * v)))
    scale = (0.15 / (subjects - 4)) ** 0.5
    lane = lax.broadcasted_iota(jnp.int32, (8, subjects), 1)
    order = PER * (lane % half) + lane // half
    for k, q in enumerate(basis):
        table = jnp.broadcast_to(q * scale, (8, subjects))

        def put(row, values):
            high = values.astype(BF16)
            rest = (values - high.astype(F32)).astype(BF16)
            at = pl.ds(k * GROUP + row, 16)
            out_ref[at, 0:subjects] = high
            out_ref[at, subjects : 2 * subjects] = high
            out_ref[at, 2 * subjects : 3 * subjects] = rest

        for g in range(PERMS // 16):
            two = []
            for h in range(2):
                who = jnp.take_along_axis(perms_ref[g * 16 + h * 8 : g * 16 + h * 8 + 8, :], order, axis=1)
                two.append(jnp.take_along_axis(table, who, axis=1))
            put(g * 16, jnp.concatenate(two, axis=0))
        plain = jnp.take_along_axis(table, order, axis=1)
        put(PERMS, jnp.concatenate([plain, plain], axis=0))


def design_rows(age, codes, perms):
    subjects = age.shape[0]
    return pl.pallas_call(
        designs_kernel,
        out_shape=jax.ShapeDtypeStruct((3 * GROUP, 3 * subjects), BF16),
        compiler_params=pltpu.CompilerParams(vmem_limit_bytes=8 * 2**20),
        cost_estimate=pl.CostEstimate(flops=4 * 10**6, bytes_accessed=800_000, transcendentals=0),
        name="design_rows",
    )(age.reshape(1, subjects), codes.reshape(1, subjects), perms)


def stats_kernel(senders, code_ref, rows_ref, tmap_ref, peaks_ref, value_ref, y_ref, sum_ref, rss_ref, top_ref, best_ref):
    subjects = PER * senders
    lane = lax.broadcasted_iota(jnp.int32, (subjects, LANES), 1)
    odd = lax.axis_index("subj") % 2
    main = odd * TAIL
    tail = (1 - odd) * MAIN
    per = 4 * CHUNK

    def unpack(i, carry):
        at = pl.ds(pl.multiple_of(i * per, 32), per)
        value_ref[at, :] = decode(code_ref[at, :].astype(F32))
        return carry

    lax.fori_loop(0, senders * CHUNK // per, unpack, 0)

    def gathered(offsets):
        return jnp.concatenate(
            [value_ref[pl.ds(offset, senders, stride=CHUNK), :] for offset in offsets], axis=0
        )

    def place(block, y):
        y = y - jnp.sum(y, axis=0, keepdims=True) * (1.0 / subjects)
        at = pl.ds(pl.multiple_of(block * LANES, LANES), LANES)
        sum_ref[0:1, at] = jnp.sum(y * y, axis=0, keepdims=True) * (0.15 / (subjects - 4)) + FLOOR
        high = y.astype(BF16)
        y_ref[0:subjects, at] = high
        y_ref[subjects : 2 * subjects, at] = (y - high.astype(F32)).astype(BF16)
        y_ref[2 * subjects : 3 * subjects, at] = high

    sides = gathered([tail + 2, tail + 6])

    def mended(y, r):
        index = jnp.where(lane == 0, 33 + r, jnp.where(lane == LANES - 1, 65 + r, 0))
        ends = jnp.take_along_axis(sides, index, axis=1)
        return jnp.where((lane == 0) | (lane == LANES - 1), ends, y)

    def place_row(r, carry):
        place(r, mended(gathered([main + r, main + BLOCK + r]), r))
        return carry

    lax.fori_loop(0, BLOCK, place_row, 0, unroll=8)
    place(BLOCK, mended(gathered([tail, tail + 4]), -1))
    place(BLOCK + 1, mended(gathered([tail + 1, tail + 5]), BLOCK))
    place(BLOCK + 2, sides)

    blocks = BLOCK + 3
    for start in range(0, blocks, 2):
        at = slice(start * LANES, min(start + 2, blocks) * LANES)
        proj = jnp.dot(rows_ref[...], y_ref[:, at], preferred_element_type=F32)
        q1, q2, q3 = (proj[k * GROUP : (k + 1) * GROUP] for k in range(3))
        rss_ref[:, at] = sum_ref[0:1, at] - q1 * q1 - q2 * q2 - q3 * q3
        top_ref[:, at] = q3

    here = lax.broadcasted_iota(jnp.int32, (8, LANES), 1)
    unscale = ((subjects - 4) / 0.15) ** 0.5

    def pseudo_t(g, r):
        at = pl.ds(pl.multiple_of(g * 8, 8), 8)

        def block(b):
            return rss_ref[at, b * LANES : (b + 1) * LANES]

        mine = block(r)
        above = block(r - 1 if r > 0 else BLOCK)
        below = block(r + 1 if r < BLOCK - 1 else BLOCK + 1)
        ends = jnp.take_along_axis(
            block(BLOCK + 2), jnp.where(here == 0, 1 + r, jnp.where(here == LANES - 1, 97 + r, 0)), axis=1
        )
        before = jnp.where(here == 0, ends, pltpu.roll(mine, 1, 1))
        after = jnp.where(here == LANES - 1, ends, pltpu.roll(mine, LANES - 1, 1))
        beside = (above + below) + (before + after)
        variance = CENTRE * mine + beside
        return top_ref[at, r * LANES : (r + 1) * LANES] * lax.rsqrt(variance)

    def body(g, carry):
        best = jnp.zeros((8, LANES), F32)
        for r in range(BLOCK):
            best = jnp.maximum(best, jnp.abs(pseudo_t(g, r)))
        best_ref[pl.ds(pl.multiple_of(g * 8, 8), 8), :] = best
        return carry

    lax.fori_loop(0, PERMS // 8, body, 0, unroll=8)
    for r in range(BLOCK):
        tmap_ref[r : r + 1, :] = pseudo_t(PERMS // 8, r)[0:1, :] * unscale
    peaks_ref[...] = jnp.max(best_ref[...].T, axis=0, keepdims=True) * unscale


def block_stats(codes, rows, senders):
    subjects = PER * senders
    columns = (BLOCK + 3) * LANES
    return pl.pallas_call(
        functools.partial(stats_kernel, senders),
        out_shape=(
            jax.ShapeDtypeStruct((BLOCK, LANES), F32),
            jax.ShapeDtypeStruct((1, PERMS), F32),
        ),
        scratch_shapes=[
            pltpu.VMEM((senders * CHUNK + CHUNK, LANES), F32),
            pltpu.VMEM((3 * subjects, columns), BF16),
            pltpu.VMEM((8, columns), F32),
            pltpu.VMEM((GROUP, columns), F32),
            pltpu.VMEM((GROUP, columns), F32),
            pltpu.VMEM((PERMS, LANES), F32),
        ],
        compiler_params=pltpu.CompilerParams(vmem_limit_bytes=24 * 2**20),
        cost_estimate=pl.CostEstimate(flops=2 * 10**9, bytes_accessed=10**6, transcendentals=10**6),
        name="block_stats",
    )(codes, rows)


def on_device(displacement, age, group_codes, perms):
    senders = lax.axis_size("subj")
    strips = lax.axis_size("strip")
    low, high = strip_edges(displacement)
    left = lax.ppermute(high, "strip", [(i, i + 1) for i in range(strips - 1)])
    right = lax.ppermute(low, "strip", [(i + 1, i) for i in range(strips - 1)])
    chunks, beside = inner_codes(displacement)
    rows = design_rows(age, group_codes, perms)
    sent = with_tails(low, high, left, right, beside, chunks)
    codes = lax.all_to_all(
        sent.reshape(senders, CHUNK, LANES), "subj", split_axis=0, concat_axis=0, tiled=True
    )
    tested, peaks = block_stats(codes.reshape(senders * CHUNK, LANES), rows, senders)

    odd = lax.axis_index("subj") % 2 == 1
    low, high = tested[: BLOCK // 2], tested[BLOCK // 2 :]
    kept = jnp.where(odd, high, low)
    swapped = lax.ppermute(
        jnp.where(odd, low, high), "subj", [(i, i ^ 1) for i in range(senders)]
    )
    t_map = jnp.stack([jnp.where(odd, swapped, kept), jnp.where(odd, kept, swapped)])

    everyone = senders * strips
    mine = jnp.broadcast_to(peaks.astype(jnp.float16).reshape(1, 2, LANES), (everyone, 2, LANES))
    theirs = lax.all_to_all(mine, ("subj", "strip"), split_axis=0, concat_axis=0, tiled=True)
    return t_map, jnp.max(theirs, axis=0).astype(F32).reshape(PERMS)


def solution(mesh):
    placed = (P("subj", None, None, None, "strip"), P(), P(), P())
    return jax.shard_map(
        on_device,
        mesh=mesh,
        in_specs=placed,
        out_specs=(P(None, "subj", "strip"), P()),
        check_vma=False,
    )
```

```python
import functools

import jax
import jax.numpy as jnp
from jax import lax
from jax.experimental import pallas as pl
from jax.experimental.pallas import tpu as pltpu
from jax.sharding import PartitionSpec as P

F32, BF16, I16 = jnp.float32, jnp.bfloat16, jnp.int16
LANES = 128
ROWS = 512
BLOCK = 16
MAIN, TAIL = 32, 8
CHUNK = MAIN + TAIL
PAIR = 2 * CHUNK
PER = 2
COMPS, PLANES = 3, 4
PERMS, GROUP = 256, 272
REACH = 0.6
REACH_T = 6800.0
LEVELS = 32767.0
CENTRE = 0.4 / 0.15
FLOOR = 1e-06 / (CENTRE + 4.0)


def encode(y):
    half = y * lax.rsqrt(jnp.maximum(jnp.abs(y), 1e-30))
    fourth = half * lax.rsqrt(jnp.maximum(jnp.abs(half), 1e-15))
    shift = 1.5 * 2.0**23
    return (fourth * (LEVELS / REACH**0.25) + shift) - shift


def decode(code):
    part = code * (REACH**0.25 / LEVELS)
    return (part * jnp.abs(part)) * (part * part)


def packed(code):
    return code.astype(jnp.int32).astype(I16)


def log_det(dz, dx, dy):
    j00, j01, j02 = 2.0 + dz[0], dx[0], dy[0]
    j10, j11, j12 = dz[1], 2.0 + dx[1], dy[1]
    j20, j21, j22 = dz[2], dx[2], 2.0 + dy[2]
    det = (
        j00 * (j11 * j22 - j12 * j21)
        - j01 * (j10 * j22 - j12 * j20)
        + j02 * (j10 * j21 - j11 * j20)
    )
    return jnp.log(det * 0.125)


def edges_kernel(disp_ref, low_ref, high_ref):
    row = lax.broadcasted_iota(jnp.int32, (32, 2 * LANES), 0)
    lane = lax.broadcasted_iota(jnp.int32, (32, 2 * LANES), 1)
    column = jnp.where(row < 16, row // 8, row // 8 - 2 + LANES - 2)
    for c in range(COMPS):
        acc = jnp.zeros((32, low_ref.shape[1]), F32)
        for q in range(PLANES):
            pick = ((row % 8 == 2 * q + lane // LANES) & (lane % LANES == column)).astype(F32)
            both = jnp.concatenate([disp_ref[0, c, q], disp_ref[1, c, q]], axis=1)
            acc = acc + lax.dot_general(
                pick.astype(BF16), both, (((1,), (1,)), ((), ())), preferred_element_type=F32
            )
        low_ref[c * 16 : c * 16 + 16, :] = acc[0:16].astype(BF16)
        high_ref[c * 16 : c * 16 + 16, :] = acc[16:32].astype(BF16)


def strip_edges(disp):
    rows = 256
    out = jax.ShapeDtypeStruct((COMPS * 16, ROWS), BF16)
    return pl.pallas_call(
        edges_kernel,
        grid=(ROWS // rows,),
        in_specs=[pl.BlockSpec((PER, COMPS, PLANES, rows, LANES), lambda i: (0, 0, 0, i, 0))],
        out_specs=[pl.BlockSpec((COMPS * 16, rows), lambda i: (0, i))] * 2,
        out_shape=(out, out),
        compiler_params=pltpu.CompilerParams(vmem_limit_bytes=8 * 2**20),
        cost_estimate=pl.CostEstimate(flops=10**8, bytes_accessed=3_200_000, transcendentals=0),
        name="strip_edges",
    )(disp)


def inner_kernel(disp_ref, out_ref, beside_ref, field_ref, pad_ref, code_ref, in_sem):
    pad, step, parts = 8, 16, 4
    rows = ROWS // parts
    zeros = jnp.zeros((pad, LANES), F32)
    copies = [
        [
            pltpu.make_async_copy(
                disp_ref.at[s, :, :, h * rows : (h + 1) * rows, :],
                field_ref.at[s, :, :, h * rows : (h + 1) * rows, :],
                in_sem.at[s, h],
            )
            for h in range(parts)
        ]
        for s in range(PER)
    ]
    for s in range(PER):
        for h in range(parts):
            copies[s][h].start()
    for k in range(2):
        code_ref[k, 0:pad, :] = zeros
        code_ref[k, pad + ROWS : 2 * pad + ROWS, :] = zeros
        for c in range(COMPS):
            pad_ref[k, c, 0:pad, :] = zeros
            pad_ref[k, c, pad + ROWS : 2 * pad + ROWS, :] = zeros

    for s in range(PER):
        for h in range(parts + 1):
            if h < parts:
                copies[s][h].wait()
                for p in range(2):
                    for c in range(COMPS):
                        pad_ref[p, c, pad + h * rows : pad + (h + 1) * rows, :] = field_ref[
                            s, c, 1 + p, h * rows : (h + 1) * rows, :
                        ].astype(F32)
            if h > 0:

                def body(i, carry):
                    base = pl.multiple_of(i * step, step)
                    for p in range(2):
                        dz, dx, dy = [], [], []
                        for c in range(COMPS):
                            up = field_ref[s, c, p + 2, pl.ds(base, step), :].astype(F32)
                            down = field_ref[s, c, p, pl.ds(base, step), :].astype(F32)
                            dz.append(up - down)
                            center = pad_ref[p, c, pl.ds(base + pad, step), :]
                            dx.append(
                                pad_ref[p, c, pl.ds(base + pad + 1, step), :]
                                - pad_ref[p, c, pl.ds(base + pad - 1, step), :]
                            )
                            dy.append(pltpu.roll(center, LANES - 1, 1) - pltpu.roll(center, 1, 1))
                        code = encode(log_det(dz, dx, dy))
                        code_ref[p, pl.ds(base + pad, step), :] = code
                        out_ref[i, 48 * p + 16 * s : 48 * p + 16 * s + 16, :] = packed(code)
                    return carry

                many = rows // step
                lax.fori_loop((h - 1) * many, h * many, body, 0, unroll=many)
        blocks = ROWS // BLOCK
        for p in range(2):
            beside_ref[2 * p + s, 0] = code_ref[p, pl.ds(pad - 1, blocks, stride=BLOCK), :]
            beside_ref[2 * p + s, 1] = code_ref[p, pl.ds(pad + BLOCK, blocks, stride=BLOCK), :]


def inner_codes(disp):
    blocks = ROWS // BLOCK
    return pl.pallas_call(
        inner_kernel,
        in_specs=[pl.BlockSpec(memory_space=pl.ANY)],
        out_shape=(
            jax.ShapeDtypeStruct((blocks, PAIR, LANES), I16),
            jax.ShapeDtypeStruct((2 * PER, 2, blocks, LANES), F32),
        ),
        scratch_shapes=[
            pltpu.VMEM((PER, COMPS, PLANES, ROWS, LANES), BF16),
            pltpu.VMEM((2, COMPS, ROWS + 16, LANES), F32),
            pltpu.VMEM((2, ROWS + 32, LANES), F32),
            pltpu.SemaphoreType.DMA((PER, 4)),
        ],
        compiler_params=pltpu.CompilerParams(vmem_limit_bytes=16 * 2**20),
        cost_estimate=pl.CostEstimate(flops=2 * 10**7, bytes_accessed=4_200_000, transcendentals=262144),
        name="inner_codes",
    )(disp)


def tail_kernel(low_ref, high_ref, left_ref, right_ref, beside_ref, chunk_ref, out_ref, pad_ref, side_ref, tail_ref, send_ref, sem):
    del chunk_ref
    strips = lax.axis_size("strip")
    me = lax.axis_index("strip")
    keep_left = (me > 0).astype(F32)
    keep_right = (me < strips - 1).astype(F32)
    lane = lax.broadcasted_iota(jnp.int32, (8, ROWS), 1)

    def columns(ref):
        return [[ref[16 * c + 8 * e : 16 * c + 8 * e + 8, :] for e in range(2)] for c in range(COMPS)]

    def codes(around):
        dz, dx, dy = [], [], []
        for before, center, after in around:
            dz.append(pltpu.roll(center, 6, 0) - pltpu.roll(center, 2, 0))
            dx.append(
                jnp.where(lane == ROWS - 1, 0.0, pltpu.roll(center, ROWS - 1, 1))
                - jnp.where(lane == 0, 0.0, pltpu.roll(center, 1, 1))
            )
            dy.append(after - before)
        return encode(log_det(dz, dx, dy))

    low, high, left, right = (
        columns(ref[...].astype(F32)) for ref in (low_ref, high_ref, left_ref, right_ref)
    )
    wide_left = [left[c] + low[c] for c in range(COMPS)]
    wide_right = [high[c] + right[c] for c in range(COMPS)]
    four = [
        codes([w[0:3] for w in wide_left]) * keep_left,
        codes([w[1:4] for w in wide_left]),
        codes([w[0:3] for w in wide_right]),
        codes([w[1:4] for w in wide_right]) * keep_right,
    ]
    zeros = jnp.zeros((8, LANES), F32)
    for k in range(4):
        pad_ref[k, :, 0:LANES] = zeros
        pad_ref[k, :, LANES : LANES + ROWS] = four[k]
        pad_ref[k, :, LANES + ROWS : 2 * LANES + ROWS] = zeros
    here = lax.broadcasted_iota(jnp.int32, (8, LANES), 1)
    blocks = ROWS // BLOCK
    for j in range(blocks):
        start = LANES + j * BLOCK - 1
        line = zeros
        for k in range(4):
            window, offset = start // LANES, start % LANES
            first = pltpu.roll(
                pad_ref[k, :, window * LANES : (window + 1) * LANES], (32 * k - offset) % LANES, 1
            )
            if offset + 18 > LANES:
                second = pltpu.roll(
                    pad_ref[k, :, (window + 1) * LANES : (window + 2) * LANES], (32 * k - offset) % LANES, 1
                )
                first = jnp.where(here - 32 * k < LANES - offset, first, second)
            line = first if k == 0 else jnp.where(here < 32 * k, line, first)
        side_ref[j * 8 : j * 8 + 8, :] = line
    for p in range(2):
        for s in range(PER):
            row = TAIL * p + 4 * s
            for h in range(2):
                tail_ref[pl.ds(row + h, blocks, stride=2 * TAIL), :] = beside_ref[2 * p + s, h]
            tail_ref[pl.ds(row + 2, blocks, stride=2 * TAIL), :] = side_ref[
                pl.ds(2 + 2 * p + s, blocks, stride=8), :
            ]
            tail_ref[pl.ds(row + 3, blocks, stride=2 * TAIL), :] = jnp.zeros((blocks, LANES), F32)
    send_ref[...] = packed(tail_ref[0 : blocks * 2 * TAIL, :]).reshape(blocks, 2 * TAIL, LANES)
    copy = pltpu.make_async_copy(send_ref, out_ref.at[:, MAIN : MAIN + 2 * TAIL, :], sem)
    copy.start()
    copy.wait()


def with_tails(low, high, left, right, beside, chunks):
    blocks = ROWS // BLOCK
    vmem = pl.BlockSpec(memory_space=pltpu.VMEM)
    anywhere = pl.BlockSpec(memory_space=pl.ANY)
    return pl.pallas_call(
        tail_kernel,
        in_specs=[vmem] * 5 + [anywhere],
        out_specs=anywhere,
        out_shape=jax.ShapeDtypeStruct(chunks.shape, chunks.dtype),
        input_output_aliases={5: 0},
        scratch_shapes=[
            pltpu.VMEM((4, 8, ROWS + 2 * LANES), F32),
            pltpu.VMEM((blocks * 8 + 8, LANES), F32),
            pltpu.VMEM((blocks * 2 * TAIL + 16, LANES), F32),
            pltpu.VMEM((blocks, 2 * TAIL, LANES), I16),
            pltpu.SemaphoreType.DMA,
        ],
        compiler_params=pltpu.CompilerParams(vmem_limit_bytes=8 * 2**20),
        cost_estimate=pl.CostEstimate(flops=10**6, bytes_accessed=5 * 10**5, transcendentals=5 * 10**4),
        name="with_tails",
    )(low, high, left, right, beside, chunks)


def designs_kernel(age_ref, code_ref, perms_ref, out_ref):
    subjects = age_ref.shape[1]
    half = subjects // PER

    def total(v):
        return jnp.sum(v, axis=1, keepdims=True)

    def centred(v):
        return v - total(v) * (1.0 / subjects)

    basis = []
    for raw in (
        (code_ref[...] == 1).astype(F32),
        age_ref[...],
        (code_ref[...] == 2).astype(F32),
    ):
        v = centred(raw)
        for _ in range(2):
            for q in basis:
                v = v - q * total(q * v)
            v = centred(v)
        basis.append(v / jnp.sqrt(total(v * v)))
    scale = (0.15 / (subjects - 4)) ** 0.5
    lane = lax.broadcasted_iota(jnp.int32, (8, subjects), 1)
    order = PER * (lane % half) + lane // half
    for k, q in enumerate(basis):
        table = jnp.broadcast_to(q * scale, (8, subjects))

        def put(row, values):
            high = values.astype(BF16)
            rest = (values - high.astype(F32)).astype(BF16)
            at = pl.ds(k * GROUP + row, 16)
            out_ref[at, 0:subjects] = high
            out_ref[at, subjects : 2 * subjects] = high
            out_ref[at, 2 * subjects : 3 * subjects] = rest

        for g in range(PERMS // 16):
            two = []
            for h in range(2):
                who = jnp.take_along_axis(perms_ref[g * 16 + h * 8 : g * 16 + h * 8 + 8, :], order, axis=1)
                two.append(jnp.take_along_axis(table, who, axis=1))
            put(g * 16, jnp.concatenate(two, axis=0))
        plain = jnp.take_along_axis(table, order, axis=1)
        put(PERMS, jnp.concatenate([plain, plain], axis=0))


def design_rows(age, codes, perms):
    subjects = age.shape[0]
    return pl.pallas_call(
        designs_kernel,
        out_shape=jax.ShapeDtypeStruct((3 * GROUP, 3 * subjects), BF16),
        compiler_params=pltpu.CompilerParams(vmem_limit_bytes=8 * 2**20),
        cost_estimate=pl.CostEstimate(flops=4 * 10**6, bytes_accessed=800_000, transcendentals=0),
        name="design_rows",
    )(age.reshape(1, subjects), codes.reshape(1, subjects), perms)


def stats_kernel(senders, code_ref, rows_ref, tmap_ref, peaks_ref, value_ref, y_ref, sum_ref, rss_ref, top_ref, best_ref):
    subjects = PER * senders
    lane = lax.broadcasted_iota(jnp.int32, (subjects, LANES), 1)
    odd = lax.axis_index("subj") % 2
    main = odd * TAIL
    tail = (1 - odd) * MAIN
    per = 4 * CHUNK

    def unpack(i, carry):
        at = pl.ds(pl.multiple_of(i * per, 32), per)
        value_ref[at, :] = decode(code_ref[at, :].astype(F32))
        return carry

    lax.fori_loop(0, senders * CHUNK // per, unpack, 0, unroll=4)

    def gathered(offsets):
        return jnp.concatenate(
            [value_ref[pl.ds(offset, senders, stride=CHUNK), :] for offset in offsets], axis=0
        )

    def place(block, y):
        y = y - jnp.sum(y, axis=0, keepdims=True) * (1.0 / subjects)
        at = pl.ds(pl.multiple_of(block * LANES, LANES), LANES)
        sum_ref[0:1, at] = jnp.sum(y * y, axis=0, keepdims=True) * (0.15 / (subjects - 4)) + FLOOR
        high = y.astype(BF16)
        y_ref[0:subjects, at] = high
        y_ref[subjects : 2 * subjects, at] = (y - high.astype(F32)).astype(BF16)
        y_ref[2 * subjects : 3 * subjects, at] = high

    far = lane // 2 + jnp.where(lane % 2 == 0, 97, 1)
    near = (lane - 36) // 2 + jnp.where(lane % 2 == 0, 64, 32)
    sides = jnp.take_along_axis(
        gathered([tail + 2, tail + 6]),
        jnp.where(lane < 32, far, jnp.where((lane >= 36) & (lane < 72), near, 0)),
        axis=1,
    )

    def mended(y, r):
        ends = pltpu.roll(sides, LANES - 39 - 2 * r, 1)
        return jnp.where((lane == 0) | (lane == LANES - 1), ends, y)

    for r in range(BLOCK):
        place(r, mended(gathered([main + r, main + BLOCK + r]), r))
    place(BLOCK, mended(gathered([tail, tail + 4]), -1))
    place(BLOCK + 1, mended(gathered([tail + 1, tail + 5]), BLOCK))
    place(BLOCK + 2, sides)

    blocks = BLOCK + 3
    for start in range(0, blocks, 2):
        at = slice(start * LANES, min(start + 2, blocks) * LANES)
        proj = jnp.dot(rows_ref[...], y_ref[:, at], preferred_element_type=F32)
        q1, q2, q3 = (proj[k * GROUP : (k + 1) * GROUP] for k in range(3))
        rss_ref[:, at] = sum_ref[0:1, at] - q1 * q1 - q2 * q2 - q3 * q3
        top_ref[:, at] = q3

    here = lax.broadcasted_iota(jnp.int32, (8, LANES), 1)
    unscale = ((subjects - 4) / 0.15) ** 0.5

    def pseudo_t(g, r):
        at = pl.ds(pl.multiple_of(g * 8, 8), 8)

        def block(b):
            return rss_ref[at, b * LANES : (b + 1) * LANES]

        mine = block(r)
        above = block(r - 1 if r > 0 else BLOCK)
        below = block(r + 1 if r < BLOCK - 1 else BLOCK + 1)
        ends = pltpu.roll(block(BLOCK + 2), LANES - 1 - 2 * r, 1)
        before = jnp.where(here == 0, ends, pltpu.roll(mine, 1, 1))
        after = jnp.where(here == LANES - 1, ends, pltpu.roll(mine, LANES - 1, 1))
        beside = (above + below) + (before + after)
        variance = CENTRE * mine + beside
        return top_ref[at, r * LANES : (r + 1) * LANES] * lax.rsqrt(variance)

    def body(g, carry):
        best = jnp.zeros((8, LANES), F32)
        for r in range(BLOCK):
            best = jnp.maximum(best, jnp.abs(pseudo_t(g, r)))
        best_ref[pl.ds(pl.multiple_of(g * 8, 8), 8), :] = best
        return carry

    lax.fori_loop(0, PERMS // 8, body, 0, unroll=32)
    half = BLOCK // 2
    for r in range(BLOCK):
        tmap_ref[(r // half + odd) % 2, r % half : r % half + 1, :] = (
            pseudo_t(PERMS // 8, r)[0:1, :] * unscale
        )
    code = jnp.max(best_ref[...].T, axis=0, keepdims=True) * (unscale / REACH_T)
    code = jnp.minimum(jnp.sqrt(jnp.sqrt(code)), 1.0) * LEVELS + 0.5
    lines = jnp.concatenate([code[:, k * LANES : (k + 1) * LANES] for k in range(PERMS // LANES)] * 4, axis=0)
    everyone = peaks_ref.shape[0]
    peaks_ref[...] = jnp.broadcast_to(packed(lines)[None], (everyone // 4, 8, LANES)).reshape(everyone, 2, LANES)


def block_stats(codes, rows, senders, everyone):
    subjects = PER * senders
    columns = (BLOCK + 3) * LANES
    return pl.pallas_call(
        functools.partial(stats_kernel, senders),
        out_shape=(
            jax.ShapeDtypeStruct((2, BLOCK // 2, LANES), F32),
            jax.ShapeDtypeStruct((everyone, PERMS // LANES, LANES), I16),
        ),
        scratch_shapes=[
            pltpu.VMEM((senders * CHUNK + CHUNK, LANES), F32),
            pltpu.VMEM((3 * subjects, columns), BF16),
            pltpu.VMEM((8, columns), F32),
            pltpu.VMEM((GROUP, columns), F32),
            pltpu.VMEM((GROUP, columns), F32),
            pltpu.VMEM((PERMS, LANES), F32),
        ],
        compiler_params=pltpu.CompilerParams(vmem_limit_bytes=24 * 2**20),
        cost_estimate=pl.CostEstimate(flops=2 * 10**9, bytes_accessed=10**6, transcendentals=10**6),
        name="block_stats",
    )(codes, rows)


def on_device(displacement, age, group_codes, perms):
    senders = lax.axis_size("subj")
    strips = lax.axis_size("strip")
    low, high = strip_edges(displacement)
    left = lax.ppermute(high, "strip", [(i, i + 1) for i in range(strips - 1)])
    right = lax.ppermute(low, "strip", [(i + 1, i) for i in range(strips - 1)])
    chunks, beside = inner_codes(displacement)
    rows = design_rows(age, group_codes, perms)
    sent = with_tails(low, high, left, right, beside, chunks)
    codes = lax.all_to_all(
        sent.reshape(senders, CHUNK, LANES), "subj", split_axis=0, concat_axis=0, tiled=True
    )
    everyone = senders * strips
    tested, mine = block_stats(codes.reshape(senders * CHUNK, LANES), rows, senders, everyone)

    odd = lax.axis_index("subj") % 2 == 1
    swapped = lax.ppermute(tested[1], "subj", [(i, i ^ 1) for i in range(senders)])
    t_map = jnp.stack([jnp.where(odd, swapped, tested[0]), jnp.where(odd, tested[0], swapped)])

    theirs = lax.all_to_all(mine, ("subj", "strip"), split_axis=0, concat_axis=0, tiled=True)
    root = theirs.astype(F32) * (REACH_T**0.25 / LEVELS)
    return t_map, jnp.max((root * root) * (root * root), axis=0).reshape(PERMS)


def solution(mesh):
    placed = (P("subj", None, None, None, "strip"), P(), P(), P())
    return jax.shard_map(
        on_device,
        mesh=mesh,
        in_specs=placed,
        out_specs=(P(None, "subj", "strip"), P()),
        check_vma=False,
    )
```

```python
import functools

import jax
import jax.numpy as jnp
from jax import lax
from jax.experimental import pallas as pl
from jax.experimental.pallas import tpu as pltpu
from jax.sharding import PartitionSpec as P

F32, BF16, I16 = jnp.float32, jnp.bfloat16, jnp.int16
LANES = 128
ROWS = 512
BLOCK = 16
MAIN, TAIL = 32, 8
CHUNK = MAIN + TAIL
PAIR = 2 * CHUNK
PER = 2
COMPS, PLANES = 3, 4
PERMS, GROUP = 256, 272
REACH = 0.6
REACH_T = 6800.0
LEVELS = 32767.0
CENTRE = 0.4 / 0.15
FLOOR = 1e-06 / (CENTRE + 4.0)


def encode(y):
    half = y * lax.rsqrt(jnp.maximum(jnp.abs(y), 1e-30))
    fourth = half * lax.rsqrt(jnp.maximum(jnp.abs(half), 1e-15))
    shift = 1.5 * 2.0**23
    return (fourth * (LEVELS / REACH**0.25) + shift) - shift


def decode(code):
    part = code * (REACH**0.25 / LEVELS)
    return (part * jnp.abs(part)) * (part * part)


def packed(code):
    return code.astype(jnp.int32).astype(I16)


def log_det(dz, dx, dy):
    j00, j01, j02 = 2.0 + dz[0], dx[0], dy[0]
    j10, j11, j12 = dz[1], 2.0 + dx[1], dy[1]
    j20, j21, j22 = dz[2], dx[2], 2.0 + dy[2]
    det = (
        j00 * (j11 * j22 - j12 * j21)
        - j01 * (j10 * j22 - j12 * j20)
        + j02 * (j10 * j21 - j11 * j20)
    )
    return jnp.log(det * 0.125)


def edges_kernel(parts, disp_ref, low_ref, high_ref, field_ref, sem):
    rows = ROWS // parts
    copies = [
        pltpu.make_async_copy(
            disp_ref.at[:, :, :, h * rows : (h + 1) * rows, :],
            field_ref.at[:, :, :, h * rows : (h + 1) * rows, :],
            sem.at[h],
        )
        for h in range(parts)
    ]
    for copy in copies:
        copy.start()
    row = lax.broadcasted_iota(jnp.int32, (32, 2 * LANES), 0)
    lane = lax.broadcasted_iota(jnp.int32, (32, 2 * LANES), 1)
    column = jnp.where(row < 16, row // 8, row // 8 - 2 + LANES - 2)
    picks = [
        ((row % 8 == 2 * q + lane // LANES) & (lane % LANES == column)).astype(F32).astype(BF16)
        for q in range(PLANES)
    ]
    for h in range(parts):
        copies[h].wait()
        at = slice(h * rows, (h + 1) * rows)
        for c in range(COMPS):
            acc = jnp.zeros((32, rows), F32)
            for q in range(PLANES):
                both = jnp.concatenate([field_ref[0, c, q, at, :], field_ref[1, c, q, at, :]], axis=1)
                acc = acc + lax.dot_general(
                    picks[q], both, (((1,), (1,)), ((), ())), preferred_element_type=F32
                )
            low_ref[c * 16 : c * 16 + 16, at] = acc[0:16].astype(BF16)
            high_ref[c * 16 : c * 16 + 16, at] = acc[16:32].astype(BF16)


def strip_edges(disp):
    parts = 4
    out = pltpu.VMEM((COMPS * 16, ROWS), BF16)
    return pl.pallas_call(
        functools.partial(edges_kernel, parts),
        in_specs=[pl.BlockSpec(memory_space=pltpu.HBM)],
        out_specs=[pl.BlockSpec(memory_space=pltpu.VMEM)] * 3,
        out_shape=(out, out, pltpu.VMEM(disp.shape, BF16)),
        scratch_shapes=[pltpu.SemaphoreType.DMA((parts,))],
        compiler_params=pltpu.CompilerParams(vmem_limit_bytes=8 * 2**20),
        cost_estimate=pl.CostEstimate(flops=10**8, bytes_accessed=3_200_000, transcendentals=0),
        name="strip_edges",
    )(pltpu.with_memory_space_constraint(disp, pltpu.HBM))


def inner_kernel(disp_ref, out_ref, beside_ref, pad_ref, code_ref):
    pad, step = 8, 16
    blocks = ROWS // BLOCK
    zeros = jnp.zeros((pad, LANES), F32)
    for k in range(2):
        code_ref[k, 0:pad, :] = zeros
        code_ref[k, pad + ROWS : 2 * pad + ROWS, :] = zeros
        for c in range(COMPS):
            pad_ref[k, c, 0:pad, :] = zeros
            pad_ref[k, c, pad + ROWS : 2 * pad + ROWS, :] = zeros
    for s in range(PER):
        for p in range(2):
            for c in range(COMPS):
                pad_ref[p, c, pad : pad + ROWS, :] = disp_ref[s, c, 1 + p].astype(F32)

            def body(i, carry):
                base = pl.multiple_of(i * step, step)
                dz, dx, dy = [], [], []
                for c in range(COMPS):
                    up = disp_ref[s, c, p + 2, pl.ds(base, step), :].astype(F32)
                    down = disp_ref[s, c, p, pl.ds(base, step), :].astype(F32)
                    dz.append(up - down)
                    center = pad_ref[p, c, pl.ds(base + pad, step), :]
                    dx.append(
                        pad_ref[p, c, pl.ds(base + pad + 1, step), :]
                        - pad_ref[p, c, pl.ds(base + pad - 1, step), :]
                    )
                    dy.append(pltpu.roll(center, LANES - 1, 1) - pltpu.roll(center, 1, 1))
                code = encode(log_det(dz, dx, dy))
                code_ref[p, pl.ds(base + pad, step), :] = code
                out_ref[s, p, i] = packed(code)
                return carry

            lax.fori_loop(0, ROWS // step, body, 0, unroll=16)
            beside_ref[2 * p + s, 0] = code_ref[p, pl.ds(pad - 1, blocks, stride=BLOCK), :]
            beside_ref[2 * p + s, 1] = code_ref[p, pl.ds(pad + BLOCK, blocks, stride=BLOCK), :]


def inner_codes(disp):
    blocks = ROWS // BLOCK
    return pl.pallas_call(
        inner_kernel,
        in_specs=[pl.BlockSpec(memory_space=pltpu.VMEM)],
        out_specs=[pl.BlockSpec(memory_space=pltpu.VMEM)] * 2,
        out_shape=(
            pltpu.VMEM((PER, 2, blocks, BLOCK, LANES), I16),
            pltpu.VMEM((2 * PER, 2, blocks, LANES), F32),
        ),
        scratch_shapes=[
            pltpu.VMEM((2, COMPS, ROWS + 16, LANES), F32),
            pltpu.VMEM((2, ROWS + 32, LANES), F32),
        ],
        compiler_params=pltpu.CompilerParams(vmem_limit_bytes=16 * 2**20),
        cost_estimate=pl.CostEstimate(flops=2 * 10**7, bytes_accessed=4_200_000, transcendentals=262144),
        name="inner_codes",
    )(pltpu.with_memory_space_constraint(disp, pltpu.VMEM))


def tail_kernel(low_ref, high_ref, left_ref, right_ref, beside_ref, main_ref, out_ref, pad_ref, side_ref, tail_ref, send_ref, sem):
    copies = [
        pltpu.make_async_copy(
            main_ref.at[s, p],
            out_ref.at[:, 48 * p + BLOCK * s : 48 * p + BLOCK * s + BLOCK, :],
            sem.at[2 * s + p],
        )
        for s in range(PER)
        for p in range(2)
    ]
    for copy in copies:
        copy.start()
    strips = lax.axis_size("strip")
    me = lax.axis_index("strip")
    keep_left = (me > 0).astype(F32)
    keep_right = (me < strips - 1).astype(F32)
    lane = lax.broadcasted_iota(jnp.int32, (8, ROWS), 1)

    def columns(ref):
        return [[ref[16 * c + 8 * e : 16 * c + 8 * e + 8, :] for e in range(2)] for c in range(COMPS)]

    def codes(around):
        dz, dx, dy = [], [], []
        for before, center, after in around:
            dz.append(pltpu.roll(center, 6, 0) - pltpu.roll(center, 2, 0))
            dx.append(
                jnp.where(lane == ROWS - 1, 0.0, pltpu.roll(center, ROWS - 1, 1))
                - jnp.where(lane == 0, 0.0, pltpu.roll(center, 1, 1))
            )
            dy.append(after - before)
        return encode(log_det(dz, dx, dy))

    low, high, left, right = (
        columns(ref[...].astype(F32)) for ref in (low_ref, high_ref, left_ref, right_ref)
    )
    wide_left = [left[c] + low[c] for c in range(COMPS)]
    wide_right = [high[c] + right[c] for c in range(COMPS)]
    four = [
        codes([w[0:3] for w in wide_left]) * keep_left,
        codes([w[1:4] for w in wide_left]),
        codes([w[0:3] for w in wide_right]),
        codes([w[1:4] for w in wide_right]) * keep_right,
    ]
    zeros = jnp.zeros((8, LANES), F32)
    for k in range(4):
        pad_ref[k, :, 0:LANES] = zeros
        pad_ref[k, :, LANES : LANES + ROWS] = four[k]
        pad_ref[k, :, LANES + ROWS : 2 * LANES + ROWS] = zeros
    here = lax.broadcasted_iota(jnp.int32, (8, LANES), 1)
    blocks = ROWS // BLOCK
    for j in range(blocks):
        start = LANES + j * BLOCK - 1
        line = zeros
        for k in range(4):
            window, offset = start // LANES, start % LANES
            first = pltpu.roll(
                pad_ref[k, :, window * LANES : (window + 1) * LANES], (32 * k - offset) % LANES, 1
            )
            if offset + 18 > LANES:
                second = pltpu.roll(
                    pad_ref[k, :, (window + 1) * LANES : (window + 2) * LANES], (32 * k - offset) % LANES, 1
                )
                first = jnp.where(here - 32 * k < LANES - offset, first, second)
            line = first if k == 0 else jnp.where(here < 32 * k, line, first)
        side_ref[j * 8 : j * 8 + 8, :] = line
    for p in range(2):
        for s in range(PER):
            row = TAIL * p + 4 * s
            for h in range(2):
                tail_ref[pl.ds(row + h, blocks, stride=2 * TAIL), :] = beside_ref[2 * p + s, h]
            tail_ref[pl.ds(row + 2, blocks, stride=2 * TAIL), :] = side_ref[
                pl.ds(2 + 2 * p + s, blocks, stride=8), :
            ]
            tail_ref[pl.ds(row + 3, blocks, stride=2 * TAIL), :] = jnp.zeros((blocks, LANES), F32)
    send_ref[...] = packed(tail_ref[0 : blocks * 2 * TAIL, :]).reshape(blocks, 2 * TAIL, LANES)
    copies.append(
        pltpu.make_async_copy(send_ref, out_ref.at[:, MAIN : MAIN + 2 * TAIL, :], sem.at[2 * PER])
    )
    copies[-1].start()
    for copy in copies:
        copy.wait()


def with_tails(low, high, left, right, beside, main):
    blocks = ROWS // BLOCK
    vmem = pl.BlockSpec(memory_space=pltpu.VMEM)
    return pl.pallas_call(
        tail_kernel,
        in_specs=[vmem] * 6,
        out_specs=pl.BlockSpec(memory_space=pltpu.HBM),
        out_shape=pltpu.HBM((blocks, PAIR, LANES), I16),
        scratch_shapes=[
            pltpu.VMEM((4, 8, ROWS + 2 * LANES), F32),
            pltpu.VMEM((blocks * 8 + 8, LANES), F32),
            pltpu.VMEM((blocks * 2 * TAIL + 16, LANES), F32),
            pltpu.VMEM((blocks, 2 * TAIL, LANES), I16),
            pltpu.SemaphoreType.DMA((2 * PER + 1,)),
        ],
        compiler_params=pltpu.CompilerParams(vmem_limit_bytes=8 * 2**20),
        cost_estimate=pl.CostEstimate(flops=10**6, bytes_accessed=5 * 10**5, transcendentals=5 * 10**4),
        name="with_tails",
    )(*(pltpu.with_memory_space_constraint(x, pltpu.VMEM) for x in (low, high, left, right, beside, main)))


def designs_kernel(age_ref, code_ref, perms_ref, out_ref):
    subjects = age_ref.shape[1]
    half = subjects // PER

    def total(v):
        return jnp.sum(v, axis=1, keepdims=True)

    def centred(v):
        return v - total(v) * (1.0 / subjects)

    basis = []
    for raw in (
        (code_ref[...] == 1).astype(F32),
        age_ref[...],
        (code_ref[...] == 2).astype(F32),
    ):
        v = centred(raw)
        for _ in range(2):
            for q in basis:
                v = v - q * total(q * v)
            v = centred(v)
        basis.append(v / jnp.sqrt(total(v * v)))
    scale = (0.15 / (subjects - 4)) ** 0.5
    lane = lax.broadcasted_iota(jnp.int32, (8, subjects), 1)
    order = PER * (lane % half) + lane // half
    for k, q in enumerate(basis):
        table = jnp.broadcast_to(q * scale, (8, subjects))

        def put(row, values):
            high = values.astype(BF16)
            rest = (values - high.astype(F32)).astype(BF16)
            at = pl.ds(k * GROUP + row, 16)
            out_ref[at, 0:subjects] = high
            out_ref[at, subjects : 2 * subjects] = high
            out_ref[at, 2 * subjects : 3 * subjects] = rest

        for g in range(PERMS // 16):
            two = []
            for h in range(2):
                who = jnp.take_along_axis(perms_ref[g * 16 + h * 8 : g * 16 + h * 8 + 8, :], order, axis=1)
                two.append(jnp.take_along_axis(table, who, axis=1))
            put(g * 16, jnp.concatenate(two, axis=0))
        plain = jnp.take_along_axis(table, order, axis=1)
        put(PERMS, jnp.concatenate([plain, plain], axis=0))


def design_rows(age, codes, perms):
    subjects = age.shape[0]
    return pl.pallas_call(
        designs_kernel,
        out_shape=jax.ShapeDtypeStruct((3 * GROUP, 3 * subjects), BF16),
        compiler_params=pltpu.CompilerParams(vmem_limit_bytes=8 * 2**20),
        cost_estimate=pl.CostEstimate(flops=4 * 10**6, bytes_accessed=800_000, transcendentals=0),
        name="design_rows",
    )(age.reshape(1, subjects), codes.reshape(1, subjects), perms)


def stats_kernel(senders, code_ref, rows_ref, tmap_ref, peaks_ref, value_ref, y_ref, sum_ref, rss_ref, top_ref, best_ref):
    subjects = PER * senders
    lane = lax.broadcasted_iota(jnp.int32, (subjects, LANES), 1)
    odd = lax.axis_index("subj") % 2
    main = odd * TAIL
    tail = (1 - odd) * MAIN
    per = 4 * CHUNK

    def unpack(i, carry):
        at = pl.ds(pl.multiple_of(i * per, 32), per)
        value_ref[at, :] = decode(code_ref[at, :].astype(F32))
        return carry

    lax.fori_loop(0, senders * CHUNK // per, unpack, 0, unroll=4)

    def gathered(offsets):
        return jnp.concatenate(
            [value_ref[pl.ds(offset, senders, stride=CHUNK), :] for offset in offsets], axis=0
        )

    def place(block, y):
        y = y - jnp.sum(y, axis=0, keepdims=True) * (1.0 / subjects)
        at = pl.ds(pl.multiple_of(block * LANES, LANES), LANES)
        sum_ref[0:1, at] = jnp.sum(y * y, axis=0, keepdims=True) * (0.15 / (subjects - 4)) + FLOOR
        high = y.astype(BF16)
        y_ref[0:subjects, at] = high
        y_ref[subjects : 2 * subjects, at] = (y - high.astype(F32)).astype(BF16)
        y_ref[2 * subjects : 3 * subjects, at] = high

    far = lane // 2 + jnp.where(lane % 2 == 0, 97, 1)
    near = (lane - 36) // 2 + jnp.where(lane % 2 == 0, 64, 32)
    sides = jnp.take_along_axis(
        gathered([tail + 2, tail + 6]),
        jnp.where(lane < 32, far, jnp.where((lane >= 36) & (lane < 72), near, 0)),
        axis=1,
    )

    def mended(y, r):
        ends = pltpu.roll(sides, LANES - 39 - 2 * r, 1)
        return jnp.where((lane == 0) | (lane == LANES - 1), ends, y)

    for r in range(BLOCK):
        place(r, mended(gathered([main + r, main + BLOCK + r]), r))
    place(BLOCK, mended(gathered([tail, tail + 4]), -1))
    place(BLOCK + 1, mended(gathered([tail + 1, tail + 5]), BLOCK))
    place(BLOCK + 2, sides)

    blocks = BLOCK + 3
    for start in range(0, blocks, 2):
        at = slice(start * LANES, min(start + 2, blocks) * LANES)
        proj = jnp.dot(rows_ref[...], y_ref[:, at], preferred_element_type=F32)
        q1, q2, q3 = (proj[k * GROUP : (k + 1) * GROUP] for k in range(3))
        rss_ref[:, at] = sum_ref[0:1, at] - q1 * q1 - q2 * q2 - q3 * q3
        top_ref[:, at] = q3

    here = lax.broadcasted_iota(jnp.int32, (8, LANES), 1)
    unscale = ((subjects - 4) / 0.15) ** 0.5

    def pseudo_t(g, r):
        at = pl.ds(pl.multiple_of(g * 8, 8), 8)

        def block(b):
            return rss_ref[at, b * LANES : (b + 1) * LANES]

        mine = block(r)
        above = block(r - 1 if r > 0 else BLOCK)
        below = block(r + 1 if r < BLOCK - 1 else BLOCK + 1)
        ends = pltpu.roll(block(BLOCK + 2), LANES - 1 - 2 * r, 1)
        before = jnp.where(here == 0, ends, pltpu.roll(mine, 1, 1))
        after = jnp.where(here == LANES - 1, ends, pltpu.roll(mine, LANES - 1, 1))
        beside = (above + below) + (before + after)
        variance = CENTRE * mine + beside
        return top_ref[at, r * LANES : (r + 1) * LANES] * lax.rsqrt(variance)

    def body(g, carry):
        best = jnp.zeros((8, LANES), F32)
        for r in range(BLOCK):
            best = jnp.maximum(best, jnp.abs(pseudo_t(g, r)))
        best_ref[pl.ds(pl.multiple_of(g * 8, 8), 8), :] = best
        return carry

    lax.fori_loop(0, PERMS // 8, body, 0, unroll=32)
    half = BLOCK // 2
    for r in range(BLOCK):
        tmap_ref[(r // half + odd) % 2, r % half : r % half + 1, :] = (
            pseudo_t(PERMS // 8, r)[0:1, :] * unscale
        )
    code = jnp.max(best_ref[...].T, axis=0, keepdims=True) * (unscale / REACH_T)
    code = jnp.minimum(jnp.sqrt(jnp.sqrt(code)), 1.0) * LEVELS + 0.5
    lines = jnp.concatenate([code[:, k * LANES : (k + 1) * LANES] for k in range(PERMS // LANES)] * 4, axis=0)
    everyone = peaks_ref.shape[0]
    peaks_ref[...] = jnp.broadcast_to(packed(lines)[None], (everyone // 4, 8, LANES)).reshape(everyone, 2, LANES)


def block_stats(codes, rows, senders, everyone):
    subjects = PER * senders
    columns = (BLOCK + 3) * LANES
    return pl.pallas_call(
        functools.partial(stats_kernel, senders),
        out_shape=(
            jax.ShapeDtypeStruct((2, BLOCK // 2, LANES), F32),
            jax.ShapeDtypeStruct((everyone, PERMS // LANES, LANES), I16),
        ),
        scratch_shapes=[
            pltpu.VMEM((senders * CHUNK + CHUNK, LANES), F32),
            pltpu.VMEM((3 * subjects, columns), BF16),
            pltpu.VMEM((8, columns), F32),
            pltpu.VMEM((GROUP, columns), F32),
            pltpu.VMEM((GROUP, columns), F32),
            pltpu.VMEM((PERMS, LANES), F32),
        ],
        compiler_params=pltpu.CompilerParams(vmem_limit_bytes=24 * 2**20),
        cost_estimate=pl.CostEstimate(flops=2 * 10**9, bytes_accessed=10**6, transcendentals=10**6),
        name="block_stats",
    )(codes, rows)


def on_device(displacement, age, group_codes, perms):
    senders = lax.axis_size("subj")
    strips = lax.axis_size("strip")
    low, high, field = strip_edges(displacement)
    left = lax.ppermute(high, "strip", [(i, i + 1) for i in range(strips - 1)])
    right = lax.ppermute(low, "strip", [(i + 1, i) for i in range(strips - 1)])
    main, beside = inner_codes(field)
    rows = design_rows(age, group_codes, perms)
    sent = with_tails(low, high, left, right, beside, main)
    codes = lax.all_to_all(
        sent.reshape(senders, CHUNK, LANES), "subj", split_axis=0, concat_axis=0, tiled=True
    )
    everyone = senders * strips
    tested, mine = block_stats(codes.reshape(senders * CHUNK, LANES), rows, senders, everyone)

    odd = lax.axis_index("subj") % 2 == 1
    swapped = lax.ppermute(tested[1], "subj", [(i, i ^ 1) for i in range(senders)])
    t_map = jnp.stack([jnp.where(odd, swapped, tested[0]), jnp.where(odd, tested[0], swapped)])

    theirs = lax.all_to_all(mine, ("subj", "strip"), split_axis=0, concat_axis=0, tiled=True)
    root = theirs.astype(F32) * (REACH_T**0.25 / LEVELS)
    return t_map, jnp.max((root * root) * (root * root), axis=0).reshape(PERMS)


def solution(mesh):
    placed = (P("subj", None, None, None, "strip"), P(), P(), P())
    return jax.shard_map(
        on_device,
        mesh=mesh,
        in_specs=placed,
        out_specs=(P(None, "subj", "strip"), P()),
        check_vma=False,
    )
```

```python
import functools

import jax
import jax.numpy as jnp
from jax import lax
from jax.experimental import pallas as pl
from jax.experimental.pallas import tpu as pltpu
from jax.sharding import PartitionSpec as P

F32, BF16, I16 = jnp.float32, jnp.bfloat16, jnp.int16
LANES = 128
ROWS = 512
BLOCK = 16
MAIN, TAIL = 32, 8
CHUNK = MAIN + TAIL
PAIR = 2 * CHUNK
PER = 2
COMPS, PLANES = 3, 4
PERMS, GROUP = 256, 272
REACH = 0.6
REACH_T = 6800.0
LEVELS = 32767.0
CENTRE = 0.4 / 0.15
FLOOR = 1e-06 / (CENTRE + 4.0)


def encode(y):
    half = y * lax.rsqrt(jnp.maximum(jnp.abs(y), 1e-30))
    fourth = half * lax.rsqrt(jnp.maximum(jnp.abs(half), 1e-15))
    shift = 1.5 * 2.0**23
    return (fourth * (LEVELS / REACH**0.25) + shift) - shift


def decode(code):
    part = code * (REACH**0.25 / LEVELS)
    return (part * jnp.abs(part)) * (part * part)


def packed(code):
    return code.astype(jnp.int32).astype(I16)


def log_det(dz, dx, dy):
    j00, j01, j02 = 2.0 + dz[0], dx[0], dy[0]
    j10, j11, j12 = dz[1], 2.0 + dx[1], dy[1]
    j20, j21, j22 = dz[2], dx[2], 2.0 + dy[2]
    det = (
        j00 * (j11 * j22 - j12 * j21)
        - j01 * (j10 * j22 - j12 * j20)
        + j02 * (j10 * j21 - j11 * j20)
    )
    return jnp.log(det * 0.125)


def edges_kernel(parts, disp_ref, low_ref, high_ref, field_ref, sem):
    rows = ROWS // parts
    copies = [
        pltpu.make_async_copy(
            disp_ref.at[:, :, :, h * rows : (h + 1) * rows, :],
            field_ref.at[:, :, :, h * rows : (h + 1) * rows, :],
            sem.at[h],
        )
        for h in range(parts)
    ]
    for copy in copies:
        copy.start()
    row = lax.broadcasted_iota(jnp.int32, (48, 2 * LANES), 0)
    lane = lax.broadcasted_iota(jnp.int32, (48, 2 * LANES), 1)
    column = jnp.where(row < 16, row // 8, row // 8 - 2 + LANES - 4)
    picks = [
        ((row % 8 == 2 * q + lane // LANES) & (lane % LANES == column)).astype(F32).astype(BF16)
        for q in range(PLANES)
    ]
    for h in range(parts):
        copies[h].wait()
        at = slice(h * rows, (h + 1) * rows)
        for c in range(COMPS):
            acc = jnp.zeros((48, rows), F32)
            for q in range(PLANES):
                both = jnp.concatenate([field_ref[0, c, q, at, :], field_ref[1, c, q, at, :]], axis=1)
                acc = acc + lax.dot_general(
                    picks[q], both, (((1,), (1,)), ((), ())), preferred_element_type=F32
                )
            low_ref[c * 16 : c * 16 + 16, at] = acc[0:16].astype(BF16)
            high_ref[c * 32 : c * 32 + 32, at] = acc[16:48].astype(BF16)


def strip_edges(disp):
    parts = 4
    out = [pltpu.VMEM((COMPS * rows, ROWS), BF16) for rows in (16, 32)]
    return pl.pallas_call(
        functools.partial(edges_kernel, parts),
        in_specs=[pl.BlockSpec(memory_space=pltpu.HBM)],
        out_specs=[pl.BlockSpec(memory_space=pltpu.VMEM)] * 3,
        out_shape=(*out, pltpu.VMEM(disp.shape, BF16)),
        scratch_shapes=[pltpu.SemaphoreType.DMA((parts,))],
        compiler_params=pltpu.CompilerParams(vmem_limit_bytes=8 * 2**20),
        cost_estimate=pl.CostEstimate(flops=10**8, bytes_accessed=3_200_000, transcendentals=0),
        name="strip_edges",
    )(pltpu.with_memory_space_constraint(disp, pltpu.HBM))


def inner_kernel(disp_ref, out_ref, beside_ref, pad_ref, code_ref):
    pad, step = 8, 16
    blocks = ROWS // BLOCK
    zeros = jnp.zeros((pad, LANES), F32)
    for k in range(2):
        code_ref[k, 0:pad, :] = zeros
        code_ref[k, pad + ROWS : 2 * pad + ROWS, :] = zeros
        for c in range(COMPS):
            pad_ref[k, c, 0:pad, :] = zeros
            pad_ref[k, c, pad + ROWS : 2 * pad + ROWS, :] = zeros
    for s in range(PER):
        for p in range(2):
            for c in range(COMPS):
                pad_ref[p, c, pad : pad + ROWS, :] = disp_ref[s, c, 1 + p].astype(F32)

            def body(i, carry):
                base = pl.multiple_of(i * step, step)
                dz, dx, dy = [], [], []
                for c in range(COMPS):
                    up = disp_ref[s, c, p + 2, pl.ds(base, step), :].astype(F32)
                    down = disp_ref[s, c, p, pl.ds(base, step), :].astype(F32)
                    dz.append(up - down)
                    center = pad_ref[p, c, pl.ds(base + pad, step), :]
                    dx.append(
                        pad_ref[p, c, pl.ds(base + pad + 1, step), :]
                        - pad_ref[p, c, pl.ds(base + pad - 1, step), :]
                    )
                    dy.append(pltpu.roll(center, LANES - 1, 1) - pltpu.roll(center, 1, 1))
                code = encode(log_det(dz, dx, dy))
                code_ref[p, pl.ds(base + pad, step), :] = code
                out_ref[s, p, i] = packed(code)
                return carry

            lax.fori_loop(0, ROWS // step, body, 0, unroll=16)
            beside_ref[2 * p + s, 0] = code_ref[p, pl.ds(pad - 1, blocks, stride=BLOCK), :]
            beside_ref[2 * p + s, 1] = code_ref[p, pl.ds(pad + BLOCK, blocks, stride=BLOCK), :]


def inner_codes(disp):
    blocks = ROWS // BLOCK
    return pl.pallas_call(
        inner_kernel,
        in_specs=[pl.BlockSpec(memory_space=pltpu.VMEM)],
        out_specs=[pl.BlockSpec(memory_space=pltpu.VMEM)] * 2,
        out_shape=(
            pltpu.VMEM((PER, 2, blocks, BLOCK, LANES), I16),
            pltpu.VMEM((2 * PER, 2, blocks, LANES), F32),
        ),
        scratch_shapes=[
            pltpu.VMEM((2, COMPS, ROWS + 16, LANES), F32),
            pltpu.VMEM((2, ROWS + 32, LANES), F32),
        ],
        compiler_params=pltpu.CompilerParams(vmem_limit_bytes=16 * 2**20),
        cost_estimate=pl.CostEstimate(flops=2 * 10**7, bytes_accessed=4_200_000, transcendentals=262144),
        name="inner_codes",
    )(pltpu.with_memory_space_constraint(disp, pltpu.VMEM))


def tail_kernel(low_ref, high_ref, left_ref, beside_ref, main_ref, out_ref, pad_ref, side_ref, tail_ref, send_ref, sem):
    copies = [
        pltpu.make_async_copy(
            main_ref.at[s, p],
            out_ref.at[:, 48 * p + BLOCK * s : 48 * p + BLOCK * s + BLOCK, :],
            sem.at[2 * s + p],
        )
        for s in range(PER)
        for p in range(2)
    ]
    for copy in copies:
        copy.start()
    inside = (lax.axis_index("strip") > 0).astype(F32)
    lane = lax.broadcasted_iota(jnp.int32, (8, ROWS), 1)

    def columns(ref):
        many = ref.shape[0] // (8 * COMPS)
        return [
            [ref[8 * (many * c + e) : 8 * (many * c + e) + 8, :] for e in range(many)] for c in range(COMPS)
        ]

    def codes(around):
        dz, dx, dy = [], [], []
        for before, center, after in around:
            dz.append(pltpu.roll(center, 6, 0) - pltpu.roll(center, 2, 0))
            dx.append(
                jnp.where(lane == ROWS - 1, 0.0, pltpu.roll(center, ROWS - 1, 1))
                - jnp.where(lane == 0, 0.0, pltpu.roll(center, 1, 1))
            )
            dy.append(after - before)
        return encode(log_det(dz, dx, dy))

    low, high, left = (columns(ref[...].astype(F32)) for ref in (low_ref, high_ref, left_ref))
    five = [
        codes([w[0:3] for w in left]),
        codes([w[1:4] for w in left]),
        codes([(w[2], w[3], v[0] * inside) for w, v in zip(left, low)]),
        codes([(w[3] * inside, v[0], v[1]) for w, v in zip(left, low)]),
        codes([w[1:4] for w in high]),
    ]
    zeros = jnp.zeros((8, LANES), F32)
    for k in range(5):
        pad_ref[k, :, 0:LANES] = zeros
        pad_ref[k, :, LANES : LANES + ROWS] = five[k]
        pad_ref[k, :, LANES + ROWS : 2 * LANES + ROWS] = zeros
    here = lax.broadcasted_iota(jnp.int32, (8, LANES), 1)
    blocks = ROWS // BLOCK
    for j in range(blocks):
        start = LANES + j * BLOCK - 1
        line = zeros
        for k in range(5):
            window, offset = start // LANES, start % LANES
            first = pltpu.roll(
                pad_ref[k, :, window * LANES : (window + 1) * LANES], (24 * k - offset) % LANES, 1
            )
            if offset + 18 > LANES:
                second = pltpu.roll(
                    pad_ref[k, :, (window + 1) * LANES : (window + 2) * LANES], (24 * k - offset) % LANES, 1
                )
                first = jnp.where(here - 24 * k < LANES - offset, first, second)
            line = first if k == 0 else jnp.where(here < 24 * k, line, first)
        side_ref[j * 8 : j * 8 + 8, :] = line
    for p in range(2):
        for s in range(PER):
            row = TAIL * p + 4 * s
            for h in range(2):
                tail_ref[pl.ds(row + h, blocks, stride=2 * TAIL), :] = beside_ref[2 * p + s, h]
            tail_ref[pl.ds(row + 2, blocks, stride=2 * TAIL), :] = side_ref[
                pl.ds(2 + 2 * p + s, blocks, stride=8), :
            ]
            tail_ref[pl.ds(row + 3, blocks, stride=2 * TAIL), :] = jnp.zeros((blocks, LANES), F32)
    send_ref[...] = packed(tail_ref[0 : blocks * 2 * TAIL, :]).reshape(blocks, 2 * TAIL, LANES)
    copies.append(
        pltpu.make_async_copy(send_ref, out_ref.at[:, MAIN : MAIN + 2 * TAIL, :], sem.at[2 * PER])
    )
    copies[-1].start()
    for copy in copies:
        copy.wait()


def with_tails(low, high, left, beside, main):
    blocks = ROWS // BLOCK
    vmem = pl.BlockSpec(memory_space=pltpu.VMEM)
    return pl.pallas_call(
        tail_kernel,
        in_specs=[vmem] * 5,
        out_specs=pl.BlockSpec(memory_space=pltpu.HBM),
        out_shape=pltpu.HBM((blocks, PAIR, LANES), I16),
        scratch_shapes=[
            pltpu.VMEM((5, 8, ROWS + 2 * LANES), F32),
            pltpu.VMEM((blocks * 8 + 8, LANES), F32),
            pltpu.VMEM((blocks * 2 * TAIL + 16, LANES), F32),
            pltpu.VMEM((blocks, 2 * TAIL, LANES), I16),
            pltpu.SemaphoreType.DMA((2 * PER + 1,)),
        ],
        compiler_params=pltpu.CompilerParams(vmem_limit_bytes=8 * 2**20),
        cost_estimate=pl.CostEstimate(flops=10**6, bytes_accessed=5 * 10**5, transcendentals=5 * 10**4),
        name="with_tails",
    )(*(pltpu.with_memory_space_constraint(x, pltpu.VMEM) for x in (low, high, left, beside, main)))


def designs_kernel(age_ref, code_ref, perms_ref, out_ref):
    subjects = age_ref.shape[1]
    half = subjects // PER

    def total(v):
        return jnp.sum(v, axis=1, keepdims=True)

    def centred(v):
        return v - total(v) * (1.0 / subjects)

    basis = []
    for raw in (
        (code_ref[...] == 1).astype(F32),
        age_ref[...],
        (code_ref[...] == 2).astype(F32),
    ):
        v = centred(raw)
        for _ in range(2):
            for q in basis:
                v = v - q * total(q * v)
            v = centred(v)
        basis.append(v / jnp.sqrt(total(v * v)))
    scale = (0.15 / (subjects - 4)) ** 0.5
    lane = lax.broadcasted_iota(jnp.int32, (8, subjects), 1)
    order = PER * (lane % half) + lane // half
    for k, q in enumerate(basis):
        table = jnp.broadcast_to(q * scale, (8, subjects))

        def put(row, values):
            high = values.astype(BF16)
            rest = (values - high.astype(F32)).astype(BF16)
            at = pl.ds(k * GROUP + row, 16)
            out_ref[at, 0:subjects] = high
            out_ref[at, subjects : 2 * subjects] = high
            out_ref[at, 2 * subjects : 3 * subjects] = rest

        for g in range(PERMS // 16):
            two = []
            for h in range(2):
                who = jnp.take_along_axis(perms_ref[g * 16 + h * 8 : g * 16 + h * 8 + 8, :], order, axis=1)
                two.append(jnp.take_along_axis(table, who, axis=1))
            put(g * 16, jnp.concatenate(two, axis=0))
        plain = jnp.take_along_axis(table, order, axis=1)
        put(PERMS, jnp.concatenate([plain, plain], axis=0))


def design_rows(age, codes, perms):
    subjects = age.shape[0]
    return pl.pallas_call(
        designs_kernel,
        out_shape=jax.ShapeDtypeStruct((3 * GROUP, 3 * subjects), BF16),
        compiler_params=pltpu.CompilerParams(vmem_limit_bytes=8 * 2**20),
        cost_estimate=pl.CostEstimate(flops=4 * 10**6, bytes_accessed=800_000, transcendentals=0),
        name="design_rows",
    )(age.reshape(1, subjects), codes.reshape(1, subjects), perms)


def stats_kernel(senders, code_ref, rows_ref, tmap_ref, peaks_ref, value_ref, y_ref, sum_ref, rss_ref, top_ref, best_ref):
    subjects = PER * senders
    lane = lax.broadcasted_iota(jnp.int32, (subjects, LANES), 1)
    odd = lax.axis_index("subj") % 2
    main = odd * TAIL
    tail = (1 - odd) * MAIN
    per = 4 * CHUNK

    def unpack(i, carry):
        at = pl.ds(pl.multiple_of(i * per, 32), per)
        value_ref[at, :] = decode(code_ref[at, :].astype(F32))
        return carry

    lax.fori_loop(0, senders * CHUNK // per, unpack, 0, unroll=4)

    def gathered(offsets):
        return jnp.concatenate(
            [value_ref[pl.ds(offset, senders, stride=CHUNK), :] for offset in offsets], axis=0
        )

    def place(block, y):
        y = y - jnp.sum(y, axis=0, keepdims=True) * (1.0 / subjects)
        at = pl.ds(pl.multiple_of(block * LANES, LANES), LANES)
        sum_ref[0:1, at] = jnp.sum(y * y, axis=0, keepdims=True) * (0.15 / (subjects - 4)) + FLOOR
        high = y.astype(BF16)
        y_ref[0:subjects, at] = high
        y_ref[subjects : 2 * subjects, at] = (y - high.astype(F32)).astype(BF16)
        y_ref[2 * subjects : 3 * subjects, at] = high

    far = lane // 2 + jnp.where(lane % 2 == 0, 97, 1)
    near = (lane - 36) // 3 + 24 * ((lane - 36) % 3 + 1)
    sides = jnp.take_along_axis(
        gathered([tail + 2, tail + 6]),
        jnp.where(lane < 32, far, jnp.where((lane >= 36) & (lane < 90), near, 0)),
        axis=1,
    )

    def mended(y, r):
        ends = pltpu.roll(sides, LANES - 41 - 3 * r, 1)
        return jnp.where((lane == 0) | (lane >= LANES - 2), ends, y)

    for r in range(BLOCK):
        place(r, mended(gathered([main + r, main + BLOCK + r]), r))
    place(BLOCK, mended(gathered([tail, tail + 4]), -1))
    place(BLOCK + 1, mended(gathered([tail + 1, tail + 5]), BLOCK))
    place(BLOCK + 2, sides)

    blocks = BLOCK + 3
    for start in range(0, blocks, 2):
        at = slice(start * LANES, min(start + 2, blocks) * LANES)
        proj = jnp.dot(rows_ref[...], y_ref[:, at], preferred_element_type=F32)
        q1, q2, q3 = (proj[k * GROUP : (k + 1) * GROUP] for k in range(3))
        rss_ref[:, at] = sum_ref[0:1, at] - q1 * q1 - q2 * q2 - q3 * q3
        top_ref[:, at] = q3

    here = lax.broadcasted_iota(jnp.int32, (8, LANES), 1)
    first = lax.axis_index("strip") == 0
    seam = (here == LANES - 3) | (here == LANES - 2)
    from_before = (here == LANES - 2) | ((here == 0) & first)
    from_after = (here == LANES - 3) | ((here == LANES - 1) & first)
    unscale = ((subjects - 4) / 0.15) ** 0.5

    def pseudo_t(g, r):
        at = pl.ds(pl.multiple_of(g * 8, 8), 8)

        def block(b):
            return rss_ref[at, b * LANES : (b + 1) * LANES]

        mine = block(r)
        above = block(r - 1 if r > 0 else BLOCK)
        below = block(r + 1 if r < BLOCK - 1 else BLOCK + 1)
        ends = jnp.where(seam, pltpu.roll(block(BLOCK + 2), LANES - 3 - 2 * r, 1), FLOOR)
        before = jnp.where(from_before, ends, pltpu.roll(mine, 1, 1))
        after = jnp.where(from_after, ends, pltpu.roll(mine, LANES - 1, 1))
        beside = (above + below) + (before + after)
        variance = CENTRE * mine + beside
        return top_ref[at, r * LANES : (r + 1) * LANES] * lax.rsqrt(variance)

    def body(g, carry):
        best = jnp.zeros((8, LANES), F32)
        for r in range(BLOCK):
            best = jnp.maximum(best, jnp.abs(pseudo_t(g, r)))
        best_ref[pl.ds(pl.multiple_of(g * 8, 8), 8), :] = best
        return carry

    lax.fori_loop(0, PERMS // 8, body, 0, unroll=32)
    half = BLOCK // 2
    for r in range(BLOCK):
        tmap_ref[(r // half + odd) % 2, r % half : r % half + 1, :] = (
            pseudo_t(PERMS // 8, r)[0:1, :] * unscale
        )
    code = jnp.max(best_ref[...].T, axis=0, keepdims=True) * (unscale / REACH_T)
    code = jnp.minimum(jnp.sqrt(jnp.sqrt(code)), 1.0) * LEVELS + 0.5
    lines = jnp.concatenate([code[:, k * LANES : (k + 1) * LANES] for k in range(PERMS // LANES)] * 4, axis=0)
    everyone = peaks_ref.shape[0]
    peaks_ref[...] = jnp.broadcast_to(packed(lines)[None], (everyone // 4, 8, LANES)).reshape(everyone, 2, LANES)


def block_stats(codes, rows, senders, everyone):
    subjects = PER * senders
    columns = (BLOCK + 3) * LANES
    return pl.pallas_call(
        functools.partial(stats_kernel, senders),
        out_shape=(
            jax.ShapeDtypeStruct((2, BLOCK // 2, LANES), F32),
            jax.ShapeDtypeStruct((everyone, PERMS // LANES, LANES), I16),
        ),
        scratch_shapes=[
            pltpu.VMEM((senders * CHUNK + CHUNK, LANES), F32),
            pltpu.VMEM((3 * subjects, columns), BF16),
            pltpu.VMEM((8, columns), F32),
            pltpu.VMEM((GROUP, columns), F32),
            pltpu.VMEM((GROUP, columns), F32),
            pltpu.VMEM((PERMS, LANES), F32),
        ],
        compiler_params=pltpu.CompilerParams(vmem_limit_bytes=24 * 2**20),
        cost_estimate=pl.CostEstimate(flops=2 * 10**9, bytes_accessed=10**6, transcendentals=10**6),
        name="block_stats",
    )(codes, rows)


def on_device(displacement, age, group_codes, perms):
    senders = lax.axis_size("subj")
    strips = lax.axis_size("strip")
    low, high, field = strip_edges(displacement)
    left = lax.ppermute(high, "strip", [(i, (i + 1) % strips) for i in range(strips)])
    main, beside = inner_codes(field)
    rows = design_rows(age, group_codes, perms)
    sent = with_tails(low, high, left, beside, main)
    codes = lax.all_to_all(
        sent.reshape(senders, CHUNK, LANES), "subj", split_axis=0, concat_axis=0, tiled=True
    )
    everyone = senders * strips
    tested, mine = block_stats(codes.reshape(senders * CHUNK, LANES), rows, senders, everyone)

    odd = lax.axis_index("subj") % 2 == 1
    swapped = lax.ppermute(tested[1], "subj", [(i, i ^ 1) for i in range(senders)])
    t_map = jnp.stack([jnp.where(odd, swapped, tested[0]), jnp.where(odd, tested[0], swapped)])
    beyond = lax.ppermute(t_map, "strip", [((i + 1) % strips, i) for i in range(strips)])
    t_map = jnp.where(lax.broadcasted_iota(jnp.int32, t_map.shape, 2) >= LANES - 2, beyond, t_map)

    theirs = lax.all_to_all(mine, ("subj", "strip"), split_axis=0, concat_axis=0, tiled=True)
    root = theirs.astype(F32) * (REACH_T**0.25 / LEVELS)
    return t_map, jnp.max((root * root) * (root * root), axis=0).reshape(PERMS)


def solution(mesh):
    placed = (P("subj", None, None, None, "strip"), P(), P(), P())
    return jax.shard_map(
        on_device,
        mesh=mesh,
        in_specs=placed,
        out_specs=(P(None, "subj", "strip"), P()),
        check_vma=False,
    )
```

```python
import functools

import jax
import jax.numpy as jnp
from jax import lax
from jax.experimental import pallas as pl
from jax.experimental.pallas import tpu as pltpu
from jax.sharding import PartitionSpec as P

F32, BF16, I16 = jnp.float32, jnp.bfloat16, jnp.int16
LANES = 128
ROWS = 512
BLOCK = 16
MAIN, TAIL = 32, 8
CHUNK = MAIN + TAIL
PAIR = 2 * CHUNK
PER = 2
COMPS, PLANES = 3, 4
PERMS, GROUP = 256, 272
REACH = 0.6
REACH_T = 6800.0
LEVELS = 32767.0
CENTRE = 0.4 / 0.15
FLOOR = 1e-06 / (CENTRE + 4.0)


def encode(y):
    half = y * lax.rsqrt(jnp.maximum(jnp.abs(y), 1e-30))
    fourth = half * lax.rsqrt(jnp.maximum(jnp.abs(half), 1e-15))
    shift = 1.5 * 2.0**23
    return (fourth * (LEVELS / REACH**0.25) + shift) - shift


def decode(code):
    part = code * (REACH**0.25 / LEVELS)
    return (part * jnp.abs(part)) * (part * part)


def packed(code):
    return code.astype(jnp.int32).astype(I16)


def log_det(dz, dx, dy):
    j00, j01, j02 = 2.0 + dz[0], dx[0], dy[0]
    j10, j11, j12 = dz[1], 2.0 + dx[1], dy[1]
    j20, j21, j22 = dz[2], dx[2], 2.0 + dy[2]
    det = (
        j00 * (j11 * j22 - j12 * j21)
        - j01 * (j10 * j22 - j12 * j20)
        + j02 * (j10 * j21 - j11 * j20)
    )
    return jnp.log(det * 0.125)


def edges_kernel(parts, disp_ref, low_ref, high_ref, field_ref, sem):
    rows = ROWS // parts
    copies = [
        pltpu.make_async_copy(
            disp_ref.at[:, :, :, h * rows : (h + 1) * rows, :],
            field_ref.at[:, :, :, h * rows : (h + 1) * rows, :],
            sem.at[h],
        )
        for h in range(parts)
    ]
    for copy in copies:
        copy.start()
    row = lax.broadcasted_iota(jnp.int32, (48, 2 * LANES), 0)
    lane = lax.broadcasted_iota(jnp.int32, (48, 2 * LANES), 1)
    column = jnp.where(row < 16, row // 8, row // 8 - 2 + LANES - 4)
    picks = [
        ((row % 8 == 2 * q + lane // LANES) & (lane % LANES == column)).astype(F32).astype(BF16)
        for q in range(PLANES)
    ]
    for h in range(parts):
        copies[h].wait()
        at = slice(h * rows, (h + 1) * rows)
        for c in range(COMPS):
            acc = jnp.zeros((48, rows), F32)
            for q in range(PLANES):
                both = jnp.concatenate([field_ref[0, c, q, at, :], field_ref[1, c, q, at, :]], axis=1)
                acc = acc + lax.dot_general(
                    picks[q], both, (((1,), (1,)), ((), ())), preferred_element_type=F32
                )
            low_ref[c * 16 : c * 16 + 16, at] = acc[0:16].astype(BF16)
            high_ref[c * 32 : c * 32 + 32, at] = acc[16:48].astype(BF16)


def strip_edges(disp):
    parts = 4
    out = [pltpu.VMEM((COMPS * rows, ROWS), BF16) for rows in (16, 32)]
    return pl.pallas_call(
        functools.partial(edges_kernel, parts),
        in_specs=[pl.BlockSpec(memory_space=pltpu.HBM)],
        out_specs=[pl.BlockSpec(memory_space=pltpu.VMEM)] * 3,
        out_shape=(*out, pltpu.VMEM(disp.shape, BF16)),
        scratch_shapes=[pltpu.SemaphoreType.DMA((parts,))],
        compiler_params=pltpu.CompilerParams(vmem_limit_bytes=8 * 2**20),
        cost_estimate=pl.CostEstimate(flops=10**8, bytes_accessed=3_200_000, transcendentals=0),
        name="strip_edges",
    )(pltpu.with_memory_space_constraint(disp, pltpu.HBM))


def inner_kernel(disp_ref, out_ref, beside_ref, pad_ref, code_ref):
    pad, step = 8, 16
    blocks = ROWS // BLOCK
    zeros = jnp.zeros((pad, LANES), F32)
    for k in range(2):
        code_ref[k, 0:pad, :] = zeros
        code_ref[k, pad + ROWS : 2 * pad + ROWS, :] = zeros
        for c in range(COMPS):
            pad_ref[k, c, 0:pad, :] = zeros
            pad_ref[k, c, pad + ROWS : 2 * pad + ROWS, :] = zeros
    for s in range(PER):
        for p in range(2):
            for c in range(COMPS):
                pad_ref[p, c, pad : pad + ROWS, :] = disp_ref[s, c, 1 + p].astype(F32)

            def body(i, carry):
                base = pl.multiple_of(i * step, step)
                dz, dx, dy = [], [], []
                for c in range(COMPS):
                    up = disp_ref[s, c, p + 2, pl.ds(base, step), :].astype(F32)
                    down = disp_ref[s, c, p, pl.ds(base, step), :].astype(F32)
                    dz.append(up - down)
                    center = pad_ref[p, c, pl.ds(base + pad, step), :]
                    dx.append(
                        pad_ref[p, c, pl.ds(base + pad + 1, step), :]
                        - pad_ref[p, c, pl.ds(base + pad - 1, step), :]
                    )
                    dy.append(pltpu.roll(center, LANES - 1, 1) - pltpu.roll(center, 1, 1))
                code = encode(log_det(dz, dx, dy))
                code_ref[p, pl.ds(base + pad, step), :] = code
                out_ref[s, p, i] = packed(code)
                return carry

            lax.fori_loop(0, ROWS // step, body, 0, unroll=32)
            beside_ref[2 * p + s, 0] = code_ref[p, pl.ds(pad - 1, blocks, stride=BLOCK), :]
            beside_ref[2 * p + s, 1] = code_ref[p, pl.ds(pad + BLOCK, blocks, stride=BLOCK), :]


def inner_codes(disp):
    blocks = ROWS // BLOCK
    return pl.pallas_call(
        inner_kernel,
        in_specs=[pl.BlockSpec(memory_space=pltpu.VMEM)],
        out_specs=[pl.BlockSpec(memory_space=pltpu.VMEM)] * 2,
        out_shape=(
            pltpu.VMEM((PER, 2, blocks, BLOCK, LANES), I16),
            pltpu.VMEM((2 * PER, 2, blocks, LANES), F32),
        ),
        scratch_shapes=[
            pltpu.VMEM((2, COMPS, ROWS + 16, LANES), F32),
            pltpu.VMEM((2, ROWS + 32, LANES), F32),
        ],
        compiler_params=pltpu.CompilerParams(vmem_limit_bytes=16 * 2**20),
        cost_estimate=pl.CostEstimate(flops=2 * 10**7, bytes_accessed=4_200_000, transcendentals=262144),
        name="inner_codes",
    )(pltpu.with_memory_space_constraint(disp, pltpu.VMEM))


def tail_kernel(low_ref, high_ref, left_ref, beside_ref, main_ref, out_ref, pad_ref, side_ref, tail_ref, send_ref, sem):
    copies = [
        pltpu.make_async_copy(
            main_ref.at[s, p],
            out_ref.at[:, 48 * p + BLOCK * s : 48 * p + BLOCK * s + BLOCK, :],
            sem.at[2 * s + p],
        )
        for s in range(PER)
        for p in range(2)
    ]
    for copy in copies:
        copy.start()
    inside = (lax.axis_index("strip") > 0).astype(F32)
    lane = lax.broadcasted_iota(jnp.int32, (8, ROWS), 1)

    def columns(ref):
        many = ref.shape[0] // (8 * COMPS)
        return [
            [ref[8 * (many * c + e) : 8 * (many * c + e) + 8, :] for e in range(many)] for c in range(COMPS)
        ]

    def codes(around):
        dz, dx, dy = [], [], []
        for before, center, after in around:
            dz.append(pltpu.roll(center, 6, 0) - pltpu.roll(center, 2, 0))
            dx.append(
                jnp.where(lane == ROWS - 1, 0.0, pltpu.roll(center, ROWS - 1, 1))
                - jnp.where(lane == 0, 0.0, pltpu.roll(center, 1, 1))
            )
            dy.append(after - before)
        return encode(log_det(dz, dx, dy))

    low, high, left = (columns(ref[...].astype(F32)) for ref in (low_ref, high_ref, left_ref))
    five = [
        codes([w[0:3] for w in left]),
        codes([w[1:4] for w in left]),
        codes([(w[2], w[3], v[0] * inside) for w, v in zip(left, low)]),
        codes([(w[3] * inside, v[0], v[1]) for w, v in zip(left, low)]),
        codes([w[1:4] for w in high]),
    ]
    zeros = jnp.zeros((8, LANES), F32)
    for k in range(5):
        pad_ref[k, :, 0:LANES] = zeros
        pad_ref[k, :, LANES : LANES + ROWS] = five[k]
        pad_ref[k, :, LANES + ROWS : 2 * LANES + ROWS] = zeros
    here = lax.broadcasted_iota(jnp.int32, (8, LANES), 1)
    blocks = ROWS // BLOCK
    for j in range(blocks):
        start = LANES + j * BLOCK - 1
        line = zeros
        for k in range(5):
            window, offset = start // LANES, start % LANES
            first = pltpu.roll(
                pad_ref[k, :, window * LANES : (window + 1) * LANES], (24 * k - offset) % LANES, 1
            )
            if offset + 18 > LANES:
                second = pltpu.roll(
                    pad_ref[k, :, (window + 1) * LANES : (window + 2) * LANES], (24 * k - offset) % LANES, 1
                )
                first = jnp.where(here - 24 * k < LANES - offset, first, second)
            line = first if k == 0 else jnp.where(here < 24 * k, line, first)
        side_ref[j * 8 : j * 8 + 8, :] = line
    for p in range(2):
        for s in range(PER):
            row = TAIL * p + 4 * s
            for h in range(2):
                tail_ref[pl.ds(row + h, blocks, stride=2 * TAIL), :] = beside_ref[2 * p + s, h]
            tail_ref[pl.ds(row + 2, blocks, stride=2 * TAIL), :] = side_ref[
                pl.ds(2 + 2 * p + s, blocks, stride=8), :
            ]
            tail_ref[pl.ds(row + 3, blocks, stride=2 * TAIL), :] = jnp.zeros((blocks, LANES), F32)
    send_ref[...] = packed(tail_ref[0 : blocks * 2 * TAIL, :]).reshape(blocks, 2 * TAIL, LANES)
    copies.append(
        pltpu.make_async_copy(send_ref, out_ref.at[:, MAIN : MAIN + 2 * TAIL, :], sem.at[2 * PER])
    )
    copies[-1].start()
    for copy in copies:
        copy.wait()


def with_tails(low, high, left, beside, main):
    blocks = ROWS // BLOCK
    vmem = pl.BlockSpec(memory_space=pltpu.VMEM)
    return pl.pallas_call(
        tail_kernel,
        in_specs=[vmem] * 5,
        out_specs=pl.BlockSpec(memory_space=pltpu.HBM),
        out_shape=pltpu.HBM((blocks, PAIR, LANES), I16),
        scratch_shapes=[
            pltpu.VMEM((5, 8, ROWS + 2 * LANES), F32),
            pltpu.VMEM((blocks * 8 + 8, LANES), F32),
            pltpu.VMEM((blocks * 2 * TAIL + 16, LANES), F32),
            pltpu.VMEM((blocks, 2 * TAIL, LANES), I16),
            pltpu.SemaphoreType.DMA((2 * PER + 1,)),
        ],
        compiler_params=pltpu.CompilerParams(vmem_limit_bytes=8 * 2**20),
        cost_estimate=pl.CostEstimate(flops=10**6, bytes_accessed=5 * 10**5, transcendentals=5 * 10**4),
        name="with_tails",
    )(*(pltpu.with_memory_space_constraint(x, pltpu.VMEM) for x in (low, high, left, beside, main)))


def designs_kernel(age_ref, code_ref, perms_ref, out_ref):
    subjects = age_ref.shape[1]
    half = subjects // PER

    def total(v):
        return jnp.sum(v, axis=1, keepdims=True)

    def centred(v):
        return v - total(v) * (1.0 / subjects)

    basis = []
    for raw in (
        (code_ref[...] == 1).astype(F32),
        age_ref[...],
        (code_ref[...] == 2).astype(F32),
    ):
        v = centred(raw)
        for _ in range(2):
            for q in basis:
                v = v - q * total(q * v)
            v = centred(v)
        basis.append(v / jnp.sqrt(total(v * v)))
    scale = (0.15 / (subjects - 4)) ** 0.5
    lane = lax.broadcasted_iota(jnp.int32, (8, subjects), 1)
    order = PER * (lane % half) + lane // half
    for k, q in enumerate(basis):
        table = jnp.broadcast_to(q * scale, (8, subjects))

        def put(row, values):
            high = values.astype(BF16)
            rest = (values - high.astype(F32)).astype(BF16)
            at = pl.ds(k * GROUP + row, 16)
            out_ref[at, 0:subjects] = high
            out_ref[at, subjects : 2 * subjects] = high
            out_ref[at, 2 * subjects : 3 * subjects] = rest

        for g in range(PERMS // 16):
            two = []
            for h in range(2):
                who = jnp.take_along_axis(perms_ref[g * 16 + h * 8 : g * 16 + h * 8 + 8, :], order, axis=1)
                two.append(jnp.take_along_axis(table, who, axis=1))
            put(g * 16, jnp.concatenate(two, axis=0))
        plain = jnp.take_along_axis(table, order, axis=1)
        put(PERMS, jnp.concatenate([plain, plain], axis=0))


def design_rows(age, codes, perms):
    subjects = age.shape[0]
    return pl.pallas_call(
        designs_kernel,
        out_shape=jax.ShapeDtypeStruct((3 * GROUP, 3 * subjects), BF16),
        compiler_params=pltpu.CompilerParams(vmem_limit_bytes=8 * 2**20),
        cost_estimate=pl.CostEstimate(flops=4 * 10**6, bytes_accessed=800_000, transcendentals=0),
        name="design_rows",
    )(age.reshape(1, subjects), codes.reshape(1, subjects), perms)


def stats_kernel(senders, code_ref, rows_ref, tmap_ref, peaks_ref, value_ref, y_ref, sum_ref, rss_ref, top_ref, best_ref):
    subjects = PER * senders
    lane = lax.broadcasted_iota(jnp.int32, (subjects, LANES), 1)
    odd = lax.axis_index("subj") % 2
    main = odd * TAIL
    tail = (1 - odd) * MAIN
    per = 4 * CHUNK

    def unpack(i, carry):
        at = pl.ds(pl.multiple_of(i * per, 32), per)
        value_ref[at, :] = decode(code_ref[at, :].astype(F32))
        return carry

    lax.fori_loop(0, senders * CHUNK // per, unpack, 0, unroll=4)

    def gathered(offsets):
        return jnp.concatenate(
            [value_ref[pl.ds(offset, senders, stride=CHUNK), :] for offset in offsets], axis=0
        )

    def place(block, y):
        y = y - jnp.sum(y, axis=0, keepdims=True) * (1.0 / subjects)
        at = pl.ds(pl.multiple_of(block * LANES, LANES), LANES)
        sum_ref[0:1, at] = jnp.sum(y * y, axis=0, keepdims=True) * (0.15 / (subjects - 4)) + FLOOR
        high = y.astype(BF16)
        y_ref[0:subjects, at] = high
        y_ref[subjects : 2 * subjects, at] = (y - high.astype(F32)).astype(BF16)
        y_ref[2 * subjects : 3 * subjects, at] = high

    far = lane // 2 + jnp.where(lane % 2 == 0, 97, 1)
    near = (lane - 36) // 3 + 24 * ((lane - 36) % 3 + 1)
    sides = jnp.take_along_axis(
        gathered([tail + 2, tail + 6]),
        jnp.where(lane < 32, far, jnp.where((lane >= 36) & (lane < 90), near, 0)),
        axis=1,
    )

    def mended(y, r):
        ends = pltpu.roll(sides, LANES - 41 - 3 * r, 1)
        return jnp.where((lane == 0) | (lane >= LANES - 2), ends, y)

    blocks = BLOCK + 3

    def placed(block):
        if block < BLOCK:
            y = mended(gathered([main + block, main + BLOCK + block]), block)
        elif block < BLOCK + 2:
            h = block - BLOCK
            y = mended(gathered([tail + h, tail + 4 + h]), BLOCK * h - 1 + h)
        else:
            y = sides
        place(block, y)

    def project(start):
        at = slice(start * LANES, min(start + 2, blocks) * LANES)
        proj = jnp.dot(rows_ref[...], y_ref[:, at], preferred_element_type=F32)
        q1, q2, q3 = (proj[k * GROUP : (k + 1) * GROUP] for k in range(3))
        rss_ref[:, at] = sum_ref[0:1, at] - q1 * q1 - q2 * q2 - q3 * q3
        top_ref[:, at] = q3

    here = lax.broadcasted_iota(jnp.int32, (8, LANES), 1)
    first = lax.axis_index("strip") == 0
    seam = (here == LANES - 3) | (here == LANES - 2)
    from_before = (here == LANES - 2) | ((here == 0) & first)
    from_after = (here == LANES - 3) | ((here == LANES - 1) & first)
    unscale = ((subjects - 4) / 0.15) ** 0.5

    def pseudo_t(g, r):
        at = slice(g * 8, g * 8 + 8) if isinstance(g, int) else pl.ds(pl.multiple_of(g * 8, 8), 8)

        def block(b):
            return rss_ref[at, b * LANES : (b + 1) * LANES]

        mine = block(r)
        above = block(r - 1 if r > 0 else BLOCK)
        below = block(r + 1 if r < BLOCK - 1 else BLOCK + 1)
        ends = jnp.where(seam, pltpu.roll(block(BLOCK + 2), LANES - 3 - 2 * r, 1), FLOOR)
        before = jnp.where(from_before, ends, pltpu.roll(mine, 1, 1))
        after = jnp.where(from_after, ends, pltpu.roll(mine, LANES - 1, 1))
        beside = (above + below) + (before + after)
        variance = CENTRE * mine + beside
        return top_ref[at, r * LANES : (r + 1) * LANES] * lax.rsqrt(variance)

    def peaks_of(first_row, last_row):
        for g in range(PERMS // 8):
            at = slice(g * 8, g * 8 + 8)
            best = best_ref[at, :] if first_row > 0 else jnp.zeros((8, LANES), F32)
            for r in range(first_row, last_row):
                best = jnp.maximum(best, jnp.abs(pseudo_t(g, r)))
            best_ref[at, :] = best

    for block in (BLOCK, BLOCK + 1, BLOCK + 2):
        placed(block)
    project(BLOCK)
    project(BLOCK + 2)
    done = 0
    for start in range(0, BLOCK, 2):
        for block in range(start, start + 2):
            placed(block)
        project(start)
        ready = start + 1 if start < BLOCK - 2 else BLOCK
        if start % 4 == 2:
            peaks_of(done, ready)
            done = ready

    half = BLOCK // 2
    for r in range(BLOCK):
        tmap_ref[(r // half + odd) % 2, r % half : r % half + 1, :] = (
            pseudo_t(PERMS // 8, r)[0:1, :] * unscale
        )
    code = jnp.max(best_ref[...].T, axis=0, keepdims=True) * (unscale / REACH_T)
    code = jnp.minimum(jnp.sqrt(jnp.sqrt(code)), 1.0) * LEVELS + 0.5
    lines = jnp.concatenate([code[:, k * LANES : (k + 1) * LANES] for k in range(PERMS // LANES)] * 4, axis=0)
    everyone = peaks_ref.shape[0]
    peaks_ref[...] = jnp.broadcast_to(packed(lines)[None], (everyone // 4, 8, LANES)).reshape(everyone, 2, LANES)


def block_stats(codes, rows, senders, everyone):
    subjects = PER * senders
    columns = (BLOCK + 3) * LANES
    return pl.pallas_call(
        functools.partial(stats_kernel, senders),
        out_shape=(
            jax.ShapeDtypeStruct((2, BLOCK // 2, LANES), F32),
            jax.ShapeDtypeStruct((everyone, PERMS // LANES, LANES), I16),
        ),
        scratch_shapes=[
            pltpu.VMEM((senders * CHUNK + CHUNK, LANES), F32),
            pltpu.VMEM((3 * subjects, columns), BF16),
            pltpu.VMEM((8, columns), F32),
            pltpu.VMEM((GROUP, columns), F32),
            pltpu.VMEM((GROUP, columns), F32),
            pltpu.VMEM((PERMS, LANES), F32),
        ],
        compiler_params=pltpu.CompilerParams(vmem_limit_bytes=24 * 2**20),
        cost_estimate=pl.CostEstimate(flops=2 * 10**9, bytes_accessed=10**6, transcendentals=10**6),
        name="block_stats",
    )(codes, rows)


def on_device(displacement, age, group_codes, perms):
    senders = lax.axis_size("subj")
    strips = lax.axis_size("strip")
    low, high, field = strip_edges(displacement)
    left = lax.ppermute(high, "strip", [(i, (i + 1) % strips) for i in range(strips)])
    main, beside = inner_codes(field)
    rows = design_rows(age, group_codes, perms)
    sent = with_tails(low, high, left, beside, main)
    codes = lax.all_to_all(
        sent.reshape(senders, CHUNK, LANES), "subj", split_axis=0, concat_axis=0, tiled=True
    )
    everyone = senders * strips
    tested, mine = block_stats(codes.reshape(senders * CHUNK, LANES), rows, senders, everyone)

    odd = lax.axis_index("subj") % 2 == 1
    swapped = lax.ppermute(tested[1], "subj", [(i, i ^ 1) for i in range(senders)])
    t_map = jnp.stack([jnp.where(odd, swapped, tested[0]), jnp.where(odd, tested[0], swapped)])
    beyond = lax.ppermute(t_map, "strip", [((i + 1) % strips, i) for i in range(strips)])
    t_map = jnp.where(lax.broadcasted_iota(jnp.int32, t_map.shape, 2) >= LANES - 2, beyond, t_map)

    theirs = lax.all_to_all(mine, ("subj", "strip"), split_axis=0, concat_axis=0, tiled=True)
    root = jnp.max(theirs.astype(F32), axis=0).reshape(PERMS) * (REACH_T**0.25 / LEVELS)
    return t_map, (root * root) * (root * root)


def solution(mesh):
    placed = (P("subj", None, None, None, "strip"), P(), P(), P())
    return jax.shard_map(
        on_device,
        mesh=mesh,
        in_specs=placed,
        out_specs=(P(None, "subj", "strip"), P()),
        check_vma=False,
    )
```

```python
import functools

import jax
import jax.numpy as jnp
from jax import lax
from jax.experimental import pallas as pl
from jax.experimental.pallas import tpu as pltpu
from jax.sharding import PartitionSpec as P

F32, BF16, I16 = jnp.float32, jnp.bfloat16, jnp.int16
LANES = 128
ROWS = 512
BLOCK = 16
PER = 2
CHUNK = BLOCK + 3
COMPS, PLANES = 3, 4
PERMS, GROUP = 256, 272
REACH = 0.6
REACH_T = 6800.0
LEVELS = 32767.0
CENTRE = 0.4 / 0.15
FLOOR = 1e-06 / (CENTRE + 4.0)


def encode(y):
    half = y * lax.rsqrt(jnp.maximum(jnp.abs(y), 1e-30))
    fourth = half * lax.rsqrt(jnp.maximum(jnp.abs(half), 1e-15))
    shift = 1.5 * 2.0**23
    return (fourth * (LEVELS / REACH**0.25) + shift) - shift


def decode(code):
    part = code * (REACH**0.25 / LEVELS)
    return (part * jnp.abs(part)) * (part * part)


def words(first, second):
    return (first.astype(jnp.int32) << 16) | (second.astype(jnp.int32) & 0xFFFF)


def codes_of(word):
    return (word >> 16).astype(F32), ((word << 16) >> 16).astype(F32)


def log_det(dz, dx, dy):
    j00, j01, j02 = 2.0 + dz[0], dx[0], dy[0]
    j10, j11, j12 = dz[1], 2.0 + dx[1], dy[1]
    j20, j21, j22 = dz[2], dx[2], 2.0 + dy[2]
    det = (
        j00 * (j11 * j22 - j12 * j21)
        - j01 * (j10 * j22 - j12 * j20)
        + j02 * (j10 * j21 - j11 * j20)
    )
    return jnp.log(det * 0.125)


def edges_kernel(parts, disp_ref, low_ref, high_ref, field_ref, sem):
    rows = ROWS // parts
    copies = [
        pltpu.make_async_copy(
            disp_ref.at[:, :, :, h * rows : (h + 1) * rows, :],
            field_ref.at[:, :, :, h * rows : (h + 1) * rows, :],
            sem.at[h],
        )
        for h in range(parts)
    ]
    for copy in copies:
        copy.start()
    row = lax.broadcasted_iota(jnp.int32, (48, 2 * LANES), 0)
    lane = lax.broadcasted_iota(jnp.int32, (48, 2 * LANES), 1)
    column = jnp.where(row < 16, row // 8, row // 8 - 2 + LANES - 4)
    picks = [
        ((row % 8 == 2 * q + lane // LANES) & (lane % LANES == column)).astype(F32).astype(BF16)
        for q in range(PLANES)
    ]
    for h in range(parts):
        copies[h].wait()
        at = slice(h * rows, (h + 1) * rows)
        for c in range(COMPS):
            acc = jnp.zeros((48, rows), F32)
            for q in range(PLANES):
                both = jnp.concatenate([field_ref[0, c, q, at, :], field_ref[1, c, q, at, :]], axis=1)
                acc = acc + lax.dot_general(
                    picks[q], both, (((1,), (1,)), ((), ())), preferred_element_type=F32
                )
            low_ref[c * 16 : c * 16 + 16, at] = acc[0:16].astype(BF16)
            high_ref[c * 32 : c * 32 + 32, at] = acc[16:48].astype(BF16)


def strip_edges(disp):
    parts = 4
    out = [pltpu.VMEM((COMPS * rows, ROWS), BF16) for rows in (16, 32)]
    return pl.pallas_call(
        functools.partial(edges_kernel, parts),
        in_specs=[pl.BlockSpec(memory_space=pltpu.HBM)],
        out_specs=[pl.BlockSpec(memory_space=pltpu.VMEM)] * 3,
        out_shape=(*out, pltpu.VMEM(disp.shape, BF16)),
        scratch_shapes=[pltpu.SemaphoreType.DMA((parts,))],
        compiler_params=pltpu.CompilerParams(vmem_limit_bytes=8 * 2**20),
        cost_estimate=pl.CostEstimate(flops=10**8, bytes_accessed=3_200_000, transcendentals=0),
        name="strip_edges",
    )(pltpu.with_memory_space_constraint(disp, pltpu.HBM))


def inner_kernel(disp_ref, out_ref, pad_ref, code_ref):
    pad, step = 8, 16
    blocks = ROWS // BLOCK
    zeros = jnp.zeros((pad, LANES), F32)
    for s in range(PER):
        code_ref[s, 0:pad, :] = zeros
        code_ref[s, pad + ROWS : 2 * pad + ROWS, :] = zeros
    for p in range(2):
        for c in range(COMPS):
            pad_ref[p, c, 0:pad, :] = zeros
            pad_ref[p, c, pad + ROWS : 2 * pad + ROWS, :] = zeros
    for p in range(2):
        for s in range(PER):
            for c in range(COMPS):
                pad_ref[s, c, pad : pad + ROWS, :] = disp_ref[s, c, 1 + p].astype(F32)

            def body(i, carry):
                base = pl.multiple_of(i * step, step)
                dz, dx, dy = [], [], []
                for c in range(COMPS):
                    up = disp_ref[s, c, p + 2, pl.ds(base, step), :].astype(F32)
                    down = disp_ref[s, c, p, pl.ds(base, step), :].astype(F32)
                    dz.append(up - down)
                    center = pad_ref[s, c, pl.ds(base + pad, step), :]
                    dx.append(
                        pad_ref[s, c, pl.ds(base + pad + 1, step), :]
                        - pad_ref[s, c, pl.ds(base + pad - 1, step), :]
                    )
                    dy.append(pltpu.roll(center, LANES - 1, 1) - pltpu.roll(center, 1, 1))
                code = encode(log_det(dz, dx, dy))
                code_ref[s, pl.ds(base + pad, step), :] = code
                if s == PER - 1:
                    out_ref[pl.ds((2 * i + p) * CHUNK, step), :] = words(
                        code_ref[0, pl.ds(base + pad, step), :], code
                    )
                return carry

            lax.fori_loop(0, ROWS // step, body, 0, unroll=32)
        for h, start in enumerate((pad - 1, pad + BLOCK)):
            out_ref[pl.ds(p * CHUNK + BLOCK + h, blocks, stride=2 * CHUNK), :] = words(
                *(code_ref[s, pl.ds(start, blocks, stride=BLOCK), :] for s in range(PER))
            )


def inner_codes(disp, chunks):
    return pl.pallas_call(
        inner_kernel,
        in_specs=[pl.BlockSpec(memory_space=pltpu.VMEM)],
        out_specs=pl.BlockSpec(memory_space=pltpu.VMEM),
        out_shape=pltpu.VMEM((chunks * CHUNK + 2 * CHUNK + 2, LANES), jnp.int32),
        scratch_shapes=[
            pltpu.VMEM((2, COMPS, ROWS + 16, LANES), F32),
            pltpu.VMEM((2, ROWS + 32, LANES), F32),
        ],
        compiler_params=pltpu.CompilerParams(vmem_limit_bytes=16 * 2**20),
        cost_estimate=pl.CostEstimate(flops=2 * 10**7, bytes_accessed=4_200_000, transcendentals=262144),
        name="inner_codes",
    )(pltpu.with_memory_space_constraint(disp, pltpu.VMEM))


def tail_kernel(low_ref, high_ref, left_ref, main_ref, out_ref, pad_ref, side_ref, send_ref, sem):
    send_ref[...] = main_ref[...]
    inside = (lax.axis_index("strip") > 0).astype(F32)
    lane = lax.broadcasted_iota(jnp.int32, (8, ROWS), 1)

    def columns(ref):
        many = ref.shape[0] // (8 * COMPS)
        return [
            [ref[8 * (many * c + e) : 8 * (many * c + e) + 8, :] for e in range(many)] for c in range(COMPS)
        ]

    def codes(around):
        dz, dx, dy = [], [], []
        for before, center, after in around:
            dz.append(pltpu.roll(center, 6, 0) - pltpu.roll(center, 2, 0))
            dx.append(
                jnp.where(lane == ROWS - 1, 0.0, pltpu.roll(center, ROWS - 1, 1))
                - jnp.where(lane == 0, 0.0, pltpu.roll(center, 1, 1))
            )
            dy.append(after - before)
        return encode(log_det(dz, dx, dy))

    low, high, left = (columns(ref[...].astype(F32)) for ref in (low_ref, high_ref, left_ref))
    five = [
        codes([w[0:3] for w in left]),
        codes([w[1:4] for w in left]),
        codes([(w[2], w[3], v[0] * inside) for w, v in zip(left, low)]),
        codes([(w[3] * inside, v[0], v[1]) for w, v in zip(left, low)]),
        codes([w[1:4] for w in high]),
    ]
    zeros = jnp.zeros((8, LANES), F32)
    for k in range(5):
        pad_ref[k, :, 0:LANES] = zeros
        pad_ref[k, :, LANES : LANES + ROWS] = five[k]
        pad_ref[k, :, LANES + ROWS : 2 * LANES + ROWS] = zeros
    here = lax.broadcasted_iota(jnp.int32, (8, LANES), 1)
    blocks = ROWS // BLOCK
    for j in range(blocks):
        start = LANES + j * BLOCK - 1
        line = zeros
        for k in range(5):
            window, offset = start // LANES, start % LANES
            first = pltpu.roll(
                pad_ref[k, :, window * LANES : (window + 1) * LANES], (24 * k - offset) % LANES, 1
            )
            if offset + 18 > LANES:
                second = pltpu.roll(
                    pad_ref[k, :, (window + 1) * LANES : (window + 2) * LANES], (24 * k - offset) % LANES, 1
                )
                first = jnp.where(here - 24 * k < LANES - offset, first, second)
            line = first if k == 0 else jnp.where(here < 24 * k, line, first)
        side_ref[j * 8 : j * 8 + 8, :] = line
    for p in range(2):
        send_ref[pl.ds(p * CHUNK + BLOCK + 2, blocks, stride=2 * CHUNK), :] = words(
            *(side_ref[pl.ds(2 + 2 * p + s, blocks, stride=8), :] for s in range(PER))
        )
    copy = pltpu.make_async_copy(send_ref.at[0 : out_ref.shape[0], :], out_ref, sem)
    copy.start()
    copy.wait()


def with_tails(low, high, left, main, chunks):
    blocks = ROWS // BLOCK
    vmem = pl.BlockSpec(memory_space=pltpu.VMEM)
    return pl.pallas_call(
        tail_kernel,
        in_specs=[vmem] * 4,
        out_specs=pl.BlockSpec(memory_space=pltpu.HBM),
        out_shape=pltpu.HBM((chunks * CHUNK, LANES), jnp.int32),
        scratch_shapes=[
            pltpu.VMEM((5, 8, ROWS + 2 * LANES), F32),
            pltpu.VMEM((blocks * 8 + 8, LANES), F32),
            pltpu.VMEM(main.shape, jnp.int32),
            pltpu.SemaphoreType.DMA,
        ],
        compiler_params=pltpu.CompilerParams(vmem_limit_bytes=8 * 2**20),
        cost_estimate=pl.CostEstimate(flops=10**6, bytes_accessed=5 * 10**5, transcendentals=5 * 10**4),
        name="with_tails",
    )(*(pltpu.with_memory_space_constraint(x, pltpu.VMEM) for x in (low, high, left, main)))


def designs_kernel(age_ref, code_ref, perms_ref, out_ref):
    subjects = age_ref.shape[1]
    half = subjects // PER

    def total(v):
        return jnp.sum(v, axis=1, keepdims=True)

    def centred(v):
        return v - total(v) * (1.0 / subjects)

    basis = []
    for raw in (
        (code_ref[...] == 1).astype(F32),
        age_ref[...],
        (code_ref[...] == 2).astype(F32),
    ):
        v = centred(raw)
        for _ in range(2):
            for q in basis:
                v = v - q * total(q * v)
            v = centred(v)
        basis.append(v / jnp.sqrt(total(v * v)))
    scale = (0.15 / (subjects - 4)) ** 0.5
    lane = lax.broadcasted_iota(jnp.int32, (8, subjects), 1)
    order = PER * (lane % half) + lane // half
    for k, q in enumerate(basis):
        table = jnp.broadcast_to(q * scale, (8, subjects))

        def put(row, values):
            high = values.astype(BF16)
            rest = (values - high.astype(F32)).astype(BF16)
            at = pl.ds(k * GROUP + row, 16)
            out_ref[at, 0:subjects] = high
            out_ref[at, subjects : 2 * subjects] = high
            out_ref[at, 2 * subjects : 3 * subjects] = rest

        for g in range(PERMS // 16):
            two = []
            for h in range(2):
                who = jnp.take_along_axis(perms_ref[g * 16 + h * 8 : g * 16 + h * 8 + 8, :], order, axis=1)
                two.append(jnp.take_along_axis(table, who, axis=1))
            put(g * 16, jnp.concatenate(two, axis=0))
        plain = jnp.take_along_axis(table, order, axis=1)
        put(PERMS, jnp.concatenate([plain, plain], axis=0))


def design_rows(age, codes, perms):
    subjects = age.shape[0]
    return pl.pallas_call(
        designs_kernel,
        out_shape=jax.ShapeDtypeStruct((3 * GROUP, 3 * subjects), BF16),
        compiler_params=pltpu.CompilerParams(vmem_limit_bytes=8 * 2**20),
        cost_estimate=pl.CostEstimate(flops=4 * 10**6, bytes_accessed=800_000, transcendentals=0),
        name="design_rows",
    )(age.reshape(1, subjects), codes.reshape(1, subjects), perms)


def stats_kernel(senders, code_ref, rows_ref, tmap_ref, peaks_ref, value_ref, y_ref, sum_ref, rss_ref, top_ref, best_ref):
    subjects = PER * senders
    lane = lax.broadcasted_iota(jnp.int32, (subjects, LANES), 1)
    odd = lax.axis_index("subj") % 2
    per = 4 * CHUNK * 2

    def unpack(i, carry):
        at = pl.ds(pl.multiple_of(i * per, 8), per)
        for s, code in enumerate(codes_of(code_ref[at, :])):
            value_ref[s, at, :] = decode(code)
        return carry

    lax.fori_loop(0, senders * CHUNK // per, unpack, 0, unroll=4)

    def gathered(row):
        return jnp.concatenate(
            [value_ref[s, pl.ds(row, senders, stride=CHUNK), :] for s in range(PER)], axis=0
        )

    def place(block, y):
        y = y - jnp.sum(y, axis=0, keepdims=True) * (1.0 / subjects)
        at = pl.ds(pl.multiple_of(block * LANES, LANES), LANES)
        sum_ref[0:1, at] = jnp.sum(y * y, axis=0, keepdims=True) * (0.15 / (subjects - 4)) + FLOOR
        high = y.astype(BF16)
        y_ref[0:subjects, at] = high
        y_ref[subjects : 2 * subjects, at] = (y - high.astype(F32)).astype(BF16)
        y_ref[2 * subjects : 3 * subjects, at] = high

    far = lane // 2 + jnp.where(lane % 2 == 0, 97, 1)
    near = (lane - 36) // 3 + 24 * ((lane - 36) % 3 + 1)
    sides = jnp.take_along_axis(
        gathered(BLOCK + 2),
        jnp.where(lane < 32, far, jnp.where((lane >= 36) & (lane < 90), near, 0)),
        axis=1,
    )

    def mended(y, r):
        ends = pltpu.roll(sides, LANES - 41 - 3 * r, 1)
        return jnp.where((lane == 0) | (lane >= LANES - 2), ends, y)

    blocks = BLOCK + 3

    def placed(block):
        if block < BLOCK + 2:
            y = mended(gathered(block), -1 if block == BLOCK else min(block, BLOCK))
        else:
            y = sides
        place(block, y)

    def project(start):
        at = slice(start * LANES, min(start + 2, blocks) * LANES)
        proj = jnp.dot(rows_ref[...], y_ref[:, at], preferred_element_type=F32)
        q1, q2, q3 = (proj[k * GROUP : (k + 1) * GROUP] for k in range(3))
        rss_ref[:, at] = sum_ref[0:1, at] - q1 * q1 - q2 * q2 - q3 * q3
        top_ref[:, at] = q3

    here = lax.broadcasted_iota(jnp.int32, (8, LANES), 1)
    first = lax.axis_index("strip") == 0
    seam = (here == LANES - 3) | (here == LANES - 2)
    from_before = (here == LANES - 2) | ((here == 0) & first)
    from_after = (here == LANES - 3) | ((here == LANES - 1) & first)
    unscale = ((subjects - 4) / 0.15) ** 0.5

    def pseudo_t(g, r):
        at = slice(g * 8, g * 8 + 8) if isinstance(g, int) else pl.ds(pl.multiple_of(g * 8, 8), 8)

        def block(b):
            return rss_ref[at, b * LANES : (b + 1) * LANES]

        mine = block(r)
        above = block(r - 1 if r > 0 else BLOCK)
        below = block(r + 1 if r < BLOCK - 1 else BLOCK + 1)
        ends = jnp.where(seam, pltpu.roll(block(BLOCK + 2), LANES - 3 - 2 * r, 1), FLOOR)
        before = jnp.where(from_before, ends, pltpu.roll(mine, 1, 1))
        after = jnp.where(from_after, ends, pltpu.roll(mine, LANES - 1, 1))
        beside = (above + below) + (before + after)
        variance = CENTRE * mine + beside
        return top_ref[at, r * LANES : (r + 1) * LANES] * lax.rsqrt(variance)

    def peaks_of(first_row, last_row):
        for g in range(PERMS // 8):
            at = slice(g * 8, g * 8 + 8)
            best = best_ref[at, :] if first_row > 0 else jnp.zeros((8, LANES), F32)
            for r in range(first_row, last_row):
                best = jnp.maximum(best, jnp.abs(pseudo_t(g, r)))
            best_ref[at, :] = best

    for block in (BLOCK, BLOCK + 1, BLOCK + 2):
        placed(block)
    project(BLOCK)
    project(BLOCK + 2)
    done = 0
    for start in range(0, BLOCK, 2):
        for block in range(start, start + 2):
            placed(block)
        project(start)
        ready = start + 1 if start < BLOCK - 2 else BLOCK
        if start % 4 == 2:
            peaks_of(done, ready)
            done = ready

    half = BLOCK // 2
    for r in range(BLOCK):
        tmap_ref[(r // half + odd) % 2, r % half : r % half + 1, :] = (
            pseudo_t(PERMS // 8, r)[0:1, :] * unscale
        )
    code = jnp.max(best_ref[...].T, axis=0, keepdims=True) * (unscale / REACH_T)
    code = jnp.minimum(jnp.sqrt(jnp.sqrt(code)), 1.0) * LEVELS + 0.5
    lines = jnp.concatenate([code[:, k * LANES : (k + 1) * LANES] for k in range(PERMS // LANES)] * 4, axis=0)
    everyone = peaks_ref.shape[0]
    peaks_ref[...] = jnp.broadcast_to(lines.astype(jnp.int32).astype(I16)[None], (everyone // 4, 8, LANES)).reshape(everyone, 2, LANES)


def block_stats(codes, rows, senders, everyone):
    subjects = PER * senders
    columns = (BLOCK + 3) * LANES
    return pl.pallas_call(
        functools.partial(stats_kernel, senders),
        out_shape=(
            jax.ShapeDtypeStruct((2, BLOCK // 2, LANES), F32),
            jax.ShapeDtypeStruct((everyone, PERMS // LANES, LANES), I16),
        ),
        scratch_shapes=[
            pltpu.VMEM((PER, senders * CHUNK + CHUNK + 5, LANES), F32),
            pltpu.VMEM((3 * subjects, columns), BF16),
            pltpu.VMEM((8, columns), F32),
            pltpu.VMEM((GROUP, columns), F32),
            pltpu.VMEM((GROUP, columns), F32),
            pltpu.VMEM((PERMS, LANES), F32),
        ],
        compiler_params=pltpu.CompilerParams(vmem_limit_bytes=24 * 2**20),
        cost_estimate=pl.CostEstimate(flops=2 * 10**9, bytes_accessed=10**6, transcendentals=10**6),
        name="block_stats",
    )(codes, rows)


def on_device(displacement, age, group_codes, perms):
    senders = lax.axis_size("subj")
    strips = lax.axis_size("strip")
    low, high, field = strip_edges(displacement)
    left = lax.ppermute(high, "strip", [(i, (i + 1) % strips) for i in range(strips)])
    main = inner_codes(field, senders)
    rows = design_rows(age, group_codes, perms)
    sent = with_tails(low, high, left, main, senders)
    codes = lax.all_to_all(
        sent.reshape(senders, CHUNK, 1, LANES), "subj", split_axis=0, concat_axis=0, tiled=True
    )
    everyone = senders * strips
    tested, mine = block_stats(codes.reshape(senders * CHUNK, LANES), rows, senders, everyone)

    odd = lax.axis_index("subj") % 2 == 1
    swapped = lax.ppermute(tested[1], "subj", [(i, i ^ 1) for i in range(senders)])
    t_map = jnp.stack([jnp.where(odd, swapped, tested[0]), jnp.where(odd, tested[0], swapped)])
    beyond = lax.ppermute(t_map, "strip", [((i + 1) % strips, i) for i in range(strips)])
    t_map = jnp.where(lax.broadcasted_iota(jnp.int32, t_map.shape, 2) >= LANES - 2, beyond, t_map)

    theirs = lax.all_to_all(mine, ("subj", "strip"), split_axis=0, concat_axis=0, tiled=True)
    root = jnp.max(theirs.astype(F32), axis=0).reshape(PERMS) * (REACH_T**0.25 / LEVELS)
    return t_map, (root * root) * (root * root)


def solution(mesh):
    placed = (P("subj", None, None, None, "strip"), P(), P(), P())
    return jax.shard_map(
        on_device,
        mesh=mesh,
        in_specs=placed,
        out_specs=(P(None, "subj", "strip"), P()),
        check_vma=False,
    )
```

```python
import functools

import jax
import jax.numpy as jnp
from jax import lax
from jax.experimental import pallas as pl
from jax.experimental.pallas import tpu as pltpu
from jax.sharding import PartitionSpec as P

F32, BF16, I16 = jnp.float32, jnp.bfloat16, jnp.int16
LANES = 128
ROWS = 512
BLOCK = 16
PER = 2
CHUNK = BLOCK + 3
COMPS, PLANES = 3, 4
PERMS, GROUP = 256, 272
REACH = 0.6
REACH_T = 6800.0
LEVELS = 32767.0
CENTRE = 0.4 / 0.15
FLOOR = 1e-06 / (CENTRE + 4.0)


def encode(y):
    half = y * lax.rsqrt(jnp.maximum(jnp.abs(y), 1e-30))
    fourth = half * lax.rsqrt(jnp.maximum(jnp.abs(half), 1e-15))
    shift = 1.5 * 2.0**23
    return (fourth * (LEVELS / REACH**0.25) + shift) - shift


def decode(code):
    part = code * (REACH**0.25 / LEVELS)
    return (part * jnp.abs(part)) * (part * part)


def words(first, second):
    return (first.astype(jnp.int32) << 16) | (second.astype(jnp.int32) & 0xFFFF)


def codes_of(word):
    return (word >> 16).astype(F32), ((word << 16) >> 16).astype(F32)


def log_det(dz, dx, dy):
    j00, j01, j02 = 2.0 + dz[0], dx[0], dy[0]
    j10, j11, j12 = dz[1], 2.0 + dx[1], dy[1]
    j20, j21, j22 = dz[2], dx[2], 2.0 + dy[2]
    det = (
        j00 * (j11 * j22 - j12 * j21)
        - j01 * (j10 * j22 - j12 * j20)
        + j02 * (j10 * j21 - j11 * j20)
    )
    return jnp.log(det * 0.125)


SENT = 7


def edge_codes(around):
    lane = lax.broadcasted_iota(jnp.int32, (8, ROWS), 1)
    dz, dx, dy = [], [], []
    for before, center, after in around:
        dz.append(pltpu.roll(center, 6, 0) - pltpu.roll(center, 2, 0))
        dx.append(
            jnp.where(lane == ROWS - 1, 0.0, pltpu.roll(center, ROWS - 1, 1))
            - jnp.where(lane == 0, 0.0, pltpu.roll(center, 1, 1))
        )
        dy.append(after - before)
    return encode(log_det(dz, dx, dy))


def two_in_tile(first, second):
    row = lax.broadcasted_iota(jnp.int32, first.shape, 0)
    return jnp.where((row >= 2) & (row < 6), first, pltpu.roll(second, 4, 0))


def split_code(code):
    shift = 1.5 * 2.0**31
    high = (code + shift) - shift
    return two_in_tile(high, code - high)


def joined_code(tile):
    return tile + pltpu.roll(tile, 4, 0)


def edges_kernel(parts, disp_ref, low_ref, sent_ref, field_ref, high_ref, sem):
    rows = ROWS // parts
    copies = [
        pltpu.make_async_copy(
            disp_ref.at[:, :, :, h * rows : (h + 1) * rows, :],
            field_ref.at[:, :, :, h * rows : (h + 1) * rows, :],
            sem.at[h],
        )
        for h in range(parts)
    ]
    for copy in copies:
        copy.start()
    row = lax.broadcasted_iota(jnp.int32, (48, 2 * LANES), 0)
    lane = lax.broadcasted_iota(jnp.int32, (48, 2 * LANES), 1)
    column = jnp.where(row < 16, row // 8, row // 8 - 2 + LANES - 4)
    picks = [
        ((row % 8 == 2 * q + lane // LANES) & (lane % LANES == column)).astype(F32).astype(BF16)
        for q in range(PLANES)
    ]
    for h in range(parts):
        copies[h].wait()
        at = slice(h * rows, (h + 1) * rows)
        for c in range(COMPS):
            acc = jnp.zeros((48, rows), F32)
            for q in range(PLANES):
                both = jnp.concatenate([field_ref[0, c, q, at, :], field_ref[1, c, q, at, :]], axis=1)
                acc = acc + lax.dot_general(
                    picks[q], both, (((1,), (1,)), ((), ())), preferred_element_type=F32
                )
            low_ref[c * 16 : c * 16 + 16, at] = acc[0:16].astype(BF16)
            high_ref[c * 32 : c * 32 + 32, at] = acc[16:48]
    high = [[high_ref[32 * c + 8 * e : 32 * c + 8 * e + 8, :] for e in range(4)] for c in range(COMPS)]
    tiles = [w[3] for w in high] + [
        two_in_tile(high[0][2], high[1][2]),
        high[2][2],
        split_code(edge_codes([w[0:3] for w in high])),
        split_code(edge_codes([w[1:4] for w in high])),
    ]
    sent_ref[...] = jnp.concatenate(tiles, axis=0).astype(BF16)


def strip_edges(disp):
    parts = 4
    out = [pltpu.VMEM((rows, ROWS), BF16) for rows in (COMPS * 16, SENT * 8)]
    return pl.pallas_call(
        functools.partial(edges_kernel, parts),
        in_specs=[pl.BlockSpec(memory_space=pltpu.HBM)],
        out_specs=[pl.BlockSpec(memory_space=pltpu.VMEM)] * 3,
        out_shape=(*out, pltpu.VMEM(disp.shape, BF16)),
        scratch_shapes=[pltpu.VMEM((COMPS * 32, ROWS), F32), pltpu.SemaphoreType.DMA((parts,))],
        compiler_params=pltpu.CompilerParams(vmem_limit_bytes=8 * 2**20),
        cost_estimate=pl.CostEstimate(flops=10**8, bytes_accessed=3_200_000, transcendentals=0),
        name="strip_edges",
    )(pltpu.with_memory_space_constraint(disp, pltpu.HBM))


def inner_kernel(disp_ref, out_ref, pad_ref, code_ref):
    pad, step = 8, 16
    blocks = ROWS // BLOCK
    zeros = jnp.zeros((pad, LANES), F32)
    for s in range(PER):
        code_ref[s, 0:pad, :] = zeros
        code_ref[s, pad + ROWS : 2 * pad + ROWS, :] = zeros
    for p in range(2):
        for c in range(COMPS):
            pad_ref[p, c, 0:pad, :] = zeros
            pad_ref[p, c, pad + ROWS : 2 * pad + ROWS, :] = zeros
    for p in range(2):
        for s in range(PER):
            for c in range(COMPS):
                pad_ref[s, c, pad : pad + ROWS, :] = disp_ref[s, c, 1 + p].astype(F32)

            def body(i, carry):
                base = pl.multiple_of(i * step, step)
                dz, dx, dy = [], [], []
                for c in range(COMPS):
                    up = disp_ref[s, c, p + 2, pl.ds(base, step), :].astype(F32)
                    down = disp_ref[s, c, p, pl.ds(base, step), :].astype(F32)
                    dz.append(up - down)
                    center = pad_ref[s, c, pl.ds(base + pad, step), :]
                    dx.append(
                        pad_ref[s, c, pl.ds(base + pad + 1, step), :]
                        - pad_ref[s, c, pl.ds(base + pad - 1, step), :]
                    )
                    dy.append(pltpu.roll(center, LANES - 1, 1) - pltpu.roll(center, 1, 1))
                code = encode(log_det(dz, dx, dy))
                code_ref[s, pl.ds(base + pad, step), :] = code
                if s == PER - 1:
                    out_ref[pl.ds((2 * i + p) * CHUNK, step), :] = words(
                        code_ref[0, pl.ds(base + pad, step), :], code
                    )
                return carry

            lax.fori_loop(0, ROWS // step, body, 0, unroll=32)
        for h, start in enumerate((pad - 1, pad + BLOCK)):
            out_ref[pl.ds(p * CHUNK + BLOCK + h, blocks, stride=2 * CHUNK), :] = words(
                *(code_ref[s, pl.ds(start, blocks, stride=BLOCK), :] for s in range(PER))
            )


def inner_codes(disp, chunks):
    return pl.pallas_call(
        inner_kernel,
        in_specs=[pl.BlockSpec(memory_space=pltpu.VMEM)],
        out_specs=pl.BlockSpec(memory_space=pltpu.VMEM),
        out_shape=pltpu.VMEM((chunks * CHUNK + 2 * CHUNK + 2, LANES), jnp.int32),
        scratch_shapes=[
            pltpu.VMEM((2, COMPS, ROWS + 16, LANES), F32),
            pltpu.VMEM((2, ROWS + 32, LANES), F32),
        ],
        compiler_params=pltpu.CompilerParams(vmem_limit_bytes=16 * 2**20),
        cost_estimate=pl.CostEstimate(flops=2 * 10**7, bytes_accessed=4_200_000, transcendentals=262144),
        name="inner_codes",
    )(pltpu.with_memory_space_constraint(disp, pltpu.VMEM))


def tail_kernel(low_ref, sent_ref, left_ref, main_ref, out_ref, pad_ref, side_ref, send_ref, sem):
    send_ref[...] = main_ref[...]
    inside = (lax.axis_index("strip") > 0).astype(F32)

    def tiles(ref):
        field = ref[...].astype(F32)
        return [field[8 * k : 8 * k + 8] for k in range(ref.shape[0] // 8)]

    low, own, left = tiles(low_ref), tiles(sent_ref), tiles(left_ref)
    last = left[0:3]
    before = [left[3], pltpu.roll(left[3], 4, 0), left[4]]
    five = [
        joined_code(left[5]),
        joined_code(left[6]),
        edge_codes([(before[c], last[c], low[2 * c] * inside) for c in range(COMPS)]),
        edge_codes([(last[c] * inside, low[2 * c], low[2 * c + 1]) for c in range(COMPS)]),
        joined_code(own[6]),
    ]
    zeros = jnp.zeros((8, LANES), F32)
    for k in range(5):
        pad_ref[k, :, 0:LANES] = zeros
        pad_ref[k, :, LANES : LANES + ROWS] = five[k]
        pad_ref[k, :, LANES + ROWS : 2 * LANES + ROWS] = zeros
    here = lax.broadcasted_iota(jnp.int32, (8, LANES), 1)
    blocks = ROWS // BLOCK
    for j in range(blocks):
        start = LANES + j * BLOCK - 1
        line = zeros
        for k in range(5):
            window, offset = start // LANES, start % LANES
            first = pltpu.roll(
                pad_ref[k, :, window * LANES : (window + 1) * LANES], (24 * k - offset) % LANES, 1
            )
            if offset + 18 > LANES:
                second = pltpu.roll(
                    pad_ref[k, :, (window + 1) * LANES : (window + 2) * LANES], (24 * k - offset) % LANES, 1
                )
                first = jnp.where(here - 24 * k < LANES - offset, first, second)
            line = first if k == 0 else jnp.where(here < 24 * k, line, first)
        side_ref[j * 8 : j * 8 + 8, :] = line
    for p in range(2):
        send_ref[pl.ds(p * CHUNK + BLOCK + 2, blocks, stride=2 * CHUNK), :] = words(
            *(side_ref[pl.ds(2 + 2 * p + s, blocks, stride=8), :] for s in range(PER))
        )
    copy = pltpu.make_async_copy(send_ref.at[0 : out_ref.shape[0], :], out_ref, sem)
    copy.start()
    copy.wait()


def with_tails(low, sent, left, main, chunks):
    blocks = ROWS // BLOCK
    vmem = pl.BlockSpec(memory_space=pltpu.VMEM)
    return pl.pallas_call(
        tail_kernel,
        in_specs=[vmem] * 4,
        out_specs=pl.BlockSpec(memory_space=pltpu.HBM),
        out_shape=pltpu.HBM((chunks * CHUNK, LANES), jnp.int32),
        scratch_shapes=[
            pltpu.VMEM((5, 8, ROWS + 2 * LANES), F32),
            pltpu.VMEM((blocks * 8 + 8, LANES), F32),
            pltpu.VMEM(main.shape, jnp.int32),
            pltpu.SemaphoreType.DMA,
        ],
        compiler_params=pltpu.CompilerParams(vmem_limit_bytes=8 * 2**20),
        cost_estimate=pl.CostEstimate(flops=10**6, bytes_accessed=5 * 10**5, transcendentals=5 * 10**4),
        name="with_tails",
    )(*(pltpu.with_memory_space_constraint(x, pltpu.VMEM) for x in (low, sent, left, main)))


def designs_kernel(age_ref, code_ref, perms_ref, out_ref):
    subjects = age_ref.shape[1]
    half = subjects // PER

    def total(v):
        return jnp.sum(v, axis=1, keepdims=True)

    def centred(v):
        return v - total(v) * (1.0 / subjects)

    basis = []
    for raw in (
        (code_ref[...] == 1).astype(F32),
        age_ref[...],
        (code_ref[...] == 2).astype(F32),
    ):
        v = centred(raw)
        for _ in range(2):
            for q in basis:
                v = v - q * total(q * v)
            v = centred(v)
        basis.append(v / jnp.sqrt(total(v * v)))
    scale = (0.15 / (subjects - 4)) ** 0.5
    lane = lax.broadcasted_iota(jnp.int32, (8, subjects), 1)
    order = PER * (lane % half) + lane // half
    for k, q in enumerate(basis):
        table = jnp.broadcast_to(q * scale, (8, subjects))

        def put(row, values):
            high = values.astype(BF16)
            rest = (values - high.astype(F32)).astype(BF16)
            at = pl.ds(k * GROUP + row, 16)
            out_ref[at, 0:subjects] = high
            out_ref[at, subjects : 2 * subjects] = high
            out_ref[at, 2 * subjects : 3 * subjects] = rest

        for g in range(PERMS // 16):
            two = []
            for h in range(2):
                who = jnp.take_along_axis(perms_ref[g * 16 + h * 8 : g * 16 + h * 8 + 8, :], order, axis=1)
                two.append(jnp.take_along_axis(table, who, axis=1))
            put(g * 16, jnp.concatenate(two, axis=0))
        plain = jnp.take_along_axis(table, order, axis=1)
        put(PERMS, jnp.concatenate([plain, plain], axis=0))


def design_rows(age, codes, perms):
    subjects = age.shape[0]
    return pl.pallas_call(
        designs_kernel,
        out_shape=jax.ShapeDtypeStruct((3 * GROUP, 3 * subjects), BF16),
        compiler_params=pltpu.CompilerParams(vmem_limit_bytes=8 * 2**20),
        cost_estimate=pl.CostEstimate(flops=4 * 10**6, bytes_accessed=800_000, transcendentals=0),
        name="design_rows",
    )(age.reshape(1, subjects), codes.reshape(1, subjects), perms)


def stats_kernel(senders, code_ref, rows_ref, tmap_ref, peaks_ref, value_ref, y_ref, sum_ref, rss_ref, top_ref, best_ref):
    subjects = PER * senders
    lane = lax.broadcasted_iota(jnp.int32, (subjects, LANES), 1)
    odd = lax.axis_index("subj") % 2
    per = 4 * CHUNK * 2

    def unpack(i, carry):
        at = pl.ds(pl.multiple_of(i * per, 8), per)
        for s, code in enumerate(codes_of(code_ref[at, :])):
            value_ref[s, at, :] = decode(code)
        return carry

    lax.fori_loop(0, senders * CHUNK // per, unpack, 0, unroll=4)

    def gathered(row):
        return jnp.concatenate(
            [value_ref[s, pl.ds(row, senders, stride=CHUNK), :] for s in range(PER)], axis=0
        )

    def place(block, y):
        y = y - jnp.sum(y, axis=0, keepdims=True) * (1.0 / subjects)
        at = pl.ds(pl.multiple_of(block * LANES, LANES), LANES)
        sum_ref[0:1, at] = jnp.sum(y * y, axis=0, keepdims=True) * (0.15 / (subjects - 4)) + FLOOR
        high = y.astype(BF16)
        y_ref[0:subjects, at] = high
        y_ref[subjects : 2 * subjects, at] = (y - high.astype(F32)).astype(BF16)
        y_ref[2 * subjects : 3 * subjects, at] = high

    far = lane // 2 + jnp.where(lane % 2 == 0, 97, 1)
    near = (lane - 36) // 3 + 24 * ((lane - 36) % 3 + 1)
    sides = jnp.take_along_axis(
        gathered(BLOCK + 2),
        jnp.where(lane < 32, far, jnp.where((lane >= 36) & (lane < 90), near, 0)),
        axis=1,
    )

    def mended(y, r):
        ends = pltpu.roll(sides, LANES - 41 - 3 * r, 1)
        return jnp.where((lane == 0) | (lane >= LANES - 2), ends, y)

    blocks = BLOCK + 3

    def placed(block):
        if block < BLOCK + 2:
            y = mended(gathered(block), -1 if block == BLOCK else min(block, BLOCK))
        else:
            y = sides
        place(block, y)

    def project(start):
        at = slice(start * LANES, min(start + 2, blocks) * LANES)
        proj = jnp.dot(rows_ref[...], y_ref[:, at], preferred_element_type=F32)
        q1, q2, q3 = (proj[k * GROUP : (k + 1) * GROUP] for k in range(3))
        rss_ref[:, at] = sum_ref[0:1, at] - q1 * q1 - q2 * q2 - q3 * q3
        top_ref[:, at] = q3

    here = lax.broadcasted_iota(jnp.int32, (8, LANES), 1)
    first = lax.axis_index("strip") == 0
    seam = (here == LANES - 3) | (here == LANES - 2)
    from_before = (here == LANES - 2) | ((here == 0) & first)
    from_after = (here == LANES - 3) | ((here == LANES - 1) & first)
    unscale = ((subjects - 4) / 0.15) ** 0.5

    def pseudo_t(g, r):
        at = slice(g * 8, g * 8 + 8) if isinstance(g, int) else pl.ds(pl.multiple_of(g * 8, 8), 8)

        def block(b):
            return rss_ref[at, b * LANES : (b + 1) * LANES]

        mine = block(r)
        above = block(r - 1 if r > 0 else BLOCK)
        below = block(r + 1 if r < BLOCK - 1 else BLOCK + 1)
        ends = jnp.where(seam, pltpu.roll(block(BLOCK + 2), LANES - 3 - 2 * r, 1), FLOOR)
        before = jnp.where(from_before, ends, pltpu.roll(mine, 1, 1))
        after = jnp.where(from_after, ends, pltpu.roll(mine, LANES - 1, 1))
        beside = (above + below) + (before + after)
        variance = CENTRE * mine + beside
        return top_ref[at, r * LANES : (r + 1) * LANES] * lax.rsqrt(variance)

    def peaks_of(first_row, last_row):
        for g in range(PERMS // 8):
            at = slice(g * 8, g * 8 + 8)
            best = best_ref[at, :] if first_row > 0 else jnp.zeros((8, LANES), F32)
            for r in range(first_row, last_row):
                best = jnp.maximum(best, jnp.abs(pseudo_t(g, r)))
            best_ref[at, :] = best

    for block in (BLOCK, BLOCK + 1, BLOCK + 2):
        placed(block)
    project(BLOCK)
    project(BLOCK + 2)
    done = 0
    for start in range(0, BLOCK, 2):
        for block in range(start, start + 2):
            placed(block)
        project(start)
        ready = start + 1 if start < BLOCK - 2 else BLOCK
        if start % 4 == 2:
            peaks_of(done, ready)
            done = ready

    half = BLOCK // 2
    for r in range(BLOCK):
        tmap_ref[(r // half + odd) % 2, r % half : r % half + 1, :] = (
            pseudo_t(PERMS // 8, r)[0:1, :] * unscale
        )
    code = jnp.max(best_ref[...].T, axis=0, keepdims=True) * (unscale / REACH_T)
    code = jnp.minimum(jnp.sqrt(jnp.sqrt(code)), 1.0) * LEVELS + 0.5
    lines = jnp.concatenate([code[:, k * LANES : (k + 1) * LANES] for k in range(PERMS // LANES)] * 4, axis=0)
    everyone = peaks_ref.shape[0]
    peaks_ref[...] = jnp.broadcast_to(lines.astype(jnp.int32).astype(I16)[None], (everyone // 4, 8, LANES)).reshape(everyone, 2, LANES)


def block_stats(codes, rows, senders, everyone):
    subjects = PER * senders
    columns = (BLOCK + 3) * LANES
    return pl.pallas_call(
        functools.partial(stats_kernel, senders),
        out_shape=(
            jax.ShapeDtypeStruct((2, BLOCK // 2, LANES), F32),
            jax.ShapeDtypeStruct((everyone, PERMS // LANES, LANES), I16),
        ),
        scratch_shapes=[
            pltpu.VMEM((PER, senders * CHUNK + CHUNK + 5, LANES), F32),
            pltpu.VMEM((3 * subjects, columns), BF16),
            pltpu.VMEM((8, columns), F32),
            pltpu.VMEM((GROUP, columns), F32),
            pltpu.VMEM((GROUP, columns), F32),
            pltpu.VMEM((PERMS, LANES), F32),
        ],
        compiler_params=pltpu.CompilerParams(vmem_limit_bytes=24 * 2**20),
        cost_estimate=pl.CostEstimate(flops=2 * 10**9, bytes_accessed=10**6, transcendentals=10**6),
        name="block_stats",
    )(codes, rows)


def on_device(displacement, age, group_codes, perms):
    senders = lax.axis_size("subj")
    strips = lax.axis_size("strip")
    low, after, field = strip_edges(displacement)
    left = lax.ppermute(after, "strip", [(i, (i + 1) % strips) for i in range(strips)])
    main = inner_codes(field, senders)
    rows = design_rows(age, group_codes, perms)
    sent = with_tails(low, after, left, main, senders)
    codes = lax.all_to_all(
        sent.reshape(senders, CHUNK, 1, LANES), "subj", split_axis=0, concat_axis=0, tiled=True
    )
    everyone = senders * strips
    tested, mine = block_stats(codes.reshape(senders * CHUNK, LANES), rows, senders, everyone)

    odd = lax.axis_index("subj") % 2 == 1
    swapped = lax.ppermute(tested[1], "subj", [(i, i ^ 1) for i in range(senders)])
    t_map = jnp.stack([jnp.where(odd, swapped, tested[0]), jnp.where(odd, tested[0], swapped)])
    beyond = lax.ppermute(t_map, "strip", [((i + 1) % strips, i) for i in range(strips)])
    t_map = jnp.where(lax.broadcasted_iota(jnp.int32, t_map.shape, 2) >= LANES - 2, beyond, t_map)

    theirs = lax.all_to_all(mine, ("subj", "strip"), split_axis=0, concat_axis=0, tiled=True)
    root = jnp.max(theirs.astype(F32), axis=0).reshape(PERMS) * (REACH_T**0.25 / LEVELS)
    return t_map, (root * root) * (root * root)


def solution(mesh):
    placed = (P("subj", None, None, None, "strip"), P(), P(), P())
    return jax.shard_map(
        on_device,
        mesh=mesh,
        in_specs=placed,
        out_specs=(P(None, "subj", "strip"), P()),
        check_vma=False,
    )
```

```python
import functools

import jax
import jax.numpy as jnp
from jax import lax
from jax.experimental import pallas as pl
from jax.experimental.pallas import tpu as pltpu
from jax.sharding import PartitionSpec as P

F32, BF16, I16 = jnp.float32, jnp.bfloat16, jnp.int16
LANES = 128
ROWS = 512
BLOCK = 16
PER = 2
CHUNK = BLOCK + 3
COMPS, PLANES = 3, 4
PERMS, GROUP = 256, 272
REACH = 0.6
REACH_T = 6800.0
LEVELS = 32767.0
CENTRE = 0.4 / 0.15
FLOOR = 1e-06 / (CENTRE + 4.0)


def encode(y):
    half = y * lax.rsqrt(jnp.maximum(jnp.abs(y), 1e-30))
    fourth = half * lax.rsqrt(jnp.maximum(jnp.abs(half), 1e-15))
    shift = 1.5 * 2.0**23
    return (fourth * (LEVELS / REACH**0.25) + shift) - shift


def decode(code):
    part = code * (REACH**0.25 / LEVELS)
    return (part * jnp.abs(part)) * (part * part)


def words(first, second):
    return (first.astype(jnp.int32) << 16) | (second.astype(jnp.int32) & 0xFFFF)


def codes_of(word):
    return (word >> 16).astype(F32), ((word << 16) >> 16).astype(F32)


def log_det(dz, dx, dy):
    j00, j01, j02 = 2.0 + dz[0], dx[0], dy[0]
    j10, j11, j12 = dz[1], 2.0 + dx[1], dy[1]
    j20, j21, j22 = dz[2], dx[2], 2.0 + dy[2]
    det = (
        j00 * (j11 * j22 - j12 * j21)
        - j01 * (j10 * j22 - j12 * j20)
        + j02 * (j10 * j21 - j11 * j20)
    )
    return jnp.log(det * 0.125)


SENT = 7


def edge_codes(around):
    lane = lax.broadcasted_iota(jnp.int32, (8, ROWS), 1)
    dz, dx, dy = [], [], []
    for before, center, after in around:
        dz.append(pltpu.roll(center, 6, 0) - pltpu.roll(center, 2, 0))
        dx.append(
            jnp.where(lane == ROWS - 1, 0.0, pltpu.roll(center, ROWS - 1, 1))
            - jnp.where(lane == 0, 0.0, pltpu.roll(center, 1, 1))
        )
        dy.append(after - before)
    return encode(log_det(dz, dx, dy))


def two_in_tile(first, second):
    row = lax.broadcasted_iota(jnp.int32, first.shape, 0)
    return jnp.where((row >= 2) & (row < 6), first, pltpu.roll(second, 4, 0))


def split_code(code):
    shift = 1.5 * 2.0**31
    high = (code + shift) - shift
    return two_in_tile(high, code - high)


def joined_code(tile):
    return tile + pltpu.roll(tile, 4, 0)


def edges_kernel(disp_ref, low_ref, sent_ref, field_ref, high_ref, sem):
    copies = [
        [pltpu.make_async_copy(disp_ref.at[s, c], field_ref.at[s, c], sem.at[c, s]) for s in range(PER)]
        for c in range(COMPS)
    ]
    for pair in copies:
        for copy in pair:
            copy.start()
    row = lax.broadcasted_iota(jnp.int32, (48, 2 * LANES), 0)
    lane = lax.broadcasted_iota(jnp.int32, (48, 2 * LANES), 1)
    column = jnp.where(row < 16, row // 8, row // 8 - 2 + LANES - 4)
    picks = [
        ((row % 8 == 2 * q + lane // LANES) & (lane % LANES == column)).astype(F32).astype(BF16)
        for q in range(PLANES)
    ]
    for c in range(COMPS):
        for copy in copies[c]:
            copy.wait()
        acc = jnp.zeros((48, ROWS), F32)
        for q in range(PLANES):
            both = jnp.concatenate([field_ref[0, c, q], field_ref[1, c, q]], axis=1)
            acc = acc + lax.dot_general(
                picks[q], both, (((1,), (1,)), ((), ())), preferred_element_type=F32
            )
        low_ref[c * 16 : c * 16 + 16, :] = acc[0:16].astype(BF16)
        high_ref[c * 32 : c * 32 + 32, :] = acc[16:48]
    high = [[high_ref[32 * c + 8 * e : 32 * c + 8 * e + 8, :] for e in range(4)] for c in range(COMPS)]
    tiles = [w[3] for w in high] + [
        two_in_tile(high[0][2], high[1][2]),
        high[2][2],
        split_code(edge_codes([w[0:3] for w in high])),
        split_code(edge_codes([w[1:4] for w in high])),
    ]
    sent_ref[...] = jnp.concatenate(tiles, axis=0).astype(BF16)


def strip_edges(disp):
    out = [pltpu.VMEM((rows, ROWS), BF16) for rows in (COMPS * 16, SENT * 8)]
    return pl.pallas_call(
        edges_kernel,
        in_specs=[pl.BlockSpec(memory_space=pltpu.HBM)],
        out_specs=[pl.BlockSpec(memory_space=pltpu.VMEM)] * 3,
        out_shape=(*out, pltpu.VMEM(disp.shape, BF16)),
        scratch_shapes=[pltpu.VMEM((COMPS * 32, ROWS), F32), pltpu.SemaphoreType.DMA((COMPS, PER))],
        compiler_params=pltpu.CompilerParams(vmem_limit_bytes=8 * 2**20),
        cost_estimate=pl.CostEstimate(flops=10**8, bytes_accessed=3_200_000, transcendentals=0),
        name="strip_edges",
    )(pltpu.with_memory_space_constraint(disp, pltpu.HBM))


def inner_kernel(disp_ref, out_ref, pad_ref, code_ref):
    pad, step = 8, 16
    blocks = ROWS // BLOCK
    zeros = jnp.zeros((pad, LANES), F32)
    for s in range(PER):
        code_ref[s, 0:pad, :] = zeros
        code_ref[s, pad + ROWS : 2 * pad + ROWS, :] = zeros
    for p in range(2):
        for c in range(COMPS):
            pad_ref[p, c, 0:pad, :] = zeros
            pad_ref[p, c, pad + ROWS : 2 * pad + ROWS, :] = zeros
    for p in range(2):
        for s in range(PER):
            for c in range(COMPS):
                pad_ref[s, c, pad : pad + ROWS, :] = disp_ref[s, c, 1 + p].astype(F32)

            def body(i, carry):
                base = pl.multiple_of(i * step, step)
                dz, dx, dy = [], [], []
                for c in range(COMPS):
                    up = disp_ref[s, c, p + 2, pl.ds(base, step), :].astype(F32)
                    down = disp_ref[s, c, p, pl.ds(base, step), :].astype(F32)
                    dz.append(up - down)
                    center = pad_ref[s, c, pl.ds(base + pad, step), :]
                    dx.append(
                        pad_ref[s, c, pl.ds(base + pad + 1, step), :]
                        - pad_ref[s, c, pl.ds(base + pad - 1, step), :]
                    )
                    dy.append(pltpu.roll(center, LANES - 1, 1) - pltpu.roll(center, 1, 1))
                code = encode(log_det(dz, dx, dy))
                code_ref[s, pl.ds(base + pad, step), :] = code
                if s == PER - 1:
                    out_ref[pl.ds((2 * i + p) * CHUNK, step), :] = words(
                        code_ref[0, pl.ds(base + pad, step), :], code
                    )
                return carry

            lax.fori_loop(0, ROWS // step, body, 0, unroll=32)
        for h, start in enumerate((pad - 1, pad + BLOCK)):
            out_ref[pl.ds(p * CHUNK + BLOCK + h, blocks, stride=2 * CHUNK), :] = words(
                *(code_ref[s, pl.ds(start, blocks, stride=BLOCK), :] for s in range(PER))
            )


def inner_codes(disp, chunks):
    return pl.pallas_call(
        inner_kernel,
        in_specs=[pl.BlockSpec(memory_space=pltpu.VMEM)],
        out_specs=pl.BlockSpec(memory_space=pltpu.VMEM),
        out_shape=pltpu.VMEM((chunks * CHUNK + 2 * CHUNK + 2, LANES), jnp.int32),
        scratch_shapes=[
            pltpu.VMEM((2, COMPS, ROWS + 16, LANES), F32),
            pltpu.VMEM((2, ROWS + 32, LANES), F32),
        ],
        compiler_params=pltpu.CompilerParams(vmem_limit_bytes=16 * 2**20),
        cost_estimate=pl.CostEstimate(flops=2 * 10**7, bytes_accessed=4_200_000, transcendentals=262144),
        name="inner_codes",
    )(pltpu.with_memory_space_constraint(disp, pltpu.VMEM))


def tail_kernel(low_ref, sent_ref, left_ref, main_ref, out_ref, pad_ref, side_ref, send_ref, sem):
    send_ref[...] = main_ref[...]
    inside = (lax.axis_index("strip") > 0).astype(F32)

    def tiles(ref):
        field = ref[...].astype(F32)
        return [field[8 * k : 8 * k + 8] for k in range(ref.shape[0] // 8)]

    low, own, left = tiles(low_ref), tiles(sent_ref), tiles(left_ref)
    last = left[0:3]
    before = [left[3], pltpu.roll(left[3], 4, 0), left[4]]
    five = [
        joined_code(left[5]),
        joined_code(left[6]),
        edge_codes([(before[c], last[c], low[2 * c] * inside) for c in range(COMPS)]),
        edge_codes([(last[c] * inside, low[2 * c], low[2 * c + 1]) for c in range(COMPS)]),
        joined_code(own[6]),
    ]
    zeros = jnp.zeros((8, LANES), F32)
    for k in range(5):
        pad_ref[k, :, 0:LANES] = zeros
        pad_ref[k, :, LANES : LANES + ROWS] = five[k]
        pad_ref[k, :, LANES + ROWS : 2 * LANES + ROWS] = zeros
    here = lax.broadcasted_iota(jnp.int32, (8, LANES), 1)
    blocks = ROWS // BLOCK
    for j in range(blocks):
        start = LANES + j * BLOCK - 1
        line = zeros
        for k in range(5):
            window, offset = start // LANES, start % LANES
            first = pltpu.roll(
                pad_ref[k, :, window * LANES : (window + 1) * LANES], (24 * k - offset) % LANES, 1
            )
            if offset + 18 > LANES:
                second = pltpu.roll(
                    pad_ref[k, :, (window + 1) * LANES : (window + 2) * LANES], (24 * k - offset) % LANES, 1
                )
                first = jnp.where(here - 24 * k < LANES - offset, first, second)
            line = first if k == 0 else jnp.where(here < 24 * k, line, first)
        side_ref[j * 8 : j * 8 + 8, :] = line
    for p in range(2):
        send_ref[pl.ds(p * CHUNK + BLOCK + 2, blocks, stride=2 * CHUNK), :] = words(
            *(side_ref[pl.ds(2 + 2 * p + s, blocks, stride=8), :] for s in range(PER))
        )
    copy = pltpu.make_async_copy(send_ref.at[0 : out_ref.shape[0], :], out_ref, sem)
    copy.start()
    copy.wait()


def with_tails(low, sent, left, main, chunks):
    blocks = ROWS // BLOCK
    vmem = pl.BlockSpec(memory_space=pltpu.VMEM)
    return pl.pallas_call(
        tail_kernel,
        in_specs=[vmem] * 4,
        out_specs=pl.BlockSpec(memory_space=pltpu.HBM),
        out_shape=pltpu.HBM((chunks * CHUNK, LANES), jnp.int32),
        scratch_shapes=[
            pltpu.VMEM((5, 8, ROWS + 2 * LANES), F32),
            pltpu.VMEM((blocks * 8 + 8, LANES), F32),
            pltpu.VMEM(main.shape, jnp.int32),
            pltpu.SemaphoreType.DMA,
        ],
        compiler_params=pltpu.CompilerParams(vmem_limit_bytes=8 * 2**20),
        cost_estimate=pl.CostEstimate(flops=10**6, bytes_accessed=5 * 10**5, transcendentals=5 * 10**4),
        name="with_tails",
    )(*(pltpu.with_memory_space_constraint(x, pltpu.VMEM) for x in (low, sent, left, main)))


def designs_kernel(age_ref, code_ref, perms_ref, out_ref):
    subjects = age_ref.shape[1]
    half = subjects // PER

    def total(v):
        return jnp.sum(v, axis=1, keepdims=True)

    def centred(v):
        return v - total(v) * (1.0 / subjects)

    basis = []
    for raw in (
        (code_ref[...] == 1).astype(F32),
        age_ref[...],
        (code_ref[...] == 2).astype(F32),
    ):
        v = centred(raw)
        for _ in range(2):
            for q in basis:
                v = v - q * total(q * v)
            v = centred(v)
        basis.append(v / jnp.sqrt(total(v * v)))
    scale = (0.15 / (subjects - 4)) ** 0.5
    lane = lax.broadcasted_iota(jnp.int32, (8, subjects), 1)
    order = PER * (lane % half) + lane // half
    for k, q in enumerate(basis):
        table = jnp.broadcast_to(q * scale, (8, subjects))

        def put(row, values):
            high = values.astype(BF16)
            rest = (values - high.astype(F32)).astype(BF16)
            at = pl.ds(k * GROUP + row, 16)
            out_ref[at, 0:subjects] = high
            out_ref[at, subjects : 2 * subjects] = high
            out_ref[at, 2 * subjects : 3 * subjects] = rest

        for g in range(PERMS // 16):
            two = []
            for h in range(2):
                who = jnp.take_along_axis(perms_ref[g * 16 + h * 8 : g * 16 + h * 8 + 8, :], order, axis=1)
                two.append(jnp.take_along_axis(table, who, axis=1))
            put(g * 16, jnp.concatenate(two, axis=0))
        plain = jnp.take_along_axis(table, order, axis=1)
        put(PERMS, jnp.concatenate([plain, plain], axis=0))


def design_rows(age, codes, perms):
    subjects = age.shape[0]
    return pl.pallas_call(
        designs_kernel,
        out_shape=jax.ShapeDtypeStruct((3 * GROUP, 3 * subjects), BF16),
        compiler_params=pltpu.CompilerParams(vmem_limit_bytes=8 * 2**20),
        cost_estimate=pl.CostEstimate(flops=4 * 10**6, bytes_accessed=800_000, transcendentals=0),
        name="design_rows",
    )(age.reshape(1, subjects), codes.reshape(1, subjects), perms)


def stats_kernel(senders, code_ref, rows_ref, tmap_ref, peaks_ref, value_ref, y_ref, sum_ref, rss_ref, top_ref, best_ref):
    subjects = PER * senders
    lane = lax.broadcasted_iota(jnp.int32, (subjects, LANES), 1)
    odd = lax.axis_index("subj") % 2
    per = 4 * CHUNK * 2

    def unpack(i, carry):
        at = pl.ds(pl.multiple_of(i * per, 8), per)
        for s, code in enumerate(codes_of(code_ref[at, :])):
            value_ref[s, at, :] = decode(code)
        return carry

    lax.fori_loop(0, senders * CHUNK // per, unpack, 0, unroll=8)

    def gathered(row):
        return jnp.concatenate(
            [value_ref[s, pl.ds(row, senders, stride=CHUNK), :] for s in range(PER)], axis=0
        )

    def place(block, y):
        y = y - jnp.sum(y, axis=0, keepdims=True) * (1.0 / subjects)
        at = pl.ds(pl.multiple_of(block * LANES, LANES), LANES)
        sum_ref[0:1, at] = jnp.sum(y * y, axis=0, keepdims=True) * (0.15 / (subjects - 4)) + FLOOR
        high = y.astype(BF16)
        y_ref[0:subjects, at] = high
        y_ref[subjects : 2 * subjects, at] = (y - high.astype(F32)).astype(BF16)
        y_ref[2 * subjects : 3 * subjects, at] = high

    far = lane // 2 + jnp.where(lane % 2 == 0, 97, 1)
    near = (lane - 36) // 3 + 24 * ((lane - 36) % 3 + 1)
    sides = jnp.take_along_axis(
        gathered(BLOCK + 2),
        jnp.where(lane < 32, far, jnp.where((lane >= 36) & (lane < 90), near, 0)),
        axis=1,
    )

    def mended(y, r):
        ends = pltpu.roll(sides, LANES - 41 - 3 * r, 1)
        return jnp.where((lane == 0) | (lane >= LANES - 2), ends, y)

    blocks = BLOCK + 3

    def placed(block):
        if block < BLOCK + 2:
            y = mended(gathered(block), -1 if block == BLOCK else min(block, BLOCK))
        else:
            y = sides
        place(block, y)

    def project(start):
        at = slice(start * LANES, min(start + 2, blocks) * LANES)
        proj = jnp.dot(rows_ref[...], y_ref[:, at], preferred_element_type=F32)
        q1, q2, q3 = (proj[k * GROUP : (k + 1) * GROUP] for k in range(3))
        rss_ref[:, at] = sum_ref[0:1, at] - q1 * q1 - q2 * q2 - q3 * q3
        top_ref[:, at] = q3

    here = lax.broadcasted_iota(jnp.int32, (8, LANES), 1)
    first = lax.axis_index("strip") == 0
    seam = (here == LANES - 3) | (here == LANES - 2)
    from_before = (here == LANES - 2) | ((here == 0) & first)
    from_after = (here == LANES - 3) | ((here == LANES - 1) & first)
    unscale = ((subjects - 4) / 0.15) ** 0.5

    def pseudo_t(g, r):
        at = slice(g * 8, g * 8 + 8) if isinstance(g, int) else pl.ds(pl.multiple_of(g * 8, 8), 8)

        def block(b):
            return rss_ref[at, b * LANES : (b + 1) * LANES]

        mine = block(r)
        above = block(r - 1 if r > 0 else BLOCK)
        below = block(r + 1 if r < BLOCK - 1 else BLOCK + 1)
        ends = jnp.where(seam, pltpu.roll(block(BLOCK + 2), LANES - 3 - 2 * r, 1), FLOOR)
        before = jnp.where(from_before, ends, pltpu.roll(mine, 1, 1))
        after = jnp.where(from_after, ends, pltpu.roll(mine, LANES - 1, 1))
        beside = (above + below) + (before + after)
        variance = CENTRE * mine + beside
        return top_ref[at, r * LANES : (r + 1) * LANES] * lax.rsqrt(variance)

    def peaks_of(first_row, last_row):
        for g in range(PERMS // 8):
            at = slice(g * 8, g * 8 + 8)
            best = best_ref[at, :] if first_row > 0 else jnp.zeros((8, LANES), F32)
            for r in range(first_row, last_row):
                best = jnp.maximum(best, jnp.abs(pseudo_t(g, r)))
            best_ref[at, :] = best

    for block in (BLOCK, BLOCK + 1, BLOCK + 2):
        placed(block)
    project(BLOCK)
    project(BLOCK + 2)
    done = 0
    for start in range(0, BLOCK, 2):
        for block in range(start, start + 2):
            placed(block)
        project(start)
        ready = start + 1 if start < BLOCK - 2 else BLOCK
        if start % 4 == 2:
            peaks_of(done, ready)
            done = ready

    half = BLOCK // 2
    for r in range(BLOCK):
        tmap_ref[(r // half + odd) % 2, r % half : r % half + 1, :] = (
            pseudo_t(PERMS // 8, r)[0:1, :] * unscale
        )
    code = jnp.max(best_ref[...].T, axis=0, keepdims=True) * (unscale / REACH_T)
    code = jnp.minimum(jnp.sqrt(jnp.sqrt(code)), 1.0) * LEVELS + 0.5
    lines = jnp.concatenate([code[:, k * LANES : (k + 1) * LANES] for k in range(PERMS // LANES)] * 4, axis=0)
    everyone = peaks_ref.shape[0]
    peaks_ref[...] = jnp.broadcast_to(lines.astype(jnp.int32).astype(I16)[None], (everyone // 4, 8, LANES)).reshape(everyone, 2, LANES)


def block_stats(codes, rows, senders, everyone):
    subjects = PER * senders
    columns = (BLOCK + 3) * LANES
    return pl.pallas_call(
        functools.partial(stats_kernel, senders),
        out_shape=(
            jax.ShapeDtypeStruct((2, BLOCK // 2, LANES), F32),
            jax.ShapeDtypeStruct((everyone, PERMS // LANES, LANES), I16),
        ),
        scratch_shapes=[
            pltpu.VMEM((PER, senders * CHUNK + CHUNK + 5, LANES), F32),
            pltpu.VMEM((3 * subjects, columns), BF16),
            pltpu.VMEM((8, columns), F32),
            pltpu.VMEM((GROUP, columns), F32),
            pltpu.VMEM((GROUP, columns), F32),
            pltpu.VMEM((PERMS, LANES), F32),
        ],
        compiler_params=pltpu.CompilerParams(vmem_limit_bytes=24 * 2**20),
        cost_estimate=pl.CostEstimate(flops=2 * 10**9, bytes_accessed=10**6, transcendentals=10**6),
        name="block_stats",
    )(codes, rows)


def largest_kernel(code_ref, out_ref):
    lines = PERMS // LANES
    code = jnp.max(code_ref[...].astype(F32), axis=0).reshape(16 // lines, lines, LANES)
    root = jnp.max(code, axis=0) * (REACH_T**0.25 / LEVELS)
    out_ref[...] = (root * root) * (root * root)


def largest(codes):
    return pl.pallas_call(
        largest_kernel,
        out_shape=jax.ShapeDtypeStruct((PERMS // LANES, LANES), F32),
        compiler_params=pltpu.CompilerParams(vmem_limit_bytes=4 * 2**20),
        name="largest",
    )(codes)


def on_device(displacement, age, group_codes, perms):
    senders = lax.axis_size("subj")
    strips = lax.axis_size("strip")
    low, after, field = strip_edges(displacement)
    left = lax.ppermute(after, "strip", [(i, (i + 1) % strips) for i in range(strips)])
    main = inner_codes(field, senders)
    rows = design_rows(age, group_codes, perms)
    sent = with_tails(low, after, left, main, senders)
    codes = lax.all_to_all(
        sent.reshape(senders, CHUNK, 1, LANES), "subj", split_axis=0, concat_axis=0, tiled=True
    )
    everyone = senders * strips
    tested, mine = block_stats(codes.reshape(senders * CHUNK, LANES), rows, senders, everyone)

    odd = lax.axis_index("subj") % 2 == 1
    swapped = lax.ppermute(tested[1], "subj", [(i, i ^ 1) for i in range(senders)])
    t_map = jnp.stack([jnp.where(odd, swapped, tested[0]), jnp.where(odd, tested[0], swapped)])
    beyond = lax.ppermute(t_map, "strip", [((i + 1) % strips, i) for i in range(strips)])
    t_map = jnp.where(lax.broadcasted_iota(jnp.int32, t_map.shape, 2) >= LANES - 2, beyond, t_map)

    theirs = lax.all_to_all(mine, ("subj", "strip"), split_axis=0, concat_axis=0, tiled=True)
    return t_map, largest(theirs.reshape(-1, 16, LANES)).reshape(PERMS)


def solution(mesh):
    placed = (P("subj", None, None, None, "strip"), P(), P(), P())
    return jax.shard_map(
        on_device,
        mesh=mesh,
        in_specs=placed,
        out_specs=(P(None, "subj", "strip"), P()),
        check_vma=False,
    )
```

```python
import functools

import jax
import jax.numpy as jnp
from jax import lax
from jax.experimental import pallas as pl
from jax.experimental.pallas import tpu as pltpu
from jax.sharding import PartitionSpec as P

F32, BF16, I16 = jnp.float32, jnp.bfloat16, jnp.int16
LANES = 128
ROWS = 512
BLOCK = 16
PER = 2
CHUNK = BLOCK + 3
COMPS, PLANES = 3, 4
PERMS, GROUP = 256, 272
REACH = 0.6
REACH_T = 6800.0
LEVELS = 32767.0
CENTRE = 0.4 / 0.15
FLOOR = 1e-06 / (CENTRE + 4.0)


def encode(y):
    half = y * lax.rsqrt(jnp.maximum(jnp.abs(y), 1e-30))
    fourth = half * lax.rsqrt(jnp.maximum(jnp.abs(half), 1e-15))
    shift = 1.5 * 2.0**23
    return (fourth * (LEVELS / REACH**0.25) + shift) - shift


def decode(code):
    part = code * (REACH**0.25 / LEVELS)
    return (part * jnp.abs(part)) * (part * part)


def words(first, second):
    return (first.astype(jnp.int32) << 16) | (second.astype(jnp.int32) & 0xFFFF)


def codes_of(word):
    return (word >> 16).astype(F32), ((word << 16) >> 16).astype(F32)


def log_det(dz, dx, dy):
    j00, j01, j02 = 2.0 + dz[0], dx[0], dy[0]
    j10, j11, j12 = dz[1], 2.0 + dx[1], dy[1]
    j20, j21, j22 = dz[2], dx[2], 2.0 + dy[2]
    det = (
        j00 * (j11 * j22 - j12 * j21)
        - j01 * (j10 * j22 - j12 * j20)
        + j02 * (j10 * j21 - j11 * j20)
    )
    return jnp.log(det * 0.125)


SENT = 7


def edge_codes(around):
    lane = lax.broadcasted_iota(jnp.int32, (8, ROWS), 1)
    dz, dx, dy = [], [], []
    for before, center, after in around:
        dz.append(pltpu.roll(center, 6, 0) - pltpu.roll(center, 2, 0))
        dx.append(
            jnp.where(lane == ROWS - 1, 0.0, pltpu.roll(center, ROWS - 1, 1))
            - jnp.where(lane == 0, 0.0, pltpu.roll(center, 1, 1))
        )
        dy.append(after - before)
    return encode(log_det(dz, dx, dy))


def two_in_tile(first, second):
    row = lax.broadcasted_iota(jnp.int32, first.shape, 0)
    return jnp.where((row >= 2) & (row < 6), first, pltpu.roll(second, 4, 0))


def split_code(code):
    shift = 1.5 * 2.0**31
    high = (code + shift) - shift
    return two_in_tile(high, code - high)


def joined_code(tile):
    return tile + pltpu.roll(tile, 4, 0)


def edges_kernel(disp_ref, low_ref, sent_ref, field_ref, high_ref, sem):
    copies = [
        [
            pltpu.make_async_copy(disp_ref.at[s, c, q : q + 2], field_ref.at[s, c, q : q + 2], sem.at[c, q // 2, s])
            for s in range(PER)
        ]
        for c in range(COMPS)
        for q in range(0, PLANES, 2)
    ]
    for pair in copies:
        for copy in pair:
            copy.start()
    row = lax.broadcasted_iota(jnp.int32, (48, 2 * LANES), 0)
    lane = lax.broadcasted_iota(jnp.int32, (48, 2 * LANES), 1)
    column = jnp.where(row < 16, row // 8, row // 8 - 2 + LANES - 4)
    picks = [
        ((row % 8 == 2 * q + lane // LANES) & (lane % LANES == column)).astype(F32).astype(BF16)
        for q in range(PLANES)
    ]
    for c in range(COMPS):
        acc = jnp.zeros((48, ROWS), F32)
        for q in range(PLANES):
            if q % 2 == 0:
                for copy in copies[c * (PLANES // 2) + q // 2]:
                    copy.wait()
            both = jnp.concatenate([field_ref[0, c, q], field_ref[1, c, q]], axis=1)
            acc = acc + lax.dot_general(
                picks[q], both, (((1,), (1,)), ((), ())), preferred_element_type=F32
            )
        low_ref[c * 16 : c * 16 + 16, :] = acc[0:16].astype(BF16)
        high_ref[c * 32 : c * 32 + 32, :] = acc[16:48]
    high = [[high_ref[32 * c + 8 * e : 32 * c + 8 * e + 8, :] for e in range(4)] for c in range(COMPS)]
    tiles = [w[3] for w in high] + [
        two_in_tile(high[0][2], high[1][2]),
        high[2][2],
        split_code(edge_codes([w[0:3] for w in high])),
        split_code(edge_codes([w[1:4] for w in high])),
    ]
    sent_ref[...] = jnp.concatenate(tiles, axis=0).astype(BF16)


def strip_edges(disp):
    out = [pltpu.VMEM((rows, ROWS), BF16) for rows in (COMPS * 16, SENT * 8)]
    return pl.pallas_call(
        edges_kernel,
        in_specs=[pl.BlockSpec(memory_space=pltpu.HBM)],
        out_specs=[pl.BlockSpec(memory_space=pltpu.VMEM)] * 3,
        out_shape=(*out, pltpu.VMEM(disp.shape, BF16)),
        scratch_shapes=[pltpu.VMEM((COMPS * 32, ROWS), F32), pltpu.SemaphoreType.DMA((COMPS, PLANES // 2, PER))],
        compiler_params=pltpu.CompilerParams(vmem_limit_bytes=8 * 2**20),
        cost_estimate=pl.CostEstimate(flops=10**8, bytes_accessed=3_200_000, transcendentals=0),
        name="strip_edges",
    )(pltpu.with_memory_space_constraint(disp, pltpu.HBM))


def inner_kernel(disp_ref, out_ref, pad_ref, code_ref):
    pad, step = 8, 16
    blocks = ROWS // BLOCK
    zeros = jnp.zeros((pad, LANES), F32)
    for s in range(PER):
        code_ref[s, 0:pad, :] = zeros
        code_ref[s, pad + ROWS : 2 * pad + ROWS, :] = zeros
    for p in range(2):
        for c in range(COMPS):
            pad_ref[p, c, 0:pad, :] = zeros
            pad_ref[p, c, pad + ROWS : 2 * pad + ROWS, :] = zeros
    for p in range(2):
        for s in range(PER):
            for c in range(COMPS):
                pad_ref[s, c, pad : pad + ROWS, :] = disp_ref[s, c, 1 + p].astype(F32)

            def body(i, carry):
                base = pl.multiple_of(i * step, step)
                dz, dx, dy = [], [], []
                for c in range(COMPS):
                    up = disp_ref[s, c, p + 2, pl.ds(base, step), :].astype(F32)
                    down = disp_ref[s, c, p, pl.ds(base, step), :].astype(F32)
                    dz.append(up - down)
                    center = pad_ref[s, c, pl.ds(base + pad, step), :]
                    dx.append(
                        pad_ref[s, c, pl.ds(base + pad + 1, step), :]
                        - pad_ref[s, c, pl.ds(base + pad - 1, step), :]
                    )
                    dy.append(pltpu.roll(center, LANES - 1, 1) - pltpu.roll(center, 1, 1))
                code = encode(log_det(dz, dx, dy))
                code_ref[s, pl.ds(base + pad, step), :] = code
                if s == PER - 1:
                    out_ref[pl.ds((2 * i + p) * CHUNK, step), :] = words(
                        code_ref[0, pl.ds(base + pad, step), :], code
                    )
                return carry

            lax.fori_loop(0, ROWS // step, body, 0, unroll=32)
        for h, start in enumerate((pad - 1, pad + BLOCK)):
            out_ref[pl.ds(p * CHUNK + BLOCK + h, blocks, stride=2 * CHUNK), :] = words(
                *(code_ref[s, pl.ds(start, blocks, stride=BLOCK), :] for s in range(PER))
            )


def inner_codes(disp, chunks):
    return pl.pallas_call(
        inner_kernel,
        in_specs=[pl.BlockSpec(memory_space=pltpu.VMEM)],
        out_specs=pl.BlockSpec(memory_space=pltpu.VMEM),
        out_shape=pltpu.VMEM((chunks * CHUNK + 2 * CHUNK + 2, LANES), jnp.int32),
        scratch_shapes=[
            pltpu.VMEM((2, COMPS, ROWS + 16, LANES), F32),
            pltpu.VMEM((2, ROWS + 32, LANES), F32),
        ],
        compiler_params=pltpu.CompilerParams(vmem_limit_bytes=16 * 2**20),
        cost_estimate=pl.CostEstimate(flops=2 * 10**7, bytes_accessed=4_200_000, transcendentals=262144),
        name="inner_codes",
    )(pltpu.with_memory_space_constraint(disp, pltpu.VMEM))


def tail_kernel(low_ref, sent_ref, left_ref, main_ref, out_ref, pad_ref, side_ref, send_ref, sem):
    send_ref[...] = main_ref[...]
    inside = (lax.axis_index("strip") > 0).astype(F32)

    def tiles(ref):
        field = ref[...].astype(F32)
        return [field[8 * k : 8 * k + 8] for k in range(ref.shape[0] // 8)]

    low, own, left = tiles(low_ref), tiles(sent_ref), tiles(left_ref)
    last = left[0:3]
    before = [left[3], pltpu.roll(left[3], 4, 0), left[4]]
    five = [
        joined_code(left[5]),
        joined_code(left[6]),
        edge_codes([(before[c], last[c], low[2 * c] * inside) for c in range(COMPS)]),
        edge_codes([(last[c] * inside, low[2 * c], low[2 * c + 1]) for c in range(COMPS)]),
        joined_code(own[6]),
    ]
    zeros = jnp.zeros((8, LANES), F32)
    for k in range(5):
        pad_ref[k, :, 0:LANES] = zeros
        pad_ref[k, :, LANES : LANES + ROWS] = five[k]
        pad_ref[k, :, LANES + ROWS : 2 * LANES + ROWS] = zeros
    here = lax.broadcasted_iota(jnp.int32, (8, LANES), 1)
    blocks = ROWS // BLOCK
    some, copies = blocks // 4, []
    for j in range(blocks):
        start = LANES + j * BLOCK - 1
        line = zeros
        for k in range(5):
            window, offset = start // LANES, start % LANES
            first = pltpu.roll(
                pad_ref[k, :, window * LANES : (window + 1) * LANES], (24 * k - offset) % LANES, 1
            )
            if offset + 18 > LANES:
                second = pltpu.roll(
                    pad_ref[k, :, (window + 1) * LANES : (window + 2) * LANES], (24 * k - offset) % LANES, 1
                )
                first = jnp.where(here - 24 * k < LANES - offset, first, second)
            line = first if k == 0 else jnp.where(here < 24 * k, line, first)
        side_ref[j * 8 : j * 8 + 8, :] = line
        if (j + 1) % some == 0:
            begin = j + 1 - some
            for p in range(2):
                at = pl.ds((2 * begin + p) * CHUNK + BLOCK + 2, some, stride=2 * CHUNK)
                send_ref[at, :] = words(
                    *(side_ref[pl.ds(8 * begin + 2 + 2 * p + s, some, stride=8), :] for s in range(PER))
                )
            part = slice(2 * begin * CHUNK, 2 * (j + 1) * CHUNK)
            copies.append(
                pltpu.make_async_copy(send_ref.at[part, :], out_ref.at[part, :], sem.at[len(copies)])
            )
            copies[-1].start()
    for copy in copies:
        copy.wait()


def with_tails(low, sent, left, main, chunks):
    blocks = ROWS // BLOCK
    vmem = pl.BlockSpec(memory_space=pltpu.VMEM)
    return pl.pallas_call(
        tail_kernel,
        in_specs=[vmem] * 4,
        out_specs=pl.BlockSpec(memory_space=pltpu.HBM),
        out_shape=pltpu.HBM((chunks * CHUNK, LANES), jnp.int32),
        scratch_shapes=[
            pltpu.VMEM((5, 8, ROWS + 2 * LANES), F32),
            pltpu.VMEM((blocks * 8 + 8, LANES), F32),
            pltpu.VMEM(main.shape, jnp.int32),
            pltpu.SemaphoreType.DMA((4,)),
        ],
        compiler_params=pltpu.CompilerParams(vmem_limit_bytes=8 * 2**20),
        cost_estimate=pl.CostEstimate(flops=10**6, bytes_accessed=5 * 10**5, transcendentals=5 * 10**4),
        name="with_tails",
    )(*(pltpu.with_memory_space_constraint(x, pltpu.VMEM) for x in (low, sent, left, main)))


def designs_kernel(age_ref, code_ref, perms_ref, out_ref):
    subjects = age_ref.shape[1]
    half = subjects // PER

    def total(v):
        return jnp.sum(v, axis=1, keepdims=True)

    def centred(v):
        return v - total(v) * (1.0 / subjects)

    basis = []
    for raw in (
        (code_ref[...] == 1).astype(F32),
        age_ref[...],
        (code_ref[...] == 2).astype(F32),
    ):
        v = centred(raw)
        for _ in range(2):
            for q in basis:
                v = v - q * total(q * v)
            v = centred(v)
        basis.append(v / jnp.sqrt(total(v * v)))
    scale = (0.15 / (subjects - 4)) ** 0.5
    lane = lax.broadcasted_iota(jnp.int32, (8, subjects), 1)
    order = PER * (lane % half) + lane // half
    for k, q in enumerate(basis):
        table = jnp.broadcast_to(q * scale, (8, subjects))

        def put(row, values):
            high = values.astype(BF16)
            rest = (values - high.astype(F32)).astype(BF16)
            at = pl.ds(k * GROUP + row, 16)
            out_ref[at, 0:subjects] = high
            out_ref[at, subjects : 2 * subjects] = high
            out_ref[at, 2 * subjects : 3 * subjects] = rest

        for g in range(PERMS // 16):
            two = []
            for h in range(2):
                who = jnp.take_along_axis(perms_ref[g * 16 + h * 8 : g * 16 + h * 8 + 8, :], order, axis=1)
                two.append(jnp.take_along_axis(table, who, axis=1))
            put(g * 16, jnp.concatenate(two, axis=0))
        plain = jnp.take_along_axis(table, order, axis=1)
        put(PERMS, jnp.concatenate([plain, plain], axis=0))


def design_rows(age, codes, perms):
    subjects = age.shape[0]
    return pl.pallas_call(
        designs_kernel,
        out_shape=jax.ShapeDtypeStruct((3 * GROUP, 3 * subjects), BF16),
        compiler_params=pltpu.CompilerParams(vmem_limit_bytes=8 * 2**20),
        cost_estimate=pl.CostEstimate(flops=4 * 10**6, bytes_accessed=800_000, transcendentals=0),
        name="design_rows",
    )(age.reshape(1, subjects), codes.reshape(1, subjects), perms)


def stats_kernel(senders, code_ref, rows_ref, tmap_ref, peaks_ref, value_ref, y_ref, sum_ref, rss_ref, top_ref, best_ref):
    subjects = PER * senders
    lane = lax.broadcasted_iota(jnp.int32, (subjects, LANES), 1)
    odd = lax.axis_index("subj") % 2
    per = 4 * CHUNK * 2

    def unpack(i, carry):
        at = pl.ds(pl.multiple_of(i * per, 8), per)
        for s, code in enumerate(codes_of(code_ref[at, :])):
            value_ref[s, at, :] = decode(code)
        return carry

    lax.fori_loop(0, senders * CHUNK // per, unpack, 0, unroll=8)

    def gathered(row):
        return jnp.concatenate(
            [value_ref[s, pl.ds(row, senders, stride=CHUNK), :] for s in range(PER)], axis=0
        )

    def place(block, y):
        y = y - jnp.sum(y, axis=0, keepdims=True) * (1.0 / subjects)
        at = pl.ds(pl.multiple_of(block * LANES, LANES), LANES)
        sum_ref[0:1, at] = jnp.sum(y * y, axis=0, keepdims=True) * (0.15 / (subjects - 4)) + FLOOR
        high = y.astype(BF16)
        y_ref[0:subjects, at] = high
        y_ref[subjects : 2 * subjects, at] = (y - high.astype(F32)).astype(BF16)
        y_ref[2 * subjects : 3 * subjects, at] = high

    far = lane // 2 + jnp.where(lane % 2 == 0, 97, 1)
    near = (lane - 36) // 3 + 24 * ((lane - 36) % 3 + 1)
    sides = jnp.take_along_axis(
        gathered(BLOCK + 2),
        jnp.where(lane < 32, far, jnp.where((lane >= 36) & (lane < 90), near, 0)),
        axis=1,
    )

    def mended(y, r):
        ends = pltpu.roll(sides, LANES - 41 - 3 * r, 1)
        return jnp.where((lane == 0) | (lane >= LANES - 2), ends, y)

    blocks = BLOCK + 3

    def placed(block):
        if block < BLOCK + 2:
            y = mended(gathered(block), -1 if block == BLOCK else min(block, BLOCK))
        else:
            y = sides
        place(block, y)

    def project(start):
        at = slice(start * LANES, min(start + 2, blocks) * LANES)
        proj = jnp.dot(rows_ref[...], y_ref[:, at], preferred_element_type=F32)
        q1, q2, q3 = (proj[k * GROUP : (k + 1) * GROUP] for k in range(3))
        rss_ref[:, at] = sum_ref[0:1, at] - q1 * q1 - q2 * q2 - q3 * q3
        top_ref[:, at] = q3

    here = lax.broadcasted_iota(jnp.int32, (8, LANES), 1)
    first = lax.axis_index("strip") == 0
    seam = (here == LANES - 3) | (here == LANES - 2)
    from_before = (here == LANES - 2) | ((here == 0) & first)
    from_after = (here == LANES - 3) | ((here == LANES - 1) & first)
    unscale = ((subjects - 4) / 0.15) ** 0.5

    def pseudo_t(g, r):
        at = slice(g * 8, g * 8 + 8) if isinstance(g, int) else pl.ds(pl.multiple_of(g * 8, 8), 8)

        def block(b):
            return rss_ref[at, b * LANES : (b + 1) * LANES]

        mine = block(r)
        above = block(r - 1 if r > 0 else BLOCK)
        below = block(r + 1 if r < BLOCK - 1 else BLOCK + 1)
        ends = jnp.where(seam, pltpu.roll(block(BLOCK + 2), LANES - 3 - 2 * r, 1), FLOOR)
        before = jnp.where(from_before, ends, pltpu.roll(mine, 1, 1))
        after = jnp.where(from_after, ends, pltpu.roll(mine, LANES - 1, 1))
        beside = (above + below) + (before + after)
        variance = CENTRE * mine + beside
        return top_ref[at, r * LANES : (r + 1) * LANES] * lax.rsqrt(variance)

    def peaks_of(first_row, last_row):
        for g in range(PERMS // 8):
            at = slice(g * 8, g * 8 + 8)
            best = best_ref[at, :] if first_row > 0 else jnp.zeros((8, LANES), F32)
            for r in range(first_row, last_row):
                best = jnp.maximum(best, jnp.abs(pseudo_t(g, r)))
            best_ref[at, :] = best

    for block in (BLOCK, BLOCK + 1, BLOCK + 2):
        placed(block)
    project(BLOCK)
    project(BLOCK + 2)
    done = 0
    for start in range(0, BLOCK, 2):
        for block in range(start, start + 2):
            placed(block)
        project(start)
        ready = start + 1 if start < BLOCK - 2 else BLOCK
        if start % 4 == 2:
            peaks_of(done, ready)
            done = ready

    half = BLOCK // 2
    for r in range(BLOCK):
        tmap_ref[(r // half + odd) % 2, r % half : r % half + 1, :] = (
            pseudo_t(PERMS // 8, r)[0:1, :] * unscale
        )
    code = jnp.max(best_ref[...].T, axis=0, keepdims=True) * (unscale / REACH_T)
    code = jnp.minimum(jnp.sqrt(jnp.sqrt(code)), 1.0) * LEVELS + 0.5
    lines = jnp.concatenate([code[:, k * LANES : (k + 1) * LANES] for k in range(PERMS // LANES)] * 4, axis=0)
    everyone = peaks_ref.shape[0]
    peaks_ref[...] = jnp.broadcast_to(lines.astype(jnp.int32).astype(I16)[None], (everyone // 4, 8, LANES)).reshape(everyone, 2, LANES)


def block_stats(codes, rows, senders, everyone):
    subjects = PER * senders
    columns = (BLOCK + 3) * LANES
    return pl.pallas_call(
        functools.partial(stats_kernel, senders),
        out_shape=(
            jax.ShapeDtypeStruct((2, BLOCK // 2, LANES), F32),
            jax.ShapeDtypeStruct((everyone, PERMS // LANES, LANES), I16),
        ),
        scratch_shapes=[
            pltpu.VMEM((PER, senders * CHUNK + CHUNK + 5, LANES), F32),
            pltpu.VMEM((3 * subjects, columns), BF16),
            pltpu.VMEM((8, columns), F32),
            pltpu.VMEM((GROUP, columns), F32),
            pltpu.VMEM((GROUP, columns), F32),
            pltpu.VMEM((PERMS, LANES), F32),
        ],
        compiler_params=pltpu.CompilerParams(vmem_limit_bytes=24 * 2**20),
        cost_estimate=pl.CostEstimate(flops=2 * 10**9, bytes_accessed=10**6, transcendentals=10**6),
        name="block_stats",
    )(codes, rows)


def largest_kernel(code_ref, out_ref):
    lines = PERMS // LANES
    code = jnp.max(code_ref[...].astype(F32), axis=0).reshape(16 // lines, lines, LANES)
    root = jnp.max(code, axis=0) * (REACH_T**0.25 / LEVELS)
    out_ref[...] = (root * root) * (root * root)


def largest(codes):
    return pl.pallas_call(
        largest_kernel,
        out_shape=jax.ShapeDtypeStruct((PERMS // LANES, LANES), F32),
        compiler_params=pltpu.CompilerParams(vmem_limit_bytes=4 * 2**20),
        name="largest",
    )(codes)


def on_device(displacement, age, group_codes, perms):
    senders = lax.axis_size("subj")
    strips = lax.axis_size("strip")
    low, after, field = strip_edges(displacement)
    left = lax.ppermute(after, "strip", [(i, (i + 1) % strips) for i in range(strips)])
    main = inner_codes(field, senders)
    rows = design_rows(age, group_codes, perms)
    sent = with_tails(low, after, left, main, senders)
    codes = lax.all_to_all(
        sent.reshape(senders, CHUNK, 1, LANES), "subj", split_axis=0, concat_axis=0, tiled=True
    )
    everyone = senders * strips
    tested, mine = block_stats(codes.reshape(senders * CHUNK, LANES), rows, senders, everyone)

    odd = lax.axis_index("subj") % 2 == 1
    swapped = lax.ppermute(tested[1], "subj", [(i, i ^ 1) for i in range(senders)])
    t_map = jnp.stack([jnp.where(odd, swapped, tested[0]), jnp.where(odd, tested[0], swapped)])
    beyond = lax.ppermute(t_map, "strip", [((i + 1) % strips, i) for i in range(strips)])
    t_map = jnp.where(lax.broadcasted_iota(jnp.int32, t_map.shape, 2) >= LANES - 2, beyond, t_map)

    theirs = lax.all_to_all(mine, ("subj", "strip"), split_axis=0, concat_axis=0, tiled=True)
    return t_map, largest(theirs.reshape(-1, 16, LANES)).reshape(PERMS)


def solution(mesh):
    placed = (P("subj", None, None, None, "strip"), P(), P(), P())
    return jax.shard_map(
        on_device,
        mesh=mesh,
        in_specs=placed,
        out_specs=(P(None, "subj", "strip"), P()),
        check_vma=False,
    )
```
